256 devices in a mesh: dp: 16 (over y, z_lo, core), patch: 16 (over z_hi, x).
Axes of the slice: x: 4, y: 4, z: 8 (z_hi: 4, z_lo: 2; z = z_hi * 2 + z_lo), core: 2. Of those that a mesh axis runs over, the one named last changes fastest.
Arguments:
- patch_queries: bfloat16 [16, 4096, 512], P('dp', 'patch'), may hold values from -6 to 6
- patch_keys: bfloat16 [16, 4096, 512], P('dp', 'patch'), may hold values from -6 to 6
- patch_values: bfloat16 [16, 4096, 512], P('dp', 'patch'), may hold values from -6 to 6
- residual: float32 [16, 4096, 1024], P('dp', 'patch'), may hold values from -2 to 2
- teacher: bfloat16 [16, 4096, 1024], P('dp', 'patch'), may hold values from -6 to 6
- output_weight: bfloat16 [512, 1024], replicated, may hold values from -0.25 to 0.25
Outputs:
- d_queries: float32 [16, 4096, 512], P('dp', 'patch')
- d_keys: float32 [16, 4096, 512], P('dp', 'patch')
- d_values: float32 [16, 4096, 512], P('dp', 'patch')
- d_features: float32 [16, 4096, 1024], P('dp', 'patch')
- d_output_weight: float32 [512, 1024], replicated
The draws below stay inside these ranges and needn't reach their ends.
All inputs are finite; a program needn't handle non-finite values.
Results may differ from the reference program's by a relative error of at most 0.017.
Values may be sent and summed in bfloat16 or wider, within the bound.
A program may use at most 128 MiB of HBM per device.

```python
import jax
import jax.numpy as jnp
from jax import lax

D = 1024
HEADS = 8
HEAD = 64
ROWS = 256
ROUNDS = 3
HD = 512
NP = 4096
PAGES = 16
N_PATCH = 16


def draw_patch_queries(key, part):
    key = jax.random.fold_in(key, 11)
    result = jnp.clip(jax.random.normal(key, (PAGES, NP, HD), jnp.float32), -4.0, 4.0)
    return result.astype(jnp.bfloat16)


def draw_patch_keys(key, part):
    key = jax.random.fold_in(key, 12)
    result = jnp.clip(jax.random.normal(key, (PAGES, NP, HD), jnp.float32), -4.0, 4.0)
    return result.astype(jnp.bfloat16)


def draw_residual(key, part):
    key = jax.random.fold_in(key, 13)
    first = jax.random.fold_in(key, 0)
    second = jax.random.fold_in(key, 1)
    fourth = jax.random.fold_in(key, 3)
    row_scale = jnp.exp(jax.random.uniform(first, (PAGES, NP, 1), jnp.float32, 0.0, 2.302585))
    noise = jnp.clip(jax.random.normal(second, (PAGES, NP, D), jnp.float32), -6.0, 6.0)
    page_index = jnp.arange(PAGES)[:, None, None]
    block_index = (jnp.arange(NP) // ROWS)[None, :, None]
    chosen = jax.random.randint(fourth, (2,), 0, PAGES * (NP // ROWS))
    middle = (page_index == PAGES // 2) & (block_index == 0)
    drawn = (page_index == chosen[0] // (NP // ROWS)) & (block_index == chosen[1] % (NP // ROWS))
    quiet = jnp.where(middle | drawn, 0.02, 1.0)
    return 0.03 * row_scale * noise * quiet


def level_of(own_key, extent, shards, low, high):
    gain, own = 1.0, jax.random.fold_in(own_key, 6)
    for dim, shards_of in shards:
        steps = jnp.exp(jax.random.uniform(jax.random.fold_in(own, dim), (shards_of,), jnp.float32, low / len(shards), high / len(shards)))
        gain = gain * jnp.repeat(steps, extent[dim] // shards_of).reshape([-1 if axis == dim else 1 for axis in range(len(extent))])
    return gain


def bell_draw(stream_key, dims, deviation, limit, cuts=(), held_as=jnp.bfloat16):
    loudness = level_of(stream_key, dims, cuts, -0.22, 0.18) if cuts else 1.0
    values = jax.random.normal(stream_key, dims, jnp.float32) * deviation * loudness
    return jnp.minimum(jnp.maximum(values, -limit), limit).astype(held_as)


def setup_inputs(seed: int = 0) -> dict:
    arg_keys = jax.random.split(jax.random.key(seed), 7)
    return {
        "patch_queries": draw_patch_queries(jax.random.fold_in(arg_keys[6], 71), 0),
        "patch_keys": draw_patch_keys(jax.random.fold_in(arg_keys[6], 71), 0),
        "patch_values": bell_draw(arg_keys[2], (PAGES, NP, HD), 1.0, 6.0, ((0, 16), (1, 16))),
        "residual": draw_residual(jax.random.fold_in(arg_keys[6], 71), 0),
        "teacher": bell_draw(arg_keys[4], (PAGES, NP, D), 1.0, 6.0, ((0, 16), (1, 16))),
        "output_weight": bell_draw(arg_keys[5], (HD, D), HD ** -0.5, 0.25),
    }


def head_forward(operands):
    head_queries, head_keys, head_values = operands
    score_scale = HEAD ** (-0.5)
    scores = jnp.dot(head_queries, head_keys.T, preferred_element_type=jnp.float32) * score_scale
    row_max = lax.optimization_barrier(jnp.max(scores, axis=1, keepdims=True))
    expo = jnp.exp(scores - row_max)
    row_total = lax.optimization_barrier(jnp.sum(expo, axis=1, keepdims=True))
    output = jnp.dot(expo.astype(jnp.bfloat16), head_values, preferred_element_type=jnp.float32) / row_total
    log_total = (row_max + jnp.log(row_total))[:, 0]
    return (output, log_total)

def head_backward(operands):
    head_queries, head_keys, head_values, head_grads, log_total, row_dot = operands
    score_scale = HEAD ** (-0.5)

    def query_block(pieces):
        block_queries, block_grads, block_total, block_dot = pieces
        scores = jnp.dot(block_queries, head_keys.T, preferred_element_type=jnp.float32) * score_scale
        prob_exact = jnp.exp(scores - block_total[:, None])
        prob_weights = prob_exact.astype(jnp.bfloat16)
        prob_grad = jnp.dot(block_grads, head_values.T, preferred_element_type=jnp.float32)
        score_grad = (prob_exact * (prob_grad - block_dot[:, None])).astype(jnp.bfloat16)
        query_grad = score_scale * jnp.dot(score_grad, head_keys, preferred_element_type=jnp.float32)
        key_part = (score_scale * jnp.dot(score_grad.T, block_queries, preferred_element_type=jnp.float32)).astype(jnp.bfloat16)
        value_part = jnp.dot(prob_weights.T, block_grads, preferred_element_type=jnp.float32).astype(jnp.bfloat16)
        return (query_grad, key_part, value_part)
    blocks = (head_queries.reshape(N_PATCH, ROWS, HEAD), head_grads.reshape(N_PATCH, ROWS, HEAD), log_total.reshape(N_PATCH, ROWS), row_dot.reshape(N_PATCH, ROWS))
    query_grad, key_parts, value_parts = lax.map(query_block, blocks)
    return (query_grad.reshape(NP, HEAD), lax.optimization_barrier(jnp.sum(key_parts.astype(jnp.float32), axis=0)), lax.optimization_barrier(jnp.sum(value_parts.astype(jnp.float32), axis=0)))

def split_heads(matrix):
    return matrix.reshape(NP, HEADS, HEAD).transpose(1, 0, 2)

def join_heads(stacked):
    return stacked.transpose(1, 0, 2).reshape(NP, HD)

def gram_tile(left_student, left_teacher, right_student, right_teacher):
    first = jnp.einsum('xad,xbd->xab', left_student.astype(jnp.float32), right_student.astype(jnp.float32))
    second = jnp.einsum('xad,xbd->xab', left_teacher.astype(jnp.float32), right_teacher.astype(jnp.float32))
    return (first - second).astype(jnp.bfloat16).astype(jnp.float32)

def page_backward(output_weight, operands):
    queries, keys_page, values_page, residual_page, teacher_page = operands
    head_out, log_total = lax.map(head_forward, (split_heads(queries), split_heads(keys_page), split_heads(values_page)))
    attended = join_heads(head_out).astype(jnp.bfloat16)
    features = residual_page + jnp.dot(attended, output_weight, preferred_element_type=jnp.float32)
    inverse = lax.rsqrt(lax.optimization_barrier(jnp.sum(features * features, axis=1, keepdims=True)) + 1e-06)
    student = features * inverse
    student_rounded = student.astype(jnp.bfloat16)
    teacher_full = teacher_page.astype(jnp.float32)
    teacher_rounded = (teacher_full * lax.rsqrt(lax.optimization_barrier(jnp.sum(teacher_full * teacher_full, axis=1, keepdims=True)) + 1e-06)).astype(jnp.bfloat16)
    student_blocks = student_rounded.reshape(N_PATCH, ROWS, D)
    teacher_blocks = teacher_rounded.reshape(N_PATCH, ROWS, D)
    student_wide = student_blocks.astype(jnp.float32)
    own_tile = gram_tile(student_blocks, teacher_blocks, student_blocks, teacher_blocks)
    gradient = jnp.einsum('xab,xbd->xad', own_tile, student_wide)
    for distance in range(1, ROUNDS + 1):
        lower_student = jnp.roll(student_blocks, distance, axis=0)
        lower_teacher = jnp.roll(teacher_blocks, distance, axis=0)
        upper_student = jnp.roll(student_blocks, -distance, axis=0)
        upper_teacher = jnp.roll(teacher_blocks, -distance, axis=0)
        lower_tile = gram_tile(student_blocks, teacher_blocks, lower_student, lower_teacher)
        gradient = gradient + jnp.einsum('xab,xbd->xad', lower_tile, lower_student.astype(jnp.float32))
        upper_tile = gram_tile(upper_student, upper_teacher, student_blocks, teacher_blocks)
        gradient = gradient + jnp.einsum('xab,xad->xbd', upper_tile, upper_student.astype(jnp.float32))
    gram_grad = 32.0 * gradient.reshape(NP, D)
    d_features = inverse * (gram_grad - student * lax.optimization_barrier(jnp.sum(student * gram_grad, axis=1, keepdims=True)))
    features_grad_rounded = d_features.astype(jnp.bfloat16)
    d_attended = jnp.dot(features_grad_rounded, output_weight.T, preferred_element_type=jnp.float32).astype(jnp.bfloat16)
    weight_term = jnp.dot(attended.T, features_grad_rounded, preferred_element_type=jnp.float32)
    row_dot = lax.optimization_barrier(jnp.sum((d_attended.astype(jnp.float32) * attended.astype(jnp.float32)).reshape(NP, HEADS, HEAD), axis=2)).T
    query_grad, key_grad, value_grad = lax.map(head_backward, (split_heads(queries), split_heads(keys_page), split_heads(values_page), split_heads(d_attended), log_total, row_dot))
    return (join_heads(query_grad), join_heads(key_grad), join_heads(value_grad), d_features, weight_term)

def reference(patch_queries, patch_keys, patch_values, residual, teacher, output_weight):

    def one_page(operands):
        return page_backward(output_weight, operands)
    d_queries, d_keys, d_values, d_features, weight_terms = lax.map(one_page, (patch_queries, patch_keys, patch_values, residual, teacher))
    return (d_queries, d_keys, d_values, d_features, lax.optimization_barrier(jnp.sum(weight_terms, axis=0)))
```

```python
import jax
import jax.numpy as jnp
from jax import lax
from jax.experimental import pallas as pl
from jax.experimental.pallas import tpu as pltpu
from jax.sharding import PartitionSpec as P

MESH = pl.DeviceIdType.MESH
F32 = jnp.float32
BF16 = jnp.bfloat16
ROWS = 256
PAIR = 128
HEAD = 64
OFFSETS = (0, 1, 3, 2)
VMEM_LIMIT = 60 * 1024 * 1024


def position():
    index = lax.axis_index("patch")
    return index // 4, index % 4


def on_patch(z, x):
    return {"patch": z * 4 + x}


def remote(src, dst, send_sem, recv_sem, device):
    return pltpu.make_async_remote_copy(
        src_ref=src,
        dst_ref=dst,
        send_sem=send_sem,
        recv_sem=recv_sem,
        device_id=device,
        device_id_type=MESH,
    )


def meet(peers):
    barrier = pltpu.get_barrier_semaphore()
    for peer in peers:
        pl.semaphore_signal(barrier, inc=1, device_id=peer, device_id_type=MESH)
    pl.semaphore_wait(barrier, len(peers))


def columns(index):
    return pl.ds(pl.multiple_of(index * PAIR, PAIR), PAIR)


def matmul(a, b):
    return jnp.dot(a, b, preferred_element_type=F32)


def matmul_t(a, b):
    return lax.dot_general(a, b, (((1,), (1,)), ((), ())), preferred_element_type=F32)


def head_lanes(rows):
    return lax.broadcasted_iota(jnp.int32, (rows, PAIR), 1) < HEAD


def normalised(block):
    return block * lax.rsqrt(jnp.sum(block * block, axis=1, keepdims=True) + 1e-06)


def forward_kernel(
    q_ref, k_ref, v_ref, t_ref,
    q2, kv, att_full, att2, fac, e_hbm, t_row, t_ud,
    e_buf, m_s, l_s, o_s,
    own_sem, zs, zr, xs, xr, rs, rr, tzs, tzr, txs, txr, trs, trr, as_, ar, a_own, e_sem,
):
    z, x = position()
    right, left, across = (x + 1) % 4, (x + 3) % 4, (x + 2) % 4
    up, down = (z + 1) % 4, (z + 3) % 4
    meet([on_patch((z + d) % 4, x) for d in (1, 2, 3)] + [on_patch(z, right), on_patch(z, left)])

    started = []

    def send(src, dst, send_sem, recv_sem, device):
        copy = remote(src, dst, send_sem, recv_sem, device)
        copy.start()
        started.append(copy)

    for d in (1, 3, 2):
        to = (z + d) % 4
        for i, source in enumerate((k_ref, v_ref)):
            send(source.at[:, columns(to)], kv.at[x, z, i], zs.at[i, d], zr.at[i, d], on_patch(to, x))
    own = [
        pltpu.make_async_copy(k_ref.at[:, columns(z)], kv.at[x, z, 0], own_sem.at[0]),
        pltpu.make_async_copy(v_ref.at[:, columns(z)], kv.at[x, z, 1], own_sem.at[1]),
        pltpu.make_async_copy(q_ref.at[:, columns(z)], q2.at[z], own_sem.at[2]),
    ]
    for copy in own:
        copy.start()
    for d in (1, 3, 2):
        to = (z + d) % 4
        send(q_ref.at[:, columns(to)], q2.at[z], zs.at[2, d], zr.at[2, d], on_patch(to, x))
    for copy in own:
        copy.wait()

    def spread(d):
        at = (z + 4 - d) % 4
        for side, to in enumerate((right, left)):
            send(kv.at[x, at], kv.at[x, at], xs.at[side, d], xr.at[side, d], on_patch(z, to))

    spread(0)
    t_row[x] = normalised(t_ref[...].astype(F32)).astype(BF16)
    for d in (1, 3, 2):
        at = (z + 4 - d) % 4
        for i in range(2):
            slot = kv.at[x, at, i]
            remote(slot, slot, zs.at[i, d], zr.at[i, d], on_patch(at, x)).wait_recv()
        spread(d)
    send(t_row.at[x], t_ud.at[0], tzs.at[0], tzr.at[0], on_patch(up, x))
    send(t_row.at[x], t_ud.at[1], tzs.at[1], tzr.at[1], on_patch(down, x))
    for d in (1, 2, 3):
        at = (z + 4 - d) % 4
        remote(q2.at[at], q2.at[at], zs.at[2, d], zr.at[2, d], on_patch(at, x)).wait_recv()

    first_head = head_lanes(ROWS)

    def chunk(c):
        xc = (x + OFFSETS[c]) % 4

        def block(qt, carry):
            keys = kv[xc, :, 0].reshape(1024, PAIR)
            values = kv[xc, :, 1].reshape(1024, PAIR)
            queries = q2[qt].astype(F32) * (HEAD ** -0.5)
            parts = []
            for h in range(2):
                mask = first_head if h == 0 else jnp.logical_not(first_head)
                masked = jnp.where(mask, queries, 0.0).astype(BF16)
                scores = matmul_t(masked, keys)
                top = jnp.max(scores, axis=1, keepdims=True)
                expo = jnp.exp(scores - top)
                total = jnp.sum(expo, axis=1, keepdims=True)
                rounded = expo.astype(BF16)
                e_buf[c, h, qt] = rounded
                parts.append((top, total, matmul(rounded, values)))
            (m0, l0, o0), (m1, l1, o1) = parts
            m_s[c, qt] = jnp.where(first_head, m0, m1)
            l_s[c, qt] = jnp.where(first_head, l0, l1)
            o_s[c, qt] = jnp.where(first_head, o0, o1)
            return carry

        lax.fori_loop(0, 4, block, 0)
        pltpu.make_async_copy(e_buf.at[c], e_hbm.at[c], e_sem.at[c]).start()

    def arrived(side, slot_x, d):
        at = (z + 4 - d) % 4
        slot = kv.at[slot_x, at]
        remote(slot, slot, xs.at[side, d], xr.at[side, d], on_patch(z, slot_x)).wait_recv()

    chunk(0)
    for d in (0, 1, 3, 2):
        at = (z + 4 - d) % 4
        arrived(1, right, d)
        send(kv.at[right, at, 0], kv.at[right, at, 0], rs.at[0, d], rr.at[0, d], on_patch(z, left))
        arrived(0, left, d)
        send(kv.at[left, at, 1], kv.at[left, at, 1], rs.at[1, d], rr.at[1, d], on_patch(z, right))
    for side, to in enumerate((right, left)):
        send(t_row.at[x], t_row.at[x], txs.at[side], txr.at[side], on_patch(z, to))
    chunk(1)
    chunk(2)
    half = ROWS // 2
    remote(t_row.at[right], t_row.at[right], txs.at[1], txr.at[1], on_patch(z, right)).wait_recv()
    upper = t_row.at[right, pl.ds(0, half)]
    send(upper, upper, trs.at[0], trr.at[0], on_patch(z, left))
    remote(t_row.at[left], t_row.at[left], txs.at[0], txr.at[0], on_patch(z, left)).wait_recv()
    lower = t_row.at[left, pl.ds(half, half)]
    send(lower, lower, trs.at[1], trr.at[1], on_patch(z, right))
    for d in range(4):
        at = (z + 4 - d) % 4
        for i in range(2):
            slot = kv.at[across, at, i]
            remote(slot, slot, rs.at[i, d], rr.at[i, d], on_patch(z, right)).wait_recv()
    chunk(3)

    for qt in range(4):
        top = jnp.maximum(
            jnp.maximum(m_s[0, qt], m_s[1, qt]), jnp.maximum(m_s[2, qt], m_s[3, qt])
        )
        scale = [jnp.exp(m_s[c, qt] - top) for c in range(4)]
        total = sum(scale[c] * l_s[c, qt] for c in range(4))
        joined = sum(scale[c] * o_s[c, qt] for c in range(4))
        inverse = 1.0 / total
        att2[qt] = (joined * inverse).astype(BF16)
        for c in range(4):
            fac[c, qt] = scale[c] * inverse
    for d in (1, 3, 2):
        to = (z + d) % 4
        send(att2.at[to], att_full.at[:, columns(z)], as_.at[d], ar.at[d], on_patch(to, x))
    own_att = pltpu.make_async_copy(att2.at[z], att_full.at[:, columns(z)], a_own)
    own_att.start()
    own_att.wait()
    for d in (1, 2, 3):
        at = (z + 4 - d) % 4
        remote(att2.at[at], att_full.at[:, columns(at)], as_.at[d], ar.at[d], on_patch(at, x)).wait_recv()
    for i in range(2):
        remote(t_ud.at[i], t_ud.at[i], tzs.at[i], tzr.at[i], on_patch(up, x)).wait_recv()
    upper, lower = t_row.at[across, pl.ds(0, half)], t_row.at[across, pl.ds(half, half)]
    remote(upper, upper, trs.at[0], trr.at[0], on_patch(z, right)).wait_recv()
    remote(lower, lower, trs.at[1], trr.at[1], on_patch(z, right)).wait_recv()
    for c in range(4):
        pltpu.make_async_copy(e_buf.at[c], e_hbm.at[c], e_sem.at[c]).wait()
    for copy in started:
        copy.wait_send()


def gram_kernel(
    att_ref, res_ref, w_ref, t_row, t_ud,
    d_features, datt2, w_term,
    s_row, s_ud, out_ud, in_ud, datt, student_s, inverse_s,
    szs, szr, sxs, sxr, srs, srr, bs, br, ds_, dr, d_own,
):
    z, x = position()
    right, left, across = (x + 1) % 4, (x + 3) % 4, (x + 2) % 4
    up, down = (z + 1) % 4, (z + 3) % 4
    half = ROWS // 2
    features = res_ref[...] + matmul(att_ref[...], w_ref[...])
    inverse = lax.rsqrt(jnp.sum(features * features, axis=1, keepdims=True) + 1e-06)
    student = features * inverse
    student_s[...] = student
    inverse_s[...] = jnp.broadcast_to(inverse, inverse_s.shape)
    s_row[x] = student.astype(BF16)
    meet([on_patch((z + d) % 4, x) for d in (1, 2, 3)] + [on_patch(z, right), on_patch(z, left)])

    started = []

    def send(src, dst, send_sem, recv_sem, device):
        copy = remote(src, dst, send_sem, recv_sem, device)
        copy.start()
        started.append(copy)

    send(s_row.at[x], s_ud.at[0], szs.at[0], szr.at[0], on_patch(up, x))
    send(s_row.at[x], s_ud.at[1], szs.at[1], szr.at[1], on_patch(down, x))
    for side, to in enumerate((right, left)):
        send(s_row.at[x], s_row.at[x], sxs.at[side], sxr.at[side], on_patch(z, to))

    remote(s_row.at[right], s_row.at[right], sxs.at[1], sxr.at[1], on_patch(z, right)).wait_recv()
    upper = s_row.at[right, pl.ds(0, half)]
    send(upper, upper, srs.at[0], srr.at[0], on_patch(z, left))
    remote(s_row.at[left], s_row.at[left], sxs.at[0], sxr.at[0], on_patch(z, left)).wait_recv()
    lower = s_row.at[left, pl.ds(half, half)]
    send(lower, lower, srs.at[1], srr.at[1], on_patch(z, right))
    upper, lower = s_row.at[across, pl.ds(0, half)], s_row.at[across, pl.ds(half, half)]
    remote(upper, upper, srs.at[0], srr.at[0], on_patch(z, right)).wait_recv()
    remote(lower, lower, srs.at[1], srr.at[1], on_patch(z, right)).wait_recv()

    def term(students, teachers, keep):
        row_students = s_row[...].reshape(1024, 1024)
        row_teachers = t_row[...].reshape(1024, 1024)
        tile = matmul_t(students, row_students) - matmul_t(teachers, row_teachers)
        if keep is not None:
            tile = jnp.where(keep(lax.broadcasted_iota(jnp.int32, tile.shape, 1)), tile, 0.0)
        return matmul(tile.astype(BF16), row_students)

    for i, to, keep in (
        (0, down, lambda column: column < x * ROWS),
        (1, up, lambda column: column >= (x + 1) * ROWS),
    ):
        remote(s_ud.at[i], s_ud.at[i], szs.at[i], szr.at[i], on_patch(to, x)).wait_recv()
        out_ud[i] = term(s_ud[i], t_ud[i], keep).astype(BF16)
        send(out_ud.at[i], in_ud.at[i], bs.at[i], br.at[i], on_patch(to, x))
    gradient = term(s_row[x], t_row[x], None)
    for i in range(2):
        remote(in_ud.at[i], in_ud.at[i], bs.at[i], br.at[i], on_patch(up, x)).wait_recv()
        gradient = gradient + in_ud[i].astype(F32)
    gram_grad = 32.0 * gradient
    student = student_s[...]
    inverse = inverse_s[:, :1]
    grad = inverse * (gram_grad - student * jnp.sum(student * gram_grad, axis=1, keepdims=True))
    d_features[...] = grad
    rounded = grad.astype(BF16)
    datt[...] = matmul_t(rounded, w_ref[...]).astype(BF16)
    for d in (1, 3, 2):
        to = (z + d) % 4
        send(datt.at[:, columns(to)], datt2.at[z], ds_.at[d], dr.at[d], on_patch(to, x))
    own = pltpu.make_async_copy(datt.at[:, columns(z)], datt2.at[z], d_own)
    own.start()
    transposed = att_ref[...].astype(F32).T.astype(BF16)
    w_term[...] = matmul(transposed, rounded).astype(BF16)
    own.wait()
    for d in (1, 2, 3):
        at = (z + 4 - d) % 4
        remote(datt2.at[at], datt2.at[at], ds_.at[d], dr.at[d], on_patch(at, x)).wait_recv()
    for copy in started:
        copy.wait_send()


def backward_kernel(
    q2, kv, att2, datt2, fac, w_term, e_hbm,
    d_queries, d_keys, d_values, d_weight,
    e_buf, q_t, dq_acc, dk_acc, dv_acc, do_t, part, rs_in, z_out, z_in, dq_out,
    ra, pa, rb, pb, rc, pc, gd, ge,
    e_sem, xs, xr, zs, zr, qs, qr,
    sa, da, sb, db, sc, dc, sd, dd, se, de,
):
    z, x = position()
    dp = lax.axis_index("dp")
    y, z_lo, core = dp // 4, (dp // 2) % 2, dp % 2
    near = y * 2 + core
    ring = z * 2 + z_lo

    def near_device(index):
        return {"dp": (index // 2) * 4 + z_lo * 2 + index % 2}

    def ring_device(index):
        return {"dp": y * 4 + (index % 2) * 2 + core, "patch": (index // 2) * 4 + x}

    for c in (3, 1, 2, 0):
        pltpu.make_async_copy(e_hbm.at[c], e_buf.at[c], e_sem.at[c]).start()
    meet(
        [ring_device((ring + d) % 8) for d in range(1, 8)]
        + [on_patch(z, (x + d) % 4) for d in range(1, 4)]
        + [near_device((near + d) % 8) for d in range(1, 8)]
    )
    started = []

    def send(src, dst, send_sem, recv_sem, device):
        copy = remote(src, dst, send_sem, recv_sem, device)
        copy.start()
        started.append(copy)

    def weight_a():
        for d in range(1, 8):
            to = (near + d) % 8
            send(w_term.at[pl.ds(pl.multiple_of(to * 64, 64), 64)], ra.at[d - 1], sa.at[d], da.at[d], near_device(to))

    def weight_b():
        total = w_term[pl.ds(pl.multiple_of(near * 64, 64), 64)].astype(F32)
        for d in range(1, 8):
            slot = ra.at[d - 1]
            remote(slot, slot, sa.at[d], da.at[d], near_device((near + d) % 8)).wait_recv()
            total = total + slot[...].astype(F32)
        pa[...] = total.astype(BF16)
        for d in range(1, 4):
            to = (x + d) % 4
            send(pa.at[pl.ds(pl.multiple_of(to * 16, 16), 16)], rb.at[d - 1], sb.at[d], db.at[d], on_patch(z, to))

    def weight_c():
        total = pa[pl.ds(pl.multiple_of(x * 16, 16), 16)].astype(F32)
        for d in range(1, 4):
            slot = rb.at[d - 1]
            remote(slot, slot, sb.at[d], db.at[d], on_patch(z, (x + d) % 4)).wait_recv()
            total = total + slot[...].astype(F32)
        pb[...] = total.astype(BF16)
        rc[ring] = pb[...]
        for d in range(1, 8):
            send(pb, rc.at[ring], sc.at[d], dc.at[d], ring_device((ring + d) % 8))

    def weight_d():
        for d in range(1, 8):
            at = (ring + 8 - d) % 8
            remote(rc.at[at], rc.at[at], sc.at[d], dc.at[d], ring_device(at)).wait_recv()
        total = rc[0].astype(F32)
        for i in range(1, 8):
            total = total + rc[i].astype(F32)
        pc[...] = total.astype(BF16)
        gd[x] = pc[...]
        for d in range(1, 4):
            send(pc, gd.at[x], sd.at[d], dd.at[d], on_patch(z, (x + d) % 4))

    def weight_e():
        for d in range(1, 4):
            at = (x + 4 - d) % 4
            remote(gd.at[at], gd.at[at], sd.at[d], dd.at[d], on_patch(z, at)).wait_recv()
        ge[near] = gd[...]
        for d in range(1, 8):
            send(gd, ge.at[near], se.at[d], de.at[d], near_device((near + d) % 8))

    def weight_out():
        for d in range(1, 8):
            at = (near + 8 - d) % 8
            remote(ge.at[at], ge.at[at], se.at[d], de.at[d], near_device(at)).wait_recv()
        d_weight[...] = ge[...].reshape(512, 1024).astype(F32)

    weight_a()
    first_head = head_lanes(ROWS)
    for qt in range(4):
        q_t[qt] = (q2[qt].astype(F32) * (HEAD ** -0.5)).T.astype(BF16)
        dq_acc[qt] = jnp.zeros((ROWS, PAIR), F32)

    def chunk(c):
        xc = (x + OFFSETS[c]) % 4
        pltpu.make_async_copy(e_hbm.at[c], e_buf.at[c], e_sem.at[c]).wait()
        dk_acc[...] = jnp.zeros_like(dk_acc)
        dv_acc[...] = jnp.zeros_like(dv_acc)

        def block(qt, carry):
            keys = kv[xc, :, 0].reshape(1024, PAIR)
            values = kv[xc, :, 1].reshape(1024, PAIR)
            factor = fac[c, qt]
            grads = datt2[qt].astype(F32)
            scaled = grads * factor
            do_t[...] = scaled.T.astype(BF16)
            dots = grads * att2[qt].astype(F32)
            found = []
            for h in range(2):
                mask = first_head if h == 0 else jnp.logical_not(first_head)
                rows = pl.ds(h * HEAD, HEAD)
                masked = jnp.where(mask, scaled, 0.0).astype(BF16)
                row_dot = jnp.sum(jnp.where(mask, dots, 0.0), axis=1, keepdims=True)
                row_dot = row_dot * factor[:, h * HEAD : h * HEAD + 1]
                expo = e_buf[c, h, qt]
                prob_grad = matmul_t(masked, values)
                score_grad = (expo.astype(F32) * (prob_grad - row_dot)).astype(BF16)
                found.append(matmul(score_grad, keys))
                dk_acc[rows] += matmul(q_t[qt, rows], score_grad)
                dv_acc[rows] += matmul(do_t[rows], expo)
            dq_acc[qt] += jnp.where(first_head, found[0], found[1])
            return carry

        lax.fori_loop(0, 4, block, 0)
        part[c, :, 0] = dk_acc[...].T.astype(BF16).reshape(4, ROWS, PAIR)
        part[c, :, 1] = dv_acc[...].T.astype(BF16).reshape(4, ROWS, PAIR)
        if c:
            send(part.at[c], rs_in.at[c - 1], xs.at[c], xr.at[c], on_patch(z, xc))

    chunk(3)
    weight_b()
    chunk(1)
    weight_c()
    chunk(2)
    weight_d()
    chunk(0)
    for qt in range(4):
        dq_out[qt] = (dq_acc[qt] * (HEAD ** -0.5)).astype(BF16)
    for d in (1, 3, 2):
        to = (z + d) % 4
        send(dq_out.at[to], z_in.at[z, 2], qs.at[d], qr.at[d], on_patch(to, x))
    z_in[z, 2] = dq_out[z]
    weight_e()
    for c in range(1, 4):
        slot = rs_in.at[c - 1]
        remote(slot, slot, xs.at[c], xr.at[c], on_patch(z, right_of(x, c))).wait_recv()
    for d in (1, 3, 2, 0):
        to = (z + d) % 4
        total = part[0, to].astype(F32)
        for c in range(3):
            total = total + rs_in[c, to].astype(F32)
        if d:
            z_out[d - 1] = total.astype(BF16)
            send(z_out.at[d - 1], z_in.at[z, pl.ds(0, 2)], zs.at[d], zr.at[d], on_patch(to, x))
        else:
            z_in[z, pl.ds(0, 2)] = total.astype(BF16)
    weight_out()
    for d in (1, 2, 3):
        at = (z + 4 - d) % 4
        slot = z_in.at[at, 2]
        remote(slot, slot, qs.at[d], qr.at[d], on_patch(at, x)).wait_recv()
        slot = z_in.at[at, pl.ds(0, 2)]
        remote(slot, slot, zs.at[d], zr.at[d], on_patch(at, x)).wait_recv()
    for at in range(4):
        lanes = pl.ds(at * PAIR, PAIR)
        d_keys[:, lanes] = z_in[at, 0].astype(F32)
        d_values[:, lanes] = z_in[at, 1].astype(F32)
        d_queries[:, lanes] = z_in[at, 2].astype(F32)
    for copy in started:
        copy.wait_send()


def right_of(x, c):
    return (x + 4 - OFFSETS[c]) % 4


def call(kernel, outs, ins, scratch, collective_id, flops):
    vmem = pl.BlockSpec(memory_space=pltpu.VMEM)
    hbm = pl.BlockSpec(memory_space=pl.ANY)
    return pl.pallas_call(
        kernel,
        out_shape=[jax.ShapeDtypeStruct(shape, dtype) for shape, dtype, _ in outs],
        in_specs=[vmem if on_chip else hbm for on_chip in ins],
        out_specs=[vmem if on_chip else hbm for _, _, on_chip in outs],
        scratch_shapes=scratch,
        compiler_params=pltpu.CompilerParams(
            collective_id=collective_id, has_side_effects=True, vmem_limit_bytes=VMEM_LIMIT
        ),
        cost_estimate=pl.CostEstimate(flops=flops, bytes_accessed=30_000_000, transcendentals=0),
    )


def dma(*shape):
    return pltpu.SemaphoreType.DMA(shape)


def on_device(patch_queries, patch_keys, patch_values, residual, teacher, output_weight):
    e_shape = (4, 2, 4, ROWS, 1024)
    q2, kv, att_full, att2, fac, expo, t_row, t_ud = call(
        forward_kernel,
        [
            ((4, ROWS, PAIR), BF16, True),
            ((4, 4, 2, ROWS, PAIR), BF16, True),
            ((ROWS, 512), BF16, True),
            ((4, ROWS, PAIR), BF16, True),
            ((4, 4, ROWS, PAIR), F32, True),
            (e_shape, BF16, False),
            ((4, ROWS, 1024), BF16, True),
            ((2, ROWS, 1024), BF16, True),
        ],
        [True] * 4,
        [
            pltpu.VMEM(e_shape, BF16),
            pltpu.VMEM((4, 4, ROWS, PAIR), F32),
            pltpu.VMEM((4, 4, ROWS, PAIR), F32),
            pltpu.VMEM((4, 4, ROWS, PAIR), F32),
            dma(3), dma(3, 4), dma(3, 4), dma(2, 4), dma(2, 4), dma(2, 4), dma(2, 4),
            dma(2), dma(2), dma(2), dma(2), dma(2), dma(2),
            dma(4), dma(4), pltpu.SemaphoreType.DMA, dma(4),
        ],
        0,
        4_000_000_000,
    )(patch_queries[0], patch_keys[0], patch_values[0], teacher[0])
    d_features, datt2, w_term = call(
        gram_kernel,
        [((ROWS, 1024), F32, True), ((4, ROWS, PAIR), BF16, True), ((512, 1024), BF16, True)],
        [True] * 5,
        [
            pltpu.VMEM((4, ROWS, 1024), BF16),
            pltpu.VMEM((2, ROWS, 1024), BF16),
            pltpu.VMEM((2, ROWS, 1024), BF16),
            pltpu.VMEM((2, ROWS, 1024), BF16),
            pltpu.VMEM((ROWS, 512), BF16),
            pltpu.VMEM((ROWS, 1024), F32),
            pltpu.VMEM((ROWS, PAIR), F32),
            dma(2), dma(2), dma(2), dma(2), dma(2), dma(2), dma(2), dma(2),
            dma(4), dma(4), pltpu.SemaphoreType.DMA,
        ],
        1,
        6_000_000_000,
    )(att_full, residual[0], output_weight, t_row, t_ud)
    d_queries, d_keys, d_values, d_weight = call(
        backward_kernel,
        [
            ((ROWS, 512), F32, True),
            ((ROWS, 512), F32, True),
            ((ROWS, 512), F32, True),
            ((512, 1024), F32, True),
        ],
        [True] * 6 + [False],
        [
            pltpu.VMEM(e_shape, BF16),
            pltpu.VMEM((4, PAIR, ROWS), BF16),
            pltpu.VMEM((4, ROWS, PAIR), F32),
            pltpu.VMEM((PAIR, 1024), F32),
            pltpu.VMEM((PAIR, 1024), F32),
            pltpu.VMEM((PAIR, ROWS), BF16),
            pltpu.VMEM((4, 4, 2, ROWS, PAIR), BF16),
            pltpu.VMEM((3, 4, 2, ROWS, PAIR), BF16),
            pltpu.VMEM((3, 2, ROWS, PAIR), BF16),
            pltpu.VMEM((4, 3, ROWS, PAIR), BF16),
            pltpu.VMEM((4, ROWS, PAIR), BF16),
            pltpu.VMEM((7, 64, 1024), BF16),
            pltpu.VMEM((64, 1024), BF16),
            pltpu.VMEM((3, 16, 1024), BF16),
            pltpu.VMEM((16, 1024), BF16),
            pltpu.VMEM((8, 16, 1024), BF16),
            pltpu.VMEM((16, 1024), BF16),
            pltpu.VMEM((4, 16, 1024), BF16),
            pltpu.VMEM((8, 4, 16, 1024), BF16),
            dma(4), dma(4), dma(4), dma(4), dma(4), dma(4), dma(4),
            dma(8), dma(8), dma(4), dma(4), dma(8), dma(8), dma(4), dma(4), dma(8), dma(8),
        ],
        2,
        8_000_000_000,
    )(q2, kv, att2, datt2, fac, w_term, expo)
    return d_queries[None], d_keys[None], d_values[None], d_features[None], d_weight


def solution(mesh):
    placed = P("dp", "patch", None)
    return jax.shard_map(
        on_device,
        mesh=mesh,
        in_specs=(placed,) * 5 + (P(),),
        out_specs=(placed,) * 4 + (P(),),
        check_vma=False,
    )
```

```python
from types import SimpleNamespace

import jax
import jax.numpy as jnp
from jax import lax
from jax.experimental import pallas as pl
from jax.experimental.pallas import tpu as pltpu
from jax.sharding import PartitionSpec as P

MESH = pl.DeviceIdType.MESH
F32 = jnp.float32
BF16 = jnp.bfloat16
ROWS = 256
HALF = 128
PAIR = 128
HEAD = 64
D = 1024
KEYS = 1024
PIECES = 2
PIECE = ROWS // PIECES
SCALE = HEAD ** -0.5
OFFSETS = (0, 1, 3, 2)
VMEM_LIMIT = 60 * 1024 * 1024


def dma(*shape):
    return pltpu.SemaphoreType.DMA(shape)


def on_chip(*shape, dtype=BF16):
    return pltpu.VMEM(shape, dtype)


OUTPUTS = {
    "z_in": ((4, 3, ROWS, PAIR), BF16),
    "ge": ((8, 4, 16, D), BF16),
    "d_features": ((ROWS, D), F32),
}
SCRATCH = {
    "t_raw": on_chip(ROWS, D),
    "res": on_chip(ROWS, D, dtype=F32),
    "w": on_chip(512, D),
    "q2": on_chip(4, ROWS, PAIR),
    "kv": on_chip(4, 4, 2, ROWS, PAIR),
    "expo": on_chip(4, 2, 4, ROWS, KEYS),
    "m": on_chip(4, 4, ROWS, PAIR, dtype=F32),
    "l": on_chip(4, 4, ROWS, PAIR, dtype=F32),
    "o": on_chip(4, 4, ROWS, PAIR, dtype=F32),
    "att2": on_chip(4, ROWS, PAIR),
    "att_full": on_chip(ROWS, 512),
    "local": dma(6),
    "qkv_s": dma(3, 4), "qkv_r": dma(3, 4),
    "spread_s": dma(2, 4), "spread_r": dma(2, 4),
    "relay_s": dma(2, 4), "relay_r": dma(2, 4),
    "att_s": dma(4), "att_r": dma(4), "att_own": dma(1),
    "t_row": on_chip(4, ROWS, D),
    "t_sh": on_chip(ROWS, D),
    "t_ext": on_chip(ROWS, D),
    "tile_own": on_chip(ROWS, KEYS, dtype=F32),
    "tile_sh": on_chip(ROWS, KEYS, dtype=F32),
    "s_row": on_chip(4, ROWS, D),
    "s_sh": on_chip(PIECES, PIECE, D),
    "s_ext": on_chip(PIECES, PIECE, D),
    "back_out": on_chip(PIECES, PIECE, D),
    "back_in": on_chip(PIECES, PIECE, D),
    "student": on_chip(ROWS, D, dtype=F32),
    "inverse": on_chip(ROWS, PAIR, dtype=F32),
    "gradient": on_chip(ROWS, D, dtype=F32),
    "grad": on_chip(ROWS, D),
    "datt": on_chip(ROWS, 512),
    "datt2": on_chip(4, ROWS, PAIR),
    "tx_s": dma(2), "tx_r": dma(2), "tr_s": dma(2), "tr_r": dma(2),
    "tz_s": dma(1), "tz_r": dma(1), "te_s": dma(1), "te_r": dma(1),
    "sx_s": dma(2), "sx_r": dma(2), "sr_s": dma(2), "sr_r": dma(2),
    "sz_s": dma(PIECES), "sz_r": dma(PIECES), "se_s": dma(PIECES), "se_r": dma(PIECES),
    "back_s": dma(PIECES), "back_r": dma(PIECES),
    "datt_s": dma(PIECES, 4), "datt_r": dma(PIECES, 4), "datt_own": dma(PIECES),
    "q_t": on_chip(4, PAIR, ROWS),
    "do_t": on_chip(PAIR, ROWS),
    "dq": on_chip(4, ROWS, PAIR, dtype=F32),
    "dk": on_chip(PAIR, KEYS, dtype=F32),
    "dv": on_chip(PAIR, KEYS, dtype=F32),
    "part": on_chip(4, 2, 4, ROWS, PAIR),
    "pass_in": on_chip(2, 4, ROWS, PAIR),
    "sum_in": on_chip(2, 2, 4, ROWS, PAIR),
    "z_out": on_chip(4, 2, ROWS, PAIR),
    "dq_out": on_chip(4, ROWS, PAIR),
    "pass_s": dma(2), "pass_r": dma(2), "sum_s": dma(2), "sum_r": dma(2),
    "zkv_s": dma(4), "zkv_r": dma(4), "zq_s": dma(4), "zq_r": dma(4),
    "w_term": on_chip(512, D),
    "ra": on_chip(7, 64, D), "pa": on_chip(64, D),
    "rb": on_chip(3, 16, D), "pb": on_chip(16, D),
    "rc": on_chip(8, 16, D), "pc": on_chip(16, D),
    "gd": on_chip(4, 16, D),
    "wa_s": dma(8), "wa_r": dma(8), "wb_s": dma(4), "wb_r": dma(4), "wc_s": dma(8), "wc_r": dma(8),
    "wd_s": dma(4), "wd_r": dma(4), "we_s": dma(8), "we_r": dma(8),
}
INPUTS = ("q", "k", "v", "teacher", "residual", "weight")
NAMES = INPUTS + tuple(OUTPUTS) + tuple(SCRATCH)


def on_patch(z, x):
    return {"patch": z * 4 + x}


def remote(src, dst, send_sem, recv_sem, device):
    return pltpu.make_async_remote_copy(
        src_ref=src,
        dst_ref=dst,
        send_sem=send_sem,
        recv_sem=recv_sem,
        device_id=device,
        device_id_type=MESH,
    )


def columns(index):
    return pl.ds(pl.multiple_of(index * PAIR, PAIR), PAIR)


def matmul(a, b):
    return jnp.dot(a, b, preferred_element_type=F32)


def matmul_t(a, b):
    return lax.dot_general(a, b, (((1,), (1,)), ((), ())), preferred_element_type=F32)


def kernel(*refs):
    r = SimpleNamespace(**dict(zip(NAMES, refs, strict=True)))
    index = lax.axis_index("patch")
    z, x = index // 4, index % 4
    dp = lax.axis_index("dp")
    y, z_lo, core = dp // 4, (dp // 2) % 2, dp % 2
    near, ring = y * 2 + core, z * 2 + z_lo
    right, left, across = (x + 1) % 4, (x + 3) % 4, (x + 2) % 4
    high = x // 2
    step = 3 - 2 * high
    shift_to, shift_from = (z + step) % 4, (z + 4 - step) % 4
    swap = x + 1 - 2 * (x % 2)
    inner = (x * (3 - x)) // 2

    def near_device(i):
        return {"dp": (i // 2) * 4 + z_lo * 2 + i % 2}

    def ring_device(i):
        return {"dp": y * 4 + (i % 2) * 2 + core, "patch": (i // 2) * 4 + x}

    started = []

    def send(src, dst, send_sem, recv_sem, device):
        copy = remote(src, dst, send_sem, recv_sem, device)
        copy.start()
        started.append(copy)

    def await_at(slot, send_sem, recv_sem, device):
        remote(slot, slot, send_sem, recv_sem, device).wait_recv()

    local = [
        pltpu.make_async_copy(r.teacher, r.t_raw, r.local.at[0]),
        pltpu.make_async_copy(r.k.at[:, columns(z)], r.kv.at[x, z, 0], r.local.at[1]),
        pltpu.make_async_copy(r.v.at[:, columns(z)], r.kv.at[x, z, 1], r.local.at[2]),
        pltpu.make_async_copy(r.q.at[:, columns(z)], r.q2.at[z], r.local.at[3]),
        pltpu.make_async_copy(r.residual, r.res, r.local.at[4]),
        pltpu.make_async_copy(r.weight, r.w, r.local.at[5]),
    ]
    for copy in local:
        copy.start()
    peers = (
        [ring_device((ring + d) % 8) for d in range(1, 8)]
        + [on_patch(z, (x + d) % 4) for d in range(1, 4)]
        + [near_device((near + d) % 8) for d in range(1, 8)]
    )
    barrier = pltpu.get_barrier_semaphore()
    for peer in peers:
        pl.semaphore_signal(barrier, inc=1, device_id=peer, device_id_type=MESH)
    pl.semaphore_wait(barrier, len(peers))

    for d in (1, 3, 2):
        to = (z + d) % 4
        for i, source in enumerate((r.k, r.v)):
            send(source.at[:, columns(to)], r.kv.at[x, z, i], r.qkv_s.at[i, d], r.qkv_r.at[i, d], on_patch(to, x))
    for d in (1, 3, 2):
        to = (z + d) % 4
        send(r.q.at[:, columns(to)], r.q2.at[z], r.qkv_s.at[2, d], r.qkv_r.at[2, d], on_patch(to, x))

    def spread(d):
        at = (z + 4 - d) % 4
        for side, to in enumerate((right, left)):
            slot = r.kv.at[x, at]
            send(slot, slot, r.spread_s.at[side, d], r.spread_r.at[side, d], on_patch(z, to))

    local[1].wait()
    local[2].wait()
    spread(0)
    local[0].wait()
    teacher = r.t_raw[...].astype(F32)
    r.t_row[x] = (
        teacher * lax.rsqrt(jnp.sum(teacher * teacher, axis=1, keepdims=True) + 1e-06)
    ).astype(BF16)
    for side, to in enumerate((right, left)):
        send(r.t_row.at[x], r.t_row.at[x], r.tx_s.at[side], r.tx_r.at[side], on_patch(z, to))
    for d in (1, 3, 2):
        at = (z + 4 - d) % 4
        for i in range(2):
            await_at(r.kv.at[x, at, i], r.qkv_s.at[i, d], r.qkv_r.at[i, d], on_patch(at, x))
        spread(d)
    send(r.t_row.at[x], r.t_sh, r.tz_s.at[0], r.tz_r.at[0], on_patch(shift_to, x))
    local[3].wait()
    for d in (1, 3, 2):
        at = (z + 4 - d) % 4
        await_at(r.q2.at[at], r.qkv_s.at[2, d], r.qkv_r.at[2, d], on_patch(at, x))

    first_head = lax.broadcasted_iota(jnp.int32, (ROWS, PAIR), 1) < HEAD

    def forward_block(c, qt):
        xc = (x + OFFSETS[c]) % 4
        keys = r.kv[xc, :, 0].reshape(KEYS, PAIR)
        values = r.kv[xc, :, 1].reshape(KEYS, PAIR)
        queries = r.q2[qt].astype(F32) * SCALE
        parts = []
        for h in range(2):
            mask = first_head if h == 0 else jnp.logical_not(first_head)
            masked = jnp.where(mask, queries, 0.0).astype(BF16)
            scores = matmul_t(masked, keys)
            top = jnp.max(scores, axis=1, keepdims=True)
            expo = jnp.exp(scores - top)
            total = jnp.sum(expo, axis=1, keepdims=True)
            rounded = expo.astype(BF16)
            r.expo[c, h, qt] = rounded
            parts.append((top, total, matmul(rounded, values)))
        (m0, l0, o0), (m1, l1, o1) = parts
        r.m[c, qt] = jnp.where(first_head, m0, m1)
        r.l[c, qt] = jnp.where(first_head, l0, l1)
        r.o[c, qt] = jnp.where(first_head, o0, o1)

    def forward_chunk(c):
        def block(qt, carry):
            forward_block(c, qt)
            return carry

        lax.fori_loop(0, 4, block, 0)

    def join(qt):
        tops = [r.m[c, qt] for c in range(4)]
        top = jnp.maximum(jnp.maximum(tops[0], tops[1]), jnp.maximum(tops[2], tops[3]))
        scale = [jnp.exp(tops[c] - top) for c in range(4)]
        total = sum(scale[c] * r.l[c, qt] for c in range(4))
        joined = sum(scale[c] * r.o[c, qt] for c in range(4))
        inverse = 1.0 / total
        r.att2[qt] = (joined * inverse).astype(BF16)
        for c in range(4):
            r.m[c, qt] = scale[c] * inverse

    forward_chunk(0)
    for d in (0, 1, 3, 2):
        at = (z + 4 - d) % 4
        await_at(r.kv.at[right, at], r.spread_s.at[1, d], r.spread_r.at[1, d], on_patch(z, right))
        slot = r.kv.at[right, at, 0]
        send(slot, slot, r.relay_s.at[0, d], r.relay_r.at[0, d], on_patch(z, left))
        await_at(r.kv.at[left, at], r.spread_s.at[0, d], r.spread_r.at[0, d], on_patch(z, left))
        slot = r.kv.at[left, at, 1]
        send(slot, slot, r.relay_s.at[1, d], r.relay_r.at[1, d], on_patch(z, right))
    forward_chunk(1)

    def pass_on(row, x_s, x_r, on_s, on_r):
        await_at(row.at[right], x_s.at[1], x_r.at[1], on_patch(z, right))
        slot = row.at[right, pl.ds(0, HALF)]
        send(slot, slot, on_s.at[0], on_r.at[0], on_patch(z, left))
        await_at(row.at[left], x_s.at[0], x_r.at[0], on_patch(z, left))
        slot = row.at[left, pl.ds(HALF, HALF)]
        send(slot, slot, on_s.at[1], on_r.at[1], on_patch(z, right))

    def await_across(row, on_s, on_r):
        for i in range(2):
            await_at(row.at[across, pl.ds(i * HALF, HALF)], on_s.at[i], on_r.at[i], on_patch(z, right))

    pass_on(r.t_row, r.tx_s, r.tx_r, r.tr_s, r.tr_r)
    forward_chunk(2)
    for d in range(4):
        at = (z + 4 - d) % 4
        for i in range(2):
            await_at(r.kv.at[across, at, i], r.relay_s.at[i, d], r.relay_r.at[i, d], on_patch(z, right))
    for d in (1, 3, 2, 0):
        to = (z + d) % 4
        forward_block(3, to)
        join(to)
        if d:
            send(r.att2.at[to], r.att_full.at[:, columns(z)], r.att_s.at[d], r.att_r.at[d], on_patch(to, x))
    own = pltpu.make_async_copy(r.att2.at[z], r.att_full.at[:, columns(z)], r.att_own.at[0])
    own.start()

    await_at(r.t_sh, r.tz_s.at[0], r.tz_r.at[0], on_patch(shift_from, x))
    send(r.t_sh, r.t_ext, r.te_s.at[0], r.te_r.at[0], on_patch(z, swap))
    own.wait()
    local[4].wait()
    local[5].wait()
    for d in (1, 3, 2):
        at = (z + 4 - d) % 4
        await_at(r.att_full.at[:, columns(at)], r.att_s.at[d], r.att_r.at[d], on_patch(at, x))

    features = r.res[...] + matmul(r.att_full[...], r.w[...])
    inverse = lax.rsqrt(jnp.sum(features * features, axis=1, keepdims=True) + 1e-06)
    student = features * inverse
    r.s_row[x] = student.astype(BF16)
    for p in range(PIECES):
        source = r.s_row.at[x, pl.ds(p * PIECE, PIECE)]
        send(source, r.s_sh.at[p], r.sz_s.at[p], r.sz_r.at[p], on_patch(shift_to, x))
    for side, to in enumerate((right, left)):
        send(r.s_row.at[x], r.s_row.at[x], r.sx_s.at[side], r.sx_r.at[side], on_patch(z, to))
    r.student[...] = student
    r.inverse[...] = jnp.broadcast_to(inverse, (ROWS, PAIR))

    await_across(r.t_row, r.tr_s, r.tr_r)
    r.tile_sh[...] = matmul_t(r.t_sh[...], r.t_row[...].reshape(KEYS, D))
    pass_on(r.s_row, r.sx_s, r.sx_r, r.sr_s, r.sr_r)
    r.tile_own[...] = matmul_t(r.t_row[x], r.t_row[...].reshape(KEYS, D))
    await_across(r.s_row, r.sr_s, r.sr_r)

    first = (1 - high) * (x + 1) * ROWS
    last = KEYS - high * (KEYS - x * ROWS)
    for p in range(PIECES):
        await_at(r.s_sh.at[p], r.sz_s.at[p], r.sz_r.at[p], on_patch(shift_from, x))
        send(r.s_sh.at[p], r.s_ext.at[p], r.se_s.at[p], r.se_r.at[p], on_patch(z, swap))
        row = r.s_row[...].reshape(KEYS, D)
        tile = matmul_t(r.s_sh[p], row) - r.tile_sh[pl.ds(p * PIECE, PIECE)]
        at = lax.broadcasted_iota(jnp.int32, tile.shape, 1)
        tile = jnp.where(jnp.logical_and(at >= first, at < last), tile, 0.0)
        r.back_out[p] = matmul(tile.astype(BF16), row).astype(BF16)
        send(r.back_out.at[p], r.back_in.at[p], r.back_s.at[p], r.back_r.at[p], on_patch(shift_from, x))
    row = r.s_row[...].reshape(KEYS, D)
    own_tile = matmul_t(r.s_row[x], row) - r.tile_own[...]
    r.gradient[...] = matmul(own_tile.astype(BF16), row)
    await_at(r.t_ext, r.te_s.at[0], r.te_r.at[0], on_patch(z, swap))
    for p in range(PIECES):
        await_at(r.s_ext.at[p], r.se_s.at[p], r.se_r.at[p], on_patch(z, swap))
    other = r.s_ext[...].reshape(ROWS, D)
    tile = matmul_t(r.s_row[x], other) - matmul_t(r.t_row[x], r.t_ext[...])
    tile = jnp.where(lax.broadcasted_iota(jnp.int32, tile.shape, 1) < inner * ROWS, tile, 0.0)
    r.gradient[...] += matmul(tile.astype(BF16), other)

    datt_own = []
    for p in range(PIECES):
        rows = pl.ds(p * PIECE, PIECE)
        await_at(r.back_in.at[p], r.back_s.at[p], r.back_r.at[p], on_patch(shift_to, x))
        gram_grad = 32.0 * (r.gradient[rows] + r.back_in[p].astype(F32))
        student = r.student[rows]
        dot = jnp.sum(student * gram_grad, axis=1, keepdims=True)
        grad = r.inverse[rows, :1] * (gram_grad - student * dot)
        r.d_features[rows] = grad
        rounded = grad.astype(BF16)
        r.grad[rows] = rounded
        r.datt[rows] = matmul_t(rounded, r.w[...]).astype(BF16)
        for d in (1, 3, 2):
            to = (z + d) % 4
            source = r.datt.at[rows, columns(to)]
            send(source, r.datt2.at[z, rows], r.datt_s.at[p, d], r.datt_r.at[p, d], on_patch(to, x))
        own = pltpu.make_async_copy(r.datt.at[rows, columns(z)], r.datt2.at[z, rows], r.datt_own.at[p])
        own.start()
        datt_own.append(own)
    transposed = r.att_full[...].astype(F32).T.astype(BF16)
    r.w_term[...] = matmul(transposed, r.grad[...]).astype(BF16)

    def weight_a():
        for d in range(1, 8):
            to = (near + d) % 8
            rows = pl.ds(pl.multiple_of(to * 64, 64), 64)
            send(r.w_term.at[rows], r.ra.at[d - 1], r.wa_s.at[d], r.wa_r.at[d], near_device(to))

    def weight_b():
        total = r.w_term[pl.ds(pl.multiple_of(near * 64, 64), 64)].astype(F32)
        for d in range(1, 8):
            await_at(r.ra.at[d - 1], r.wa_s.at[d], r.wa_r.at[d], near_device((near + d) % 8))
            total = total + r.ra[d - 1].astype(F32)
        r.pa[...] = total.astype(BF16)
        for d in range(1, 4):
            to = (x + d) % 4
            rows = pl.ds(pl.multiple_of(to * 16, 16), 16)
            send(r.pa.at[rows], r.rb.at[d - 1], r.wb_s.at[d], r.wb_r.at[d], on_patch(z, to))

    def weight_c():
        total = r.pa[pl.ds(pl.multiple_of(x * 16, 16), 16)].astype(F32)
        for d in range(1, 4):
            await_at(r.rb.at[d - 1], r.wb_s.at[d], r.wb_r.at[d], on_patch(z, (x + d) % 4))
            total = total + r.rb[d - 1].astype(F32)
        r.pb[...] = total.astype(BF16)
        r.rc[ring] = r.pb[...]
        for d in range(1, 8):
            send(r.pb, r.rc.at[ring], r.wc_s.at[d], r.wc_r.at[d], ring_device((ring + d) % 8))

    def weight_d():
        for d in range(1, 8):
            at = (ring + 8 - d) % 8
            await_at(r.rc.at[at], r.wc_s.at[d], r.wc_r.at[d], ring_device(at))
        total = r.rc[0].astype(F32)
        for i in range(1, 8):
            total = total + r.rc[i].astype(F32)
        r.pc[...] = total.astype(BF16)
        r.gd[x] = r.pc[...]
        for d in range(1, 4):
            send(r.pc, r.gd.at[x], r.wd_s.at[d], r.wd_r.at[d], on_patch(z, (x + d) % 4))

    def weight_e():
        for d in range(1, 4):
            at = (x + 4 - d) % 4
            await_at(r.gd.at[at], r.wd_s.at[d], r.wd_r.at[d], on_patch(z, at))
        r.ge[near] = r.gd[...]
        for d in range(1, 8):
            send(r.gd, r.ge.at[near], r.we_s.at[d], r.we_r.at[d], near_device((near + d) % 8))

    def weight_out():
        for d in range(1, 8):
            at = (near + 8 - d) % 8
            await_at(r.ge.at[at], r.we_s.at[d], r.we_r.at[d], near_device(at))

    weight_a()
    for qt in range(4):
        r.q_t[qt] = (r.q2[qt].astype(F32) * SCALE).T.astype(BF16)
        r.dq[qt] = jnp.zeros((ROWS, PAIR), F32)
    for p in range(PIECES):
        datt_own[p].wait()
        for d in (1, 3, 2):
            at = (z + 4 - d) % 4
            slot = r.datt2.at[at, pl.ds(p * PIECE, PIECE)]
            await_at(slot, r.datt_s.at[p, d], r.datt_r.at[p, d], on_patch(at, x))

    def backward_chunk(c):
        xc = (x + OFFSETS[c]) % 4
        r.dk[...] = jnp.zeros((PAIR, KEYS), F32)
        r.dv[...] = jnp.zeros((PAIR, KEYS), F32)

        def block(qt, carry):
            keys = r.kv[xc, :, 0].reshape(KEYS, PAIR)
            values = r.kv[xc, :, 1].reshape(KEYS, PAIR)
            factor = r.m[c, qt]
            grads = r.datt2[qt].astype(F32)
            scaled = grads * factor
            r.do_t[...] = scaled.T.astype(BF16)
            dots = grads * r.att2[qt].astype(F32)
            found = []
            for h in range(2):
                mask = first_head if h == 0 else jnp.logical_not(first_head)
                rows = pl.ds(h * HEAD, HEAD)
                masked = jnp.where(mask, scaled, 0.0).astype(BF16)
                row_dot = jnp.sum(jnp.where(mask, dots, 0.0), axis=1, keepdims=True)
                row_dot = row_dot * factor[:, h * HEAD : h * HEAD + 1]
                expo = r.expo[c, h, qt]
                prob_grad = matmul_t(masked, values)
                score_grad = (expo.astype(F32) * (prob_grad - row_dot)).astype(BF16)
                found.append(matmul(score_grad, keys))
                r.dk[rows] += matmul(r.q_t[qt, rows], score_grad)
                r.dv[rows] += matmul(r.do_t[rows], expo)
            r.dq[qt] += jnp.where(first_head, found[0], found[1])
            return carry

        lax.fori_loop(0, 4, block, 0)
        return r.dk[...].T.reshape(4, ROWS, PAIR), r.dv[...].T.reshape(4, ROWS, PAIR)

    dk, dv = backward_chunk(3)
    r.part[3, 0], r.part[3, 1] = dk.astype(BF16), dv.astype(BF16)
    send(r.part.at[3, 0], r.pass_in.at[0], r.pass_s.at[0], r.pass_r.at[0], on_patch(z, right))
    send(r.part.at[3, 1], r.pass_in.at[1], r.pass_s.at[1], r.pass_r.at[1], on_patch(z, left))
    weight_b()
    dk, dv = backward_chunk(1)
    await_at(r.pass_in.at[0], r.pass_s.at[0], r.pass_r.at[0], on_patch(z, left))
    r.part[1, 0], r.part[1, 1] = (dk + r.pass_in[0].astype(F32)).astype(BF16), dv.astype(BF16)
    send(r.part.at[1], r.sum_in.at[0], r.sum_s.at[0], r.sum_r.at[0], on_patch(z, right))
    weight_c()
    dk, dv = backward_chunk(2)
    await_at(r.pass_in.at[1], r.pass_s.at[1], r.pass_r.at[1], on_patch(z, right))
    r.part[2, 0], r.part[2, 1] = dk.astype(BF16), (dv + r.pass_in[1].astype(F32)).astype(BF16)
    send(r.part.at[2], r.sum_in.at[1], r.sum_s.at[1], r.sum_r.at[1], on_patch(z, left))
    weight_d()
    dk, dv = backward_chunk(0)
    r.part[0, 0], r.part[0, 1] = dk.astype(BF16), dv.astype(BF16)
    for d in (1, 3, 2, 0):
        to = (z + d) % 4
        r.dq_out[to] = (r.dq[to] * SCALE).astype(BF16)
        if d:
            send(r.dq_out.at[to], r.z_in.at[z, 2], r.zq_s.at[d], r.zq_r.at[d], on_patch(to, x))
        else:
            r.z_in[z, 2] = r.dq_out[z]
    weight_e()
    await_at(r.sum_in.at[0], r.sum_s.at[0], r.sum_r.at[0], on_patch(z, left))
    await_at(r.sum_in.at[1], r.sum_s.at[1], r.sum_r.at[1], on_patch(z, right))
    for d in (1, 3, 2, 0):
        to = (z + d) % 4
        for i in range(2):
            total = r.part[0, i, to].astype(F32)
            total = total + r.sum_in[0, i, to].astype(F32) + r.sum_in[1, i, to].astype(F32)
            if d:
                r.z_out[d, i] = total.astype(BF16)
            else:
                r.z_in[z, i] = total.astype(BF16)
        if d:
            send(r.z_out.at[d], r.z_in.at[z, pl.ds(0, 2)], r.zkv_s.at[d], r.zkv_r.at[d], on_patch(to, x))
    weight_out()
    for d in (1, 3, 2):
        at = (z + 4 - d) % 4
        await_at(r.z_in.at[at, 2], r.zq_s.at[d], r.zq_r.at[d], on_patch(at, x))
        await_at(r.z_in.at[at, pl.ds(0, 2)], r.zkv_s.at[d], r.zkv_r.at[d], on_patch(at, x))
    for copy in started:
        copy.wait_send()


def finish(z_in, weight, features, d_queries, d_keys, d_values, d_weight, d_features):
    d_keys[...] = z_in[0, 0].astype(F32)
    d_values[...] = z_in[0, 1].astype(F32)
    d_queries[...] = z_in[0, 2].astype(F32)
    d_weight[...] = weight[...].astype(F32)
    d_features[...] = features[...]


def on_device(patch_queries, patch_keys, patch_values, residual, teacher, output_weight):
    vmem = pl.BlockSpec(memory_space=pltpu.VMEM)
    hbm = pl.BlockSpec(memory_space=pl.ANY)
    z_in, weight, features = pl.pallas_call(
        kernel,
        out_shape=[jax.ShapeDtypeStruct(shape, dtype) for shape, dtype in OUTPUTS.values()],
        in_specs=[hbm] * 6,
        out_specs=[vmem] * 3,
        scratch_shapes=list(SCRATCH.values()),
        compiler_params=pltpu.CompilerParams(
            collective_id=0, has_side_effects=True, vmem_limit_bytes=VMEM_LIMIT
        ),
        cost_estimate=pl.CostEstimate(
            flops=18_000_000_000, bytes_accessed=10_000_000, transcendentals=9_000_000
        ),
    )(patch_queries[0], patch_keys[0], patch_values[0], teacher[0], residual[0], output_weight)
    head_columns = pl.BlockSpec((ROWS, PAIR), lambda i: (0, i))
    d_queries, d_keys, d_values, d_weight, d_features = pl.pallas_call(
        finish,
        grid=(4,),
        out_shape=[jax.ShapeDtypeStruct((ROWS, 512), F32)] * 3
        + [jax.ShapeDtypeStruct((512, D), F32), jax.ShapeDtypeStruct((ROWS, D), F32)],
        in_specs=[
            pl.BlockSpec((1, 3, ROWS, PAIR), lambda i: (i, 0, 0, 0)),
            pl.BlockSpec((PAIR, D), lambda i: (i, 0)),
            pl.BlockSpec((64, D), lambda i: (i, 0)),
        ],
        out_specs=[head_columns] * 3
        + [pl.BlockSpec((PAIR, D), lambda i: (i, 0)), pl.BlockSpec((64, D), lambda i: (i, 0))],
    )(z_in, weight.reshape(512, D), features)
    return d_queries[None], d_keys[None], d_values[None], d_features[None], d_weight


def solution(mesh):
    placed = P("dp", "patch", None)
    return jax.shard_map(
        on_device,
        mesh=mesh,
        in_specs=(placed,) * 5 + (P(),),
        out_specs=(placed,) * 4 + (P(),),
        check_vma=False,
    )
```

```python
from types import SimpleNamespace

import jax
import jax.numpy as jnp
from jax import lax
from jax.experimental import pallas as pl
from jax.experimental.pallas import tpu as pltpu
from jax.sharding import PartitionSpec as P

MESH = pl.DeviceIdType.MESH
F32 = jnp.float32
BF16 = jnp.bfloat16
ROWS = 256
HALF = 128
PAIR = 128
HEAD = 64
D = 1024
KEYS = 1024
QUERIES = 512
SCALE = HEAD ** -0.5
OFFSETS = (0, 1, 3, 2)
VMEM_LIMIT = 60 * 1024 * 1024


def dma(*shape):
    return pltpu.SemaphoreType.DMA(shape)


def on_chip(*shape, dtype=BF16):
    return pltpu.VMEM(shape, dtype)


OUTPUTS = {
    "z_in": ((4, 3, 2, HALF, PAIR), BF16),
    "ge": ((8, 4, 16, D), BF16),
    "d_features": ((ROWS, D), F32),
}
SCRATCH = {
    "t_raw": on_chip(ROWS, D),
    "res": on_chip(ROWS, D, dtype=F32),
    "w": on_chip(512, D),
    "q2": on_chip(2, 4, HALF, PAIR),
    "kv": on_chip(4, 2, 4, 2, HALF, PAIR),
    "expo": on_chip(4, 2, 2, 4, HALF, KEYS),
    "m": on_chip(4, 2, 4, HALF, PAIR, dtype=F32),
    "l": on_chip(4, 2, 4, HALF, PAIR, dtype=F32),
    "o": on_chip(4, 2, 4, HALF, PAIR, dtype=F32),
    "att2": on_chip(2, 4, HALF, PAIR),
    "att_full": on_chip(ROWS, 512),
    "local": dma(6),
    "qkv_s": dma(3, 4), "qkv_r": dma(3, 4),
    "spread_s": dma(2, 4), "spread_r": dma(2, 4),
    "relay_s": dma(2, 4), "relay_r": dma(2, 4),
    "att_s": dma(2, 4), "att_r": dma(2, 4), "att_own": dma(2),
    "t_row": on_chip(4, ROWS, D),
    "t_sh": on_chip(ROWS, D),
    "t_ext": on_chip(ROWS, D),
    "tile_own": on_chip(ROWS, KEYS, dtype=F32),
    "tile_sh": on_chip(ROWS, KEYS, dtype=F32),
    "s_row": on_chip(4, ROWS, D),
    "s_sh": on_chip(2, HALF, D),
    "s_ext": on_chip(2, HALF, D),
    "back_out": on_chip(2, HALF, D),
    "back_in": on_chip(2, HALF, D),
    "student": on_chip(ROWS, D, dtype=F32),
    "inverse": on_chip(ROWS, PAIR, dtype=F32),
    "gradient": on_chip(ROWS, D, dtype=F32),
    "grad": on_chip(ROWS, D),
    "datt": on_chip(ROWS, 512),
    "datt2": on_chip(2, 4, HALF, PAIR),
    "tx_s": dma(2), "tx_r": dma(2), "tr_s": dma(2), "tr_r": dma(2),
    "tz_s": dma(1), "tz_r": dma(1), "te_s": dma(1), "te_r": dma(1),
    "sx_s": dma(2, 2), "sx_r": dma(2, 2), "sr_s": dma(2), "sr_r": dma(2),
    "sz_s": dma(2), "sz_r": dma(2), "se_s": dma(2), "se_r": dma(2),
    "back_s": dma(2), "back_r": dma(2),
    "datt_s": dma(2, 4), "datt_r": dma(2, 4), "datt_own": dma(2),
    "q_t": on_chip(2, PAIR, QUERIES),
    "do_m": on_chip(4, 2, 2, QUERIES, PAIR),
    "do_t": on_chip(4, 2, PAIR, QUERIES),
    "dots": on_chip(4, 2, QUERIES, PAIR, dtype=F32),
    "dq": on_chip(2, QUERIES, PAIR, dtype=F32),
    "dk": on_chip(PAIR, QUERIES, dtype=F32),
    "dv": on_chip(PAIR, QUERIES, dtype=F32),
    "part": on_chip(2, 4, 2, 4, HALF, PAIR),
    "pass_in": on_chip(2, 2, 4, HALF, PAIR),
    "sum_in": on_chip(2, 2, 2, 4, HALF, PAIR),
    "z_out": on_chip(2, 4, 2, HALF, PAIR),
    "dq_out": on_chip(4, 2, HALF, PAIR),
    "pass_s": dma(2, 2), "pass_r": dma(2, 2), "sum_s": dma(2, 2), "sum_r": dma(2, 2),
    "zkv_s": dma(2, 4), "zkv_r": dma(2, 4), "zq_s": dma(4), "zq_r": dma(4),
    "w_term": on_chip(512, D),
    "ra": on_chip(7, 64, D), "pa": on_chip(64, D),
    "rb": on_chip(3, 16, D), "pb": on_chip(16, D),
    "rc": on_chip(8, 16, D), "pc": on_chip(16, D),
    "gd": on_chip(4, 16, D),
    "wa_s": dma(8), "wa_r": dma(8), "wb_s": dma(4), "wb_r": dma(4), "wc_s": dma(8), "wc_r": dma(8),
    "wd_s": dma(4), "wd_r": dma(4), "we_s": dma(8), "we_r": dma(8),
}
INPUTS = ("q", "k", "v", "teacher", "residual", "weight")
NAMES = INPUTS + tuple(OUTPUTS) + tuple(SCRATCH)


def on_patch(z, x):
    return {"patch": z * 4 + x}


def remote(src, dst, send_sem, recv_sem, device):
    return pltpu.make_async_remote_copy(
        src_ref=src,
        dst_ref=dst,
        send_sem=send_sem,
        recv_sem=recv_sem,
        device_id=device,
        device_id_type=MESH,
    )


def columns(index):
    return pl.ds(pl.multiple_of(index * PAIR, PAIR), PAIR)


def matmul(a, b):
    return jnp.dot(a, b, preferred_element_type=F32)


def matmul_t(a, b):
    return lax.dot_general(a, b, (((1,), (1,)), ((), ())), preferred_element_type=F32)


def kernel(*refs):
    r = SimpleNamespace(**dict(zip(NAMES, refs, strict=True)))
    index = lax.axis_index("patch")
    z, x = index // 4, index % 4
    dp = lax.axis_index("dp")
    y, z_lo, core = dp // 4, (dp // 2) % 2, dp % 2
    near, ring = y * 2 + core, z * 2 + z_lo
    right, left, across = (x + 1) % 4, (x + 3) % 4, (x + 2) % 4
    high = x // 2
    step = 3 - 2 * high
    shift_to, shift_from = (z + step) % 4, (z + 4 - step) % 4
    swap = x + 1 - 2 * (x % 2)
    inner = (x * (3 - x)) // 2

    def near_device(i):
        return {"dp": (i // 2) * 4 + z_lo * 2 + i % 2}

    def ring_device(i):
        return {"dp": y * 4 + (i % 2) * 2 + core, "patch": (i // 2) * 4 + x}

    started = []

    def send(src, dst, send_sem, recv_sem, device):
        copy = remote(src, dst, send_sem, recv_sem, device)
        copy.start()
        started.append(copy)

    def await_at(slot, send_sem, recv_sem, device):
        remote(slot, slot, send_sem, recv_sem, device).wait_recv()

    local = [
        pltpu.make_async_copy(r.teacher, r.t_raw, r.local.at[0]),
        pltpu.make_async_copy(r.k.at[:, :, columns(z)], r.kv.at[x, :, z, 0], r.local.at[1]),
        pltpu.make_async_copy(r.v.at[:, :, columns(z)], r.kv.at[x, :, z, 1], r.local.at[2]),
        pltpu.make_async_copy(r.q.at[:, :, columns(z)], r.q2.at[:, z], r.local.at[3]),
        pltpu.make_async_copy(r.residual, r.res, r.local.at[4]),
        pltpu.make_async_copy(r.weight, r.w, r.local.at[5]),
    ]
    for copy in local:
        copy.start()
    peers = (
        [ring_device((ring + d) % 8) for d in range(1, 8)]
        + [on_patch(z, (x + d) % 4) for d in range(1, 4)]
        + [near_device((near + d) % 8) for d in range(1, 8)]
    )
    barrier = pltpu.get_barrier_semaphore()
    for peer in peers:
        pl.semaphore_signal(barrier, inc=1, device_id=peer, device_id_type=MESH)
    pl.semaphore_wait(barrier, len(peers))

    for d in (1, 3, 2):
        to = (z + d) % 4
        for i, source in enumerate((r.k, r.v)):
            send(source.at[:, :, columns(to)], r.kv.at[x, :, z, i], r.qkv_s.at[i, d], r.qkv_r.at[i, d], on_patch(to, x))
    for d in (1, 3, 2):
        to = (z + d) % 4
        send(r.q.at[:, :, columns(to)], r.q2.at[:, z], r.qkv_s.at[2, d], r.qkv_r.at[2, d], on_patch(to, x))

    def spread(d):
        at = (z + 4 - d) % 4
        for side, to in enumerate((right, left)):
            slot = r.kv.at[x, :, at]
            send(slot, slot, r.spread_s.at[side, d], r.spread_r.at[side, d], on_patch(z, to))

    local[1].wait()
    local[2].wait()
    spread(0)
    local[0].wait()
    teacher = r.t_raw[...].astype(F32)
    r.t_row[x] = (
        teacher * lax.rsqrt(jnp.sum(teacher * teacher, axis=1, keepdims=True) + 1e-06)
    ).astype(BF16)
    for side, to in enumerate((right, left)):
        send(r.t_row.at[x], r.t_row.at[x], r.tx_s.at[side], r.tx_r.at[side], on_patch(z, to))
    for d in (1, 3, 2):
        at = (z + 4 - d) % 4
        for i in range(2):
            await_at(r.kv.at[x, :, at, i], r.qkv_s.at[i, d], r.qkv_r.at[i, d], on_patch(at, x))
        spread(d)
    send(r.t_row.at[x], r.t_sh, r.tz_s.at[0], r.tz_r.at[0], on_patch(shift_to, x))
    local[3].wait()
    for d in (1, 3, 2):
        at = (z + 4 - d) % 4
        await_at(r.q2.at[:, at], r.qkv_s.at[2, d], r.qkv_r.at[2, d], on_patch(at, x))

    def first_head(rows):
        return lax.broadcasted_iota(jnp.int32, (rows, PAIR), 1) < HEAD

    def of_head(h, block):
        mask = first_head(block.shape[0])
        return jnp.where(mask if h == 0 else jnp.logical_not(mask), block, 0.0)

    def forward_block(c, half, blocks):
        xc = (x + OFFSETS[c]) % 4
        keys = r.kv[xc, :, :, 0].reshape(KEYS, PAIR)
        values = r.kv[xc, :, :, 1].reshape(KEYS, PAIR)
        queries = jnp.concatenate([r.q2[half, qt] for qt in blocks], axis=0).astype(F32) * SCALE
        parts = []
        for h in range(2):
            scores = matmul_t(of_head(h, queries).astype(BF16), keys)
            top = jnp.max(scores, axis=1, keepdims=True)
            expo = jnp.exp(scores - top)
            total = jnp.sum(expo, axis=1, keepdims=True)
            rounded = expo.astype(BF16)
            for i, qt in enumerate(blocks):
                r.expo[c, h, half, qt] = rounded[i * HALF : (i + 1) * HALF]
            parts.append((top, total, matmul(rounded, values)))
        for ref, first, second in zip((r.m, r.l, r.o), *parts):
            both = jnp.where(first_head(ROWS), first, second)
            for i, qt in enumerate(blocks):
                ref[c, half, qt] = both[i * HALF : (i + 1) * HALF]

    def forward_part(c, half):
        def block(pair, carry):
            forward_block(c, half, (2 * pair, 2 * pair + 1))
            return carry

        lax.fori_loop(0, 2, block, 0)

    def join(half, qt):
        tops = [r.m[c, half, qt] for c in range(4)]
        top = jnp.maximum(jnp.maximum(tops[0], tops[1]), jnp.maximum(tops[2], tops[3]))
        scale = [jnp.exp(tops[c] - top) for c in range(4)]
        total = sum(scale[c] * r.l[c, half, qt] for c in range(4))
        joined = sum(scale[c] * r.o[c, half, qt] for c in range(4))
        inverse = 1.0 / total
        r.att2[half, qt] = (joined * inverse).astype(BF16)
        for c in range(4):
            r.m[c, half, qt] = scale[c] * inverse

    att_own = []

    def forward_last(half):
        rows = pl.ds(half * HALF, HALF)
        for pair in ((1, 2), (3, 0)):
            forward_block(3, half, tuple((z + d) % 4 for d in pair))
            for d in pair:
                to = (z + d) % 4
                join(half, to)
                source, target = r.att2.at[half, to], r.att_full.at[rows, columns(z)]
                if d:
                    send(source, target, r.att_s.at[half, d], r.att_r.at[half, d], on_patch(to, x))
                else:
                    own = pltpu.make_async_copy(source, target, r.att_own.at[half])
                    own.start()
                    att_own.append(own)

    def features(half):
        rows = pl.ds(half * HALF, HALF)
        att_own[half].wait()
        for d in (1, 3, 2):
            at = (z + 4 - d) % 4
            slot = r.att_full.at[rows, columns(at)]
            await_at(slot, r.att_s.at[half, d], r.att_r.at[half, d], on_patch(at, x))
        values = r.res[rows] + matmul(r.att_full[rows], r.w[...])
        inverse = lax.rsqrt(jnp.sum(values * values, axis=1, keepdims=True) + 1e-06)
        student = values * inverse
        r.s_row[x, rows] = student.astype(BF16)
        source = r.s_row.at[x, rows]
        send(source, r.s_sh.at[half], r.sz_s.at[half], r.sz_r.at[half], on_patch(shift_to, x))
        for side, to in enumerate((right, left)):
            send(source, source, r.sx_s.at[side, half], r.sx_r.at[side, half], on_patch(z, to))
        r.student[rows] = student
        r.inverse[rows] = jnp.broadcast_to(inverse, (HALF, PAIR))

    def pass_students(half):
        rows = pl.ds(half * HALF, HALF)
        for side, origin, to in ((1, right, left), (0, left, right)):
            slot = r.s_row.at[origin, rows]
            await_at(slot, r.sx_s.at[side, half], r.sx_r.at[side, half], on_patch(z, origin))
            if side != half:
                send(slot, slot, r.sr_s.at[half], r.sr_r.at[half], on_patch(z, to))

    def swap_students(half):
        slot = r.s_sh.at[half]
        await_at(slot, r.sz_s.at[half], r.sz_r.at[half], on_patch(shift_from, x))
        send(slot, r.s_ext.at[half], r.se_s.at[half], r.se_r.at[half], on_patch(z, swap))

    for half in range(2):
        forward_part(0, half)
    for d in (0, 1, 3, 2):
        at = (z + 4 - d) % 4
        for side, origin, to in ((1, right, left), (0, left, right)):
            await_at(r.kv.at[origin, :, at], r.spread_s.at[side, d], r.spread_r.at[side, d], on_patch(z, origin))
            slot = r.kv.at[origin, :, at, 1 - side]
            send(slot, slot, r.relay_s.at[1 - side, d], r.relay_r.at[1 - side, d], on_patch(z, to))
    forward_part(1, 0)
    for side, origin, to in ((1, right, left), (0, left, right)):
        await_at(r.t_row.at[origin], r.tx_s.at[side], r.tx_r.at[side], on_patch(z, origin))
        slot = r.t_row.at[origin, pl.ds((1 - side) * HALF, HALF)]
        send(slot, slot, r.tr_s.at[1 - side], r.tr_r.at[1 - side], on_patch(z, to))
    forward_part(2, 0)
    for d in range(4):
        at = (z + 4 - d) % 4
        for i in range(2):
            await_at(r.kv.at[across, :, at, i], r.relay_s.at[i, d], r.relay_r.at[i, d], on_patch(z, right))
    forward_last(0)
    forward_part(1, 1)
    local[4].wait()
    local[5].wait()
    features(0)
    forward_part(2, 1)
    pass_students(0)
    forward_last(1)
    await_at(r.t_sh, r.tz_s.at[0], r.tz_r.at[0], on_patch(shift_from, x))
    send(r.t_sh, r.t_ext, r.te_s.at[0], r.te_r.at[0], on_patch(z, swap))
    swap_students(0)
    features(1)

    for i in range(2):
        await_at(r.t_row.at[across, pl.ds(i * HALF, HALF)], r.tr_s.at[i], r.tr_r.at[i], on_patch(z, right))
    r.tile_sh[...] = matmul_t(r.t_sh[...], r.t_row[...].reshape(KEYS, D))
    pass_students(1)
    r.tile_own[...] = matmul_t(r.t_row[x], r.t_row[...].reshape(KEYS, D))
    for i in range(2):
        await_at(r.s_row.at[across, pl.ds(i * HALF, HALF)], r.sr_s.at[i], r.sr_r.at[i], on_patch(z, right))

    first = (1 - high) * (x + 1) * ROWS
    last = KEYS - high * (KEYS - x * ROWS)
    for p in range(2):
        if p:
            swap_students(p)
        row = r.s_row[...].reshape(KEYS, D)
        tile = matmul_t(r.s_sh[p], row) - r.tile_sh[pl.ds(p * HALF, HALF)]
        at = lax.broadcasted_iota(jnp.int32, tile.shape, 1)
        tile = jnp.where(jnp.logical_and(at >= first, at < last), tile, 0.0)
        r.back_out[p] = matmul(tile.astype(BF16), row).astype(BF16)
        send(r.back_out.at[p], r.back_in.at[p], r.back_s.at[p], r.back_r.at[p], on_patch(shift_from, x))
    row = r.s_row[...].reshape(KEYS, D)
    own_tile = matmul_t(r.s_row[x], row) - r.tile_own[...]
    r.gradient[...] = matmul(own_tile.astype(BF16), row)
    await_at(r.t_ext, r.te_s.at[0], r.te_r.at[0], on_patch(z, swap))
    for p in range(2):
        await_at(r.s_ext.at[p], r.se_s.at[p], r.se_r.at[p], on_patch(z, swap))
    other = r.s_ext[...].reshape(ROWS, D)
    tile = matmul_t(r.s_row[x], other) - matmul_t(r.t_row[x], r.t_ext[...])
    tile = jnp.where(lax.broadcasted_iota(jnp.int32, tile.shape, 1) < inner * ROWS, tile, 0.0)
    r.gradient[...] += matmul(tile.astype(BF16), other)

    datt_own = []
    for p in range(2):
        rows = pl.ds(p * HALF, HALF)
        await_at(r.back_in.at[p], r.back_s.at[p], r.back_r.at[p], on_patch(shift_to, x))
        gram_grad = 32.0 * (r.gradient[rows] + r.back_in[p].astype(F32))
        student = r.student[rows]
        dot = jnp.sum(student * gram_grad, axis=1, keepdims=True)
        grad = r.inverse[rows, :1] * (gram_grad - student * dot)
        r.d_features[rows] = grad
        rounded = grad.astype(BF16)
        r.grad[rows] = rounded
        r.datt[rows] = matmul_t(rounded, r.w[...]).astype(BF16)
        for d in (1, 3, 2):
            to = (z + d) % 4
            source = r.datt.at[rows, columns(to)]
            send(source, r.datt2.at[p, z], r.datt_s.at[p, d], r.datt_r.at[p, d], on_patch(to, x))
        own = pltpu.make_async_copy(r.datt.at[rows, columns(z)], r.datt2.at[p, z], r.datt_own.at[p])
        own.start()
        datt_own.append(own)
    transposed = r.att_full[...].astype(F32).T.astype(BF16)
    r.w_term[...] = matmul(transposed, r.grad[...]).astype(BF16)

    def weight_a():
        for d in range(1, 8):
            to = (near + d) % 8
            rows = pl.ds(pl.multiple_of(to * 64, 64), 64)
            send(r.w_term.at[rows], r.ra.at[d - 1], r.wa_s.at[d], r.wa_r.at[d], near_device(to))

    def weight_b():
        total = r.w_term[pl.ds(pl.multiple_of(near * 64, 64), 64)].astype(F32)
        for d in range(1, 8):
            await_at(r.ra.at[d - 1], r.wa_s.at[d], r.wa_r.at[d], near_device((near + d) % 8))
            total = total + r.ra[d - 1].astype(F32)
        r.pa[...] = total.astype(BF16)
        for d in range(1, 4):
            to = (x + d) % 4
            rows = pl.ds(pl.multiple_of(to * 16, 16), 16)
            send(r.pa.at[rows], r.rb.at[d - 1], r.wb_s.at[d], r.wb_r.at[d], on_patch(z, to))

    def weight_c():
        total = r.pa[pl.ds(pl.multiple_of(x * 16, 16), 16)].astype(F32)
        for d in range(1, 4):
            await_at(r.rb.at[d - 1], r.wb_s.at[d], r.wb_r.at[d], on_patch(z, (x + d) % 4))
            total = total + r.rb[d - 1].astype(F32)
        r.pb[...] = total.astype(BF16)
        r.rc[ring] = r.pb[...]
        for d in range(1, 8):
            send(r.pb, r.rc.at[ring], r.wc_s.at[d], r.wc_r.at[d], ring_device((ring + d) % 8))

    def weight_d():
        for d in range(1, 8):
            at = (ring + 8 - d) % 8
            await_at(r.rc.at[at], r.wc_s.at[d], r.wc_r.at[d], ring_device(at))
        total = r.rc[0].astype(F32)
        for i in range(1, 8):
            total = total + r.rc[i].astype(F32)
        r.pc[...] = total.astype(BF16)
        r.gd[x] = r.pc[...]
        for d in range(1, 4):
            send(r.pc, r.gd.at[x], r.wd_s.at[d], r.wd_r.at[d], on_patch(z, (x + d) % 4))

    def weight_e():
        for d in range(1, 4):
            at = (x + 4 - d) % 4
            await_at(r.gd.at[at], r.wd_s.at[d], r.wd_r.at[d], on_patch(z, at))
        r.ge[near] = r.gd[...]
        for d in range(1, 8):
            send(r.gd, r.ge.at[near], r.we_s.at[d], r.we_r.at[d], near_device((near + d) % 8))

    def weight_out():
        for d in range(1, 8):
            at = (near + 8 - d) % 8
            await_at(r.ge.at[at], r.we_s.at[d], r.we_r.at[d], near_device(at))

    weight_a()
    for half in range(2):
        r.q_t[half] = (r.q2[half].reshape(QUERIES, PAIR).astype(F32) * SCALE).T.astype(BF16)
        r.dq[half] = jnp.zeros((QUERIES, PAIR), F32)

    def await_grads(p):
        datt_own[p].wait()
        for d in (1, 3, 2):
            at = (z + 4 - d) % 4
            await_at(r.datt2.at[p, at], r.datt_s.at[p, d], r.datt_r.at[p, d], on_patch(at, x))

    def prepare(c, half):
        factor = r.m[c, half].reshape(QUERIES, PAIR)
        grads = r.datt2[half].reshape(QUERIES, PAIR).astype(F32)
        scaled = grads * factor
        r.do_t[c, half] = scaled.T.astype(BF16)
        dots = scaled * r.att2[half].reshape(QUERIES, PAIR).astype(F32)
        sums = []
        for h in range(2):
            r.do_m[c, half, h] = of_head(h, scaled).astype(BF16)
            sums.append(jnp.sum(of_head(h, dots), axis=1, keepdims=True))
        r.dots[c, half] = jnp.where(first_head(QUERIES), sums[0], sums[1])

    def backward_part(c, keys_half):
        xc = (x + OFFSETS[c]) % 4
        places = pl.ds(keys_half * QUERIES, QUERIES)

        def block(half, carry):
            if keys_half == 0:
                prepare(c, half)
            keys = r.kv[xc, keys_half, :, 0].reshape(QUERIES, PAIR)
            values = r.kv[xc, keys_half, :, 1].reshape(QUERIES, PAIR)
            found = []
            for h in range(2):
                rows = pl.ds(h * HEAD, HEAD)
                expo = r.expo[c, h, half, :, :, places].reshape(QUERIES, QUERIES)
                prob_grad = matmul_t(r.do_m[c, half, h], values)
                row_dot = r.dots[c, half, :, h * HEAD : h * HEAD + 1]
                score_grad = (expo.astype(F32) * (prob_grad - row_dot)).astype(BF16)
                found.append(matmul(score_grad, keys))
                r.dk[rows] += matmul(r.q_t[half, rows], score_grad)
                r.dv[rows] += matmul(r.do_t[c, half, rows], expo)
            r.dq[half] += jnp.where(first_head(QUERIES), found[0], found[1])
            return carry

        r.dk[...] = jnp.zeros((PAIR, QUERIES), F32)
        r.dv[...] = jnp.zeros((PAIR, QUERIES), F32)
        if c == 3 and keys_half == 0:
            await_grads(0)
            block(0, 0)
            await_grads(1)
            block(1, 0)
        else:
            lax.fori_loop(0, 2, block, 0)
        return r.dk[...].T.reshape(4, HALF, PAIR), r.dv[...].T.reshape(4, HALF, PAIR)

    def weight_step(number):
        for at, work in ((1, weight_b), (3, weight_c), (4, weight_d), (6, weight_e)):
            if number == at:
                work()

    def backward_keys(i):
        part = r.part.at[i]
        dk, dv = backward_part(3, i)
        part[3, 0], part[3, 1] = dk.astype(BF16), dv.astype(BF16)
        for kind, to in ((0, right), (1, left)):
            send(part.at[3, kind], r.pass_in.at[i, kind], r.pass_s.at[i, kind], r.pass_r.at[i, kind], on_patch(z, to))
        if i:
            return_keys(0)
        for c, kind, origin, to in ((1, 0, left, right), (2, 1, right, left)):
            weight_step(4 * i + c - 1)
            found = list(backward_part(c, i))
            await_at(r.pass_in.at[i, kind], r.pass_s.at[i, kind], r.pass_r.at[i, kind], on_patch(z, origin))
            found[kind] = found[kind] + r.pass_in[i, kind].astype(F32)
            part[c, 0], part[c, 1] = found[0].astype(BF16), found[1].astype(BF16)
            send(part.at[c], r.sum_in.at[i, c - 1], r.sum_s.at[i, c - 1], r.sum_r.at[i, c - 1], on_patch(z, to))
        weight_step(4 * i + 2)
        dk, dv = backward_part(0, i)
        part[0, 0], part[0, 1] = dk.astype(BF16), dv.astype(BF16)
        weight_step(4 * i + 3)

    def return_keys(i):
        await_at(r.sum_in.at[i, 0], r.sum_s.at[i, 0], r.sum_r.at[i, 0], on_patch(z, left))
        await_at(r.sum_in.at[i, 1], r.sum_s.at[i, 1], r.sum_r.at[i, 1], on_patch(z, right))
        for d in (1, 3, 2, 0):
            to = (z + d) % 4
            for kind in range(2):
                total = r.part[i, 0, kind, to].astype(F32)
                total = total + r.sum_in[i, 0, kind, to].astype(F32) + r.sum_in[i, 1, kind, to].astype(F32)
                if d:
                    r.z_out[i, d, kind] = total.astype(BF16)
                else:
                    r.z_in[z, kind, i] = total.astype(BF16)
            if d:
                target = r.z_in.at[z, pl.ds(0, 2), i]
                send(r.z_out.at[i, d], target, r.zkv_s.at[i, d], r.zkv_r.at[i, d], on_patch(to, x))

    backward_keys(0)
    backward_keys(1)
    for half in range(2):
        blocks = (r.dq[half] * SCALE).astype(BF16).reshape(4, HALF, PAIR)
        for to in range(4):
            r.dq_out[to, half] = blocks[to]
    for d in (1, 3, 2):
        to = (z + d) % 4
        send(r.dq_out.at[to], r.z_in.at[z, 2], r.zq_s.at[d], r.zq_r.at[d], on_patch(to, x))
    r.z_in[z, 2] = r.dq_out[z]
    return_keys(1)
    weight_out()
    for d in (1, 3, 2):
        at = (z + 4 - d) % 4
        await_at(r.z_in.at[at, 2], r.zq_s.at[d], r.zq_r.at[d], on_patch(at, x))
        for i in range(2):
            await_at(r.z_in.at[at, pl.ds(0, 2), i], r.zkv_s.at[i, d], r.zkv_r.at[i, d], on_patch(at, x))
    for copy in started:
        copy.wait_send()


def finish(z_in, weight, features, d_queries, d_keys, d_values, d_weight, d_features):
    d_keys[...] = z_in[0, 0].reshape(ROWS, PAIR).astype(F32)
    d_values[...] = z_in[0, 1].reshape(ROWS, PAIR).astype(F32)
    d_queries[...] = z_in[0, 2].reshape(ROWS, PAIR).astype(F32)
    d_weight[...] = weight[...].astype(F32)
    d_features[...] = features[...]


def on_device(patch_queries, patch_keys, patch_values, residual, teacher, output_weight):
    vmem = pl.BlockSpec(memory_space=pltpu.VMEM)
    hbm = pl.BlockSpec(memory_space=pl.ANY)
    z_in, weight, features = pl.pallas_call(
        kernel,
        out_shape=[jax.ShapeDtypeStruct(shape, dtype) for shape, dtype in OUTPUTS.values()],
        in_specs=[hbm] * 6,
        out_specs=[vmem] * 3,
        scratch_shapes=list(SCRATCH.values()),
        compiler_params=pltpu.CompilerParams(
            collective_id=0, has_side_effects=True, vmem_limit_bytes=VMEM_LIMIT
        ),
        cost_estimate=pl.CostEstimate(
            flops=18_000_000_000, bytes_accessed=10_000_000, transcendentals=9_000_000
        ),
    )(
        *(array.reshape(2, HALF, 512) for array in (patch_queries, patch_keys, patch_values)),
        teacher[0],
        residual[0],
        output_weight,
    )
    head_columns = pl.BlockSpec((ROWS, PAIR), lambda i: (0, i))
    d_queries, d_keys, d_values, d_weight, d_features = pl.pallas_call(
        finish,
        grid=(4,),
        out_shape=[jax.ShapeDtypeStruct((ROWS, 512), F32)] * 3
        + [jax.ShapeDtypeStruct((512, D), F32), jax.ShapeDtypeStruct((ROWS, D), F32)],
        in_specs=[
            pl.BlockSpec((1, 3, 2, HALF, PAIR), lambda i: (i, 0, 0, 0, 0)),
            pl.BlockSpec((PAIR, D), lambda i: (i, 0)),
            pl.BlockSpec((64, D), lambda i: (i, 0)),
        ],
        out_specs=[head_columns] * 3
        + [pl.BlockSpec((PAIR, D), lambda i: (i, 0)), pl.BlockSpec((64, D), lambda i: (i, 0))],
        compiler_params=pltpu.CompilerParams(vmem_limit_bytes=VMEM_LIMIT),
    )(z_in, weight.reshape(512, D), features)
    return d_queries[None], d_keys[None], d_values[None], d_features[None], d_weight


def solution(mesh):
    placed = P("dp", "patch", None)
    return jax.shard_map(
        on_device,
        mesh=mesh,
        in_specs=(placed,) * 5 + (P(),),
        out_specs=(placed,) * 4 + (P(),),
        check_vma=False,
    )
```

```python
from types import SimpleNamespace

import jax
import jax.numpy as jnp
from jax import lax
from jax.experimental import pallas as pl
from jax.experimental.pallas import tpu as pltpu
from jax.sharding import PartitionSpec as P

MESH = pl.DeviceIdType.MESH
F32 = jnp.float32
BF16 = jnp.bfloat16
ROWS = 256
HALF = 128
PAIR = 128
HEAD = 64
D = 1024
KEYS = 1024
PIECES = 2
PIECE = ROWS // PIECES
SCALE = HEAD ** -0.5
OFFSETS = (0, 1, 3, 2)
VMEM_LIMIT = 60 * 1024 * 1024


def dma(*shape):
    return pltpu.SemaphoreType.DMA(shape)


def on_chip(*shape, dtype=BF16):
    return pltpu.VMEM(shape, dtype)


OUTPUTS = {
    "z_in": ((4, 3, ROWS, PAIR), BF16),
    "ge": ((2, 4, 4, 16, D), BF16),
    "d_features": ((ROWS, D), F32),
}
SCRATCH = {
    "t_raw": on_chip(ROWS, D),
    "res": on_chip(ROWS, D, dtype=F32),
    "w": on_chip(512, D),
    "q2": on_chip(4, ROWS, PAIR),
    "kv": on_chip(4, 4, 2, ROWS, PAIR),
    "expo": on_chip(4, 2, 4, ROWS, KEYS),
    "m": on_chip(4, 4, ROWS, PAIR, dtype=F32),
    "l": on_chip(4, 4, ROWS, PAIR, dtype=F32),
    "o": on_chip(4, 4, ROWS, PAIR, dtype=F32),
    "att2": on_chip(4, ROWS, PAIR),
    "att_full": on_chip(ROWS, 512),
    "local": dma(6),
    "qkv_s": dma(3, 4), "qkv_r": dma(3, 4),
    "spread_s": dma(2, 4), "spread_r": dma(2, 4),
    "relay_s": dma(2, 4), "relay_r": dma(2, 4),
    "att_s": dma(4), "att_r": dma(4), "att_own": dma(1),
    "far_kv": on_chip(2, ROWS, PAIR),
    "far_q": on_chip(2, HALF, PAIR),
    "far_att": on_chip(2, HALF, PAIR),
    "far_datt": on_chip(2, HALF, PAIR),
    "far_dkv": on_chip(2, ROWS, PAIR),
    "far_dq": on_chip(2, HALF, PAIR),
    "first_s": dma(6, 2), "first_r": dma(6, 2), "second_s": dma(6, 2), "second_r": dma(6, 2),
    "t_row": on_chip(4, ROWS, D),
    "t_sh": on_chip(ROWS, D),
    "t_ext": on_chip(ROWS, D),
    "tile_own": on_chip(ROWS, KEYS, dtype=F32),
    "tile_sh": on_chip(ROWS, KEYS, dtype=F32),
    "s_row": on_chip(4, ROWS, D),
    "s_sh": on_chip(PIECES, PIECE, D),
    "s_ext": on_chip(PIECES, PIECE, D),
    "back_out": on_chip(PIECES, PIECE, D),
    "back_in": on_chip(PIECES, PIECE, D),
    "student": on_chip(ROWS, D, dtype=F32),
    "inverse": on_chip(ROWS, PAIR, dtype=F32),
    "gradient": on_chip(ROWS, D, dtype=F32),
    "grad": on_chip(ROWS, D),
    "datt": on_chip(ROWS, 512),
    "datt2": on_chip(4, ROWS, PAIR),
    "tx_s": dma(2), "tx_r": dma(2), "tr_s": dma(2), "tr_r": dma(2),
    "tz_s": dma(1), "tz_r": dma(1), "te_s": dma(1), "te_r": dma(1),
    "sx_s": dma(2), "sx_r": dma(2), "sr_s": dma(2), "sr_r": dma(2),
    "sz_s": dma(PIECES), "sz_r": dma(PIECES), "se_s": dma(PIECES), "se_r": dma(PIECES),
    "back_s": dma(PIECES), "back_r": dma(PIECES),
    "datt_s": dma(PIECES, 4), "datt_r": dma(PIECES, 4), "datt_own": dma(PIECES),
    "q_t": on_chip(4, PAIR, ROWS),
    "do_t": on_chip(PAIR, ROWS),
    "dq": on_chip(4, ROWS, PAIR, dtype=F32),
    "dk": on_chip(PAIR, KEYS, dtype=F32),
    "dv": on_chip(PAIR, KEYS, dtype=F32),
    "part": on_chip(4, 2, 4, ROWS, PAIR),
    "pass_in": on_chip(2, 4, ROWS, PAIR),
    "sum_in": on_chip(2, 2, 4, ROWS, PAIR),
    "z_out": on_chip(4, 2, ROWS, PAIR),
    "dq_out": on_chip(4, ROWS, PAIR),
    "pass_s": dma(2), "pass_r": dma(2), "sum_s": dma(2), "sum_r": dma(2),
    "zkv_s": dma(4), "zkv_r": dma(4), "zq_s": dma(4), "zq_r": dma(4),
    "w_term": on_chip(512, D),
    "rs": on_chip(256, D), "ps": on_chip(256, D),
    "ra": on_chip(3, 64, D), "pa": on_chip(64, D),
    "rb": on_chip(3, 16, D), "pb": on_chip(16, D),
    "rc": on_chip(8, 16, D), "pc": on_chip(16, D),
    "gd": on_chip(4, 16, D),
    "ws_s": dma(1), "ws_r": dma(1), "wa_s": dma(4), "wa_r": dma(4), "wb_s": dma(4), "wb_r": dma(4), "wc_s": dma(8), "wc_r": dma(8),
    "wd_s": dma(4), "wd_r": dma(4), "we_s": dma(4), "we_r": dma(4), "wf_s": dma(1), "wf_r": dma(1),
}
INPUTS = ("q", "k", "v", "teacher", "residual", "weight")
NAMES = INPUTS + tuple(OUTPUTS) + tuple(SCRATCH)


def on_patch(z, x):
    return {"patch": z * 4 + x}


def remote(src, dst, send_sem, recv_sem, device):
    return pltpu.make_async_remote_copy(
        src_ref=src,
        dst_ref=dst,
        send_sem=send_sem,
        recv_sem=recv_sem,
        device_id=device,
        device_id_type=MESH,
    )


def columns(index):
    return pl.ds(pl.multiple_of(index * PAIR, PAIR), PAIR)


def matmul(a, b):
    return jnp.dot(a, b, preferred_element_type=F32)


def matmul_t(a, b):
    return lax.dot_general(a, b, (((1,), (1,)), ((), ())), preferred_element_type=F32)


def kernel(*refs):
    r = SimpleNamespace(**dict(zip(NAMES, refs, strict=True)))
    index = lax.axis_index("patch")
    z, x = index // 4, index % 4
    dp = lax.axis_index("dp")
    y, z_lo, core = dp // 4, (dp // 2) % 2, dp % 2
    ring = z * 2 + z_lo
    right, left, across = (x + 1) % 4, (x + 3) % 4, (x + 2) % 4
    up, down, opposite = (z + 1) % 4, (z + 3) % 4, (z + 2) % 4
    high = x // 2
    step = 3 - 2 * high
    shift_to, shift_from = (z + step) % 4, (z + 4 - step) % 4
    swap = x + 1 - 2 * (x % 2)
    inner = (x * (3 - x)) // 2

    sibling = {"dp": y * 4 + z_lo * 2 + 1 - core}

    def on_y(i):
        return {"dp": i * 4 + z_lo * 2 + core}

    def ring_device(i):
        return {"dp": y * 4 + (i % 2) * 2 + core, "patch": (i // 2) * 4 + x}

    started = []

    def send(src, dst, send_sem, recv_sem, device):
        copy = remote(src, dst, send_sem, recv_sem, device)
        copy.start()
        started.append(copy)

    def await_at(slot, send_sem, recv_sem, device):
        remote(slot, slot, send_sem, recv_sem, device).wait_recv()

    def first_leg(n, relay, by_up, by_down):
        send(by_up, relay.at[0], r.first_s.at[n, 0], r.first_r.at[n, 0], on_patch(up, x))
        send(by_down, relay.at[1], r.first_s.at[n, 1], r.first_r.at[n, 1], on_patch(down, x))

    def second_leg(n, relay, to_up, to_down):
        for i, origin, to, target in ((0, down, up, to_up), (1, up, down, to_down)):
            await_at(relay.at[i], r.first_s.at[n, i], r.first_r.at[n, i], on_patch(origin, x))
            send(relay.at[i], target, r.second_s.at[n, i], r.second_r.at[n, i], on_patch(to, x))

    def await_far(n, by_up, by_down):
        await_at(by_up, r.second_s.at[n, 0], r.second_r.at[n, 0], on_patch(down, x))
        await_at(by_down, r.second_s.at[n, 1], r.second_r.at[n, 1], on_patch(up, x))

    top, low = pl.ds(0, HALF), pl.ds(HALF, HALF)

    local = [
        pltpu.make_async_copy(r.teacher, r.t_raw, r.local.at[0]),
        pltpu.make_async_copy(r.k.at[:, columns(z)], r.kv.at[x, z, 0], r.local.at[1]),
        pltpu.make_async_copy(r.v.at[:, columns(z)], r.kv.at[x, z, 1], r.local.at[2]),
        pltpu.make_async_copy(r.q.at[:, columns(z)], r.q2.at[z], r.local.at[3]),
        pltpu.make_async_copy(r.residual, r.res, r.local.at[4]),
        pltpu.make_async_copy(r.weight, r.w, r.local.at[5]),
    ]
    for copy in local:
        copy.start()
    peers = (
        [ring_device((ring + d) % 8) for d in range(1, 8)]
        + [on_patch(z, (x + d) % 4) for d in range(1, 4)]
        + [on_y((y + d) % 4) for d in range(1, 4)]
        + [sibling]
    )
    barrier = pltpu.get_barrier_semaphore()
    for peer in peers:
        pl.semaphore_signal(barrier, inc=1, device_id=peer, device_id_type=MESH)
    pl.semaphore_wait(barrier, len(peers))

    first_leg(0, r.far_kv, r.k.at[:, columns(opposite)], r.v.at[:, columns(opposite)])
    for d in (1, 3):
        to = (z + d) % 4
        for i, source in enumerate((r.k, r.v)):
            send(source.at[:, columns(to)], r.kv.at[x, z, i], r.qkv_s.at[i, d], r.qkv_r.at[i, d], on_patch(to, x))
    first_leg(1, r.far_q, r.q.at[top, columns(opposite)], r.q.at[low, columns(opposite)])
    for d in (1, 3):
        to = (z + d) % 4
        send(r.q.at[:, columns(to)], r.q2.at[z], r.qkv_s.at[2, d], r.qkv_r.at[2, d], on_patch(to, x))

    def spread(d):
        at = (z + 4 - d) % 4
        for side, to in enumerate((right, left)):
            slot = r.kv.at[x, at]
            send(slot, slot, r.spread_s.at[side, d], r.spread_r.at[side, d], on_patch(z, to))

    local[1].wait()
    local[2].wait()
    spread(0)
    local[0].wait()
    teacher = r.t_raw[...].astype(F32)
    r.t_row[x] = (
        teacher * lax.rsqrt(jnp.sum(teacher * teacher, axis=1, keepdims=True) + 1e-06)
    ).astype(BF16)
    for side, to in enumerate((right, left)):
        send(r.t_row.at[x], r.t_row.at[x], r.tx_s.at[side], r.tx_r.at[side], on_patch(z, to))
    second_leg(0, r.far_kv, r.kv.at[x, down, 0], r.kv.at[x, up, 1])
    for d in (1, 3):
        at = (z + 4 - d) % 4
        for i in range(2):
            await_at(r.kv.at[x, at, i], r.qkv_s.at[i, d], r.qkv_r.at[i, d], on_patch(at, x))
        spread(d)
    second_leg(1, r.far_q, r.q2.at[down, top], r.q2.at[up, low])
    await_far(0, r.kv.at[x, opposite, 0], r.kv.at[x, opposite, 1])
    spread(2)
    send(r.t_row.at[x], r.t_sh, r.tz_s.at[0], r.tz_r.at[0], on_patch(shift_to, x))
    local[3].wait()

    first_head = lax.broadcasted_iota(jnp.int32, (ROWS, PAIR), 1) < HEAD

    def forward_block(c, qt):
        xc = (x + OFFSETS[c]) % 4
        keys = r.kv[xc, :, 0].reshape(KEYS, PAIR)
        values = r.kv[xc, :, 1].reshape(KEYS, PAIR)
        queries = r.q2[qt].astype(F32) * SCALE
        parts = []
        for h in range(2):
            mask = first_head if h == 0 else jnp.logical_not(first_head)
            masked = jnp.where(mask, queries, 0.0).astype(BF16)
            scores = matmul_t(masked, keys)
            top = jnp.max(scores, axis=1, keepdims=True)
            expo = jnp.exp(scores - top)
            total = jnp.sum(expo, axis=1, keepdims=True)
            rounded = expo.astype(BF16)
            r.expo[c, h, qt] = rounded
            parts.append((top, total, matmul(rounded, values)))
        (m0, l0, o0), (m1, l1, o1) = parts
        r.m[c, qt] = jnp.where(first_head, m0, m1)
        r.l[c, qt] = jnp.where(first_head, l0, l1)
        r.o[c, qt] = jnp.where(first_head, o0, o1)

    def forward_chunk(c):
        def block(qt, carry):
            forward_block(c, qt)
            return carry

        lax.fori_loop(0, 4, block, 0)

    def join(qt):
        tops = [r.m[c, qt] for c in range(4)]
        top = jnp.maximum(jnp.maximum(tops[0], tops[1]), jnp.maximum(tops[2], tops[3]))
        scale = [jnp.exp(tops[c] - top) for c in range(4)]
        total = sum(scale[c] * r.l[c, qt] for c in range(4))
        joined = sum(scale[c] * r.o[c, qt] for c in range(4))
        inverse = 1.0 / total
        r.att2[qt] = (joined * inverse).astype(BF16)
        for c in range(4):
            r.m[c, qt] = scale[c] * inverse

    def first_block(i, carry):
        d = i + (i // 2) * (1 - 2 * (i % 2))
        for near in (1, 3):

            @pl.when(d == near)
            def _():
                at = (z + 4 - near) % 4
                await_at(r.q2.at[at], r.qkv_s.at[2, near], r.qkv_r.at[2, near], on_patch(at, x))

        @pl.when(d == 2)
        def _():
            await_far(1, r.q2.at[opposite, top], r.q2.at[opposite, low])

        forward_block(0, (z + 4 - d) % 4)
        return carry

    lax.fori_loop(0, 4, first_block, 0)
    for d in (0, 1, 3, 2):
        at = (z + 4 - d) % 4
        await_at(r.kv.at[right, at], r.spread_s.at[1, d], r.spread_r.at[1, d], on_patch(z, right))
        slot = r.kv.at[right, at, 0]
        send(slot, slot, r.relay_s.at[0, d], r.relay_r.at[0, d], on_patch(z, left))
        await_at(r.kv.at[left, at], r.spread_s.at[0, d], r.spread_r.at[0, d], on_patch(z, left))
        slot = r.kv.at[left, at, 1]
        send(slot, slot, r.relay_s.at[1, d], r.relay_r.at[1, d], on_patch(z, right))
    forward_chunk(1)

    def pass_on(row, x_s, x_r, on_s, on_r):
        await_at(row.at[right], x_s.at[1], x_r.at[1], on_patch(z, right))
        slot = row.at[right, pl.ds(0, HALF)]
        send(slot, slot, on_s.at[0], on_r.at[0], on_patch(z, left))
        await_at(row.at[left], x_s.at[0], x_r.at[0], on_patch(z, left))
        slot = row.at[left, pl.ds(HALF, HALF)]
        send(slot, slot, on_s.at[1], on_r.at[1], on_patch(z, right))

    def await_across(row, on_s, on_r):
        for i in range(2):
            await_at(row.at[across, pl.ds(i * HALF, HALF)], on_s.at[i], on_r.at[i], on_patch(z, right))

    pass_on(r.t_row, r.tx_s, r.tx_r, r.tr_s, r.tr_r)
    forward_chunk(2)
    for d in range(4):
        at = (z + 4 - d) % 4
        for i in range(2):
            await_at(r.kv.at[across, at, i], r.relay_s.at[i, d], r.relay_r.at[i, d], on_patch(z, right))
    for d in (2, 1, 3, 0):
        to = (z + d) % 4
        forward_block(3, to)
        join(to)
        if d == 2:
            first_leg(2, r.far_att, r.att2.at[to, top], r.att2.at[to, low])
        elif d:
            send(r.att2.at[to], r.att_full.at[:, columns(z)], r.att_s.at[d], r.att_r.at[d], on_patch(to, x))
    own = pltpu.make_async_copy(r.att2.at[z], r.att_full.at[:, columns(z)], r.att_own.at[0])
    own.start()
    second_leg(2, r.far_att, r.att_full.at[top, columns(down)], r.att_full.at[low, columns(up)])

    await_at(r.t_sh, r.tz_s.at[0], r.tz_r.at[0], on_patch(shift_from, x))
    send(r.t_sh, r.t_ext, r.te_s.at[0], r.te_r.at[0], on_patch(z, swap))
    own.wait()
    local[4].wait()
    local[5].wait()
    await_far(2, r.att_full.at[top, columns(opposite)], r.att_full.at[low, columns(opposite)])
    for d in (1, 3):
        at = (z + 4 - d) % 4
        await_at(r.att_full.at[:, columns(at)], r.att_s.at[d], r.att_r.at[d], on_patch(at, x))

    features = r.res[...] + matmul(r.att_full[...], r.w[...])
    inverse = lax.rsqrt(jnp.sum(features * features, axis=1, keepdims=True) + 1e-06)
    student = features * inverse
    r.s_row[x] = student.astype(BF16)
    for p in range(PIECES):
        source = r.s_row.at[x, pl.ds(p * PIECE, PIECE)]
        send(source, r.s_sh.at[p], r.sz_s.at[p], r.sz_r.at[p], on_patch(shift_to, x))
    for side, to in enumerate((right, left)):
        send(r.s_row.at[x], r.s_row.at[x], r.sx_s.at[side], r.sx_r.at[side], on_patch(z, to))
    r.student[...] = student
    r.inverse[...] = jnp.broadcast_to(inverse, (ROWS, PAIR))

    await_across(r.t_row, r.tr_s, r.tr_r)
    r.tile_sh[...] = matmul_t(r.t_sh[...], r.t_row[...].reshape(KEYS, D))
    pass_on(r.s_row, r.sx_s, r.sx_r, r.sr_s, r.sr_r)
    r.tile_own[...] = matmul_t(r.t_row[x], r.t_row[...].reshape(KEYS, D))
    await_across(r.s_row, r.sr_s, r.sr_r)

    first = (1 - high) * (x + 1) * ROWS
    last = KEYS - high * (KEYS - x * ROWS)
    for p in range(PIECES):
        await_at(r.s_sh.at[p], r.sz_s.at[p], r.sz_r.at[p], on_patch(shift_from, x))
        send(r.s_sh.at[p], r.s_ext.at[p], r.se_s.at[p], r.se_r.at[p], on_patch(z, swap))
        row = r.s_row[...].reshape(KEYS, D)
        tile = matmul_t(r.s_sh[p], row) - r.tile_sh[pl.ds(p * PIECE, PIECE)]
        at = lax.broadcasted_iota(jnp.int32, tile.shape, 1)
        tile = jnp.where(jnp.logical_and(at >= first, at < last), tile, 0.0)
        r.back_out[p] = matmul(tile.astype(BF16), row).astype(BF16)
        send(r.back_out.at[p], r.back_in.at[p], r.back_s.at[p], r.back_r.at[p], on_patch(shift_from, x))
    row = r.s_row[...].reshape(KEYS, D)
    own_tile = matmul_t(r.s_row[x], row) - r.tile_own[...]
    r.gradient[...] = matmul(own_tile.astype(BF16), row)
    await_at(r.t_ext, r.te_s.at[0], r.te_r.at[0], on_patch(z, swap))
    for p in range(PIECES):
        await_at(r.s_ext.at[p], r.se_s.at[p], r.se_r.at[p], on_patch(z, swap))
    other = r.s_ext[...].reshape(ROWS, D)
    tile = matmul_t(r.s_row[x], other) - matmul_t(r.t_row[x], r.t_ext[...])
    tile = jnp.where(lax.broadcasted_iota(jnp.int32, tile.shape, 1) < inner * ROWS, tile, 0.0)
    r.gradient[...] += matmul(tile.astype(BF16), other)

    datt_own = []
    for p in range(PIECES):
        rows = pl.ds(p * PIECE, PIECE)
        await_at(r.back_in.at[p], r.back_s.at[p], r.back_r.at[p], on_patch(shift_to, x))
        gram_grad = 32.0 * (r.gradient[rows] + r.back_in[p].astype(F32))
        student = r.student[rows]
        dot = jnp.sum(student * gram_grad, axis=1, keepdims=True)
        grad = r.inverse[rows, :1] * (gram_grad - student * dot)
        r.d_features[rows] = grad
        rounded = grad.astype(BF16)
        r.grad[rows] = rounded
        r.datt[rows] = matmul_t(rounded, r.w[...]).astype(BF16)
        side = (up, down)[p]
        source = r.datt.at[rows, columns(opposite)]
        send(source, r.far_datt.at[p], r.first_s.at[3, p], r.first_r.at[3, p], on_patch(side, x))
        for d in (1, 3):
            to = (z + d) % 4
            source = r.datt.at[rows, columns(to)]
            send(source, r.datt2.at[z, rows], r.datt_s.at[p, d], r.datt_r.at[p, d], on_patch(to, x))
        own = pltpu.make_async_copy(r.datt.at[rows, columns(z)], r.datt2.at[z, rows], r.datt_own.at[p])
        own.start()
        datt_own.append(own)
    second_leg(3, r.far_datt, r.datt2.at[down, top], r.datt2.at[up, low])
    transposed = r.att_full[...].astype(F32).T.astype(BF16)
    r.w_term[...] = matmul(transposed, r.grad[...]).astype(BF16)

    def weight_sibling():
        rows = pl.ds(pl.multiple_of((1 - core) * 256, 256), 256)
        send(r.w_term.at[rows], r.rs, r.ws_s.at[0], r.ws_r.at[0], sibling)

    def weight_a():
        await_at(r.rs, r.ws_s.at[0], r.ws_r.at[0], sibling)
        own_rows = pl.ds(pl.multiple_of(core * 256, 256), 256)
        r.ps[...] = (r.w_term[own_rows].astype(F32) + r.rs[...].astype(F32)).astype(BF16)
        for d in (2, 1, 3):
            to = (y + d) % 4
            rows = pl.ds(pl.multiple_of(to * 64, 64), 64)
            send(r.ps.at[rows], r.ra.at[d - 1], r.wa_s.at[d], r.wa_r.at[d], on_y(to))

    def weight_b():
        total = r.ps[pl.ds(pl.multiple_of(y * 64, 64), 64)].astype(F32)
        for d in range(1, 4):
            await_at(r.ra.at[d - 1], r.wa_s.at[d], r.wa_r.at[d], on_y((y + d) % 4))
            total = total + r.ra[d - 1].astype(F32)
        r.pa[...] = total.astype(BF16)
        for d in range(1, 4):
            to = (x + d) % 4
            rows = pl.ds(pl.multiple_of(to * 16, 16), 16)
            send(r.pa.at[rows], r.rb.at[d - 1], r.wb_s.at[d], r.wb_r.at[d], on_patch(z, to))

    def weight_c():
        total = r.pa[pl.ds(pl.multiple_of(x * 16, 16), 16)].astype(F32)
        for d in range(1, 4):
            await_at(r.rb.at[d - 1], r.wb_s.at[d], r.wb_r.at[d], on_patch(z, (x + d) % 4))
            total = total + r.rb[d - 1].astype(F32)
        r.pb[...] = total.astype(BF16)
        r.rc[ring] = r.pb[...]
        for d in range(1, 8):
            send(r.pb, r.rc.at[ring], r.wc_s.at[d], r.wc_r.at[d], ring_device((ring + d) % 8))

    def weight_d():
        for d in range(1, 8):
            at = (ring + 8 - d) % 8
            await_at(r.rc.at[at], r.wc_s.at[d], r.wc_r.at[d], ring_device(at))
        total = r.rc[0].astype(F32)
        for i in range(1, 8):
            total = total + r.rc[i].astype(F32)
        r.pc[...] = total.astype(BF16)
        r.gd[x] = r.pc[...]
        for d in range(1, 4):
            send(r.pc, r.gd.at[x], r.wd_s.at[d], r.wd_r.at[d], on_patch(z, (x + d) % 4))

    def weight_e():
        for d in range(1, 4):
            at = (x + 4 - d) % 4
            await_at(r.gd.at[at], r.wd_s.at[d], r.wd_r.at[d], on_patch(z, at))
        r.ge[core, y] = r.gd[...]
        for d in range(1, 4):
            send(r.gd, r.ge.at[core, y], r.we_s.at[d], r.we_r.at[d], on_y((y + d) % 4))

    def weight_f():
        for d in range(1, 4):
            at = (y + 4 - d) % 4
            await_at(r.ge.at[core, at], r.we_s.at[d], r.we_r.at[d], on_y(at))
        send(r.ge.at[core], r.ge.at[core], r.wf_s.at[0], r.wf_r.at[0], sibling)

    def weight_out():
        await_at(r.ge.at[1 - core], r.wf_s.at[0], r.wf_r.at[0], sibling)

    weight_sibling()
    for qt in range(4):
        r.q_t[qt] = (r.q2[qt].astype(F32) * SCALE).T.astype(BF16)
        r.dq[qt] = jnp.zeros((ROWS, PAIR), F32)
    weight_a()
    for p in range(2):
        datt_own[p].wait()
        for d in (1, 3):
            at = (z + 4 - d) % 4
            slot = r.datt2.at[at, pl.ds(p * PIECE, PIECE)]
            await_at(slot, r.datt_s.at[p, d], r.datt_r.at[p, d], on_patch(at, x))
    await_far(3, r.datt2.at[opposite, top], r.datt2.at[opposite, low])

    def backward_chunk(c):
        xc = (x + OFFSETS[c]) % 4
        r.dk[...] = jnp.zeros((PAIR, KEYS), F32)
        r.dv[...] = jnp.zeros((PAIR, KEYS), F32)

        def block(qt, carry):
            keys = r.kv[xc, :, 0].reshape(KEYS, PAIR)
            values = r.kv[xc, :, 1].reshape(KEYS, PAIR)
            factor = r.m[c, qt]
            grads = r.datt2[qt].astype(F32)
            scaled = grads * factor
            r.do_t[...] = scaled.T.astype(BF16)
            dots = grads * r.att2[qt].astype(F32)
            found = []
            for h in range(2):
                mask = first_head if h == 0 else jnp.logical_not(first_head)
                rows = pl.ds(h * HEAD, HEAD)
                masked = jnp.where(mask, scaled, 0.0).astype(BF16)
                row_dot = jnp.sum(jnp.where(mask, dots, 0.0), axis=1, keepdims=True)
                row_dot = row_dot * factor[:, h * HEAD : h * HEAD + 1]
                expo = r.expo[c, h, qt]
                prob_grad = matmul_t(masked, values)
                score_grad = (expo.astype(F32) * (prob_grad - row_dot)).astype(BF16)
                found.append(matmul(score_grad, keys))
                r.dk[rows] += matmul(r.q_t[qt, rows], score_grad)
                r.dv[rows] += matmul(r.do_t[rows], expo)
            r.dq[qt] += jnp.where(first_head, found[0], found[1])
            return carry

        lax.fori_loop(0, 4, block, 0)
        return r.dk[...].T.reshape(4, ROWS, PAIR), r.dv[...].T.reshape(4, ROWS, PAIR)

    dk, dv = backward_chunk(3)
    r.part[3, 0], r.part[3, 1] = dk.astype(BF16), dv.astype(BF16)
    send(r.part.at[3, 0], r.pass_in.at[0], r.pass_s.at[0], r.pass_r.at[0], on_patch(z, right))
    send(r.part.at[3, 1], r.pass_in.at[1], r.pass_s.at[1], r.pass_r.at[1], on_patch(z, left))
    weight_b()
    dk, dv = backward_chunk(1)
    await_at(r.pass_in.at[0], r.pass_s.at[0], r.pass_r.at[0], on_patch(z, left))
    r.part[1, 0], r.part[1, 1] = (dk + r.pass_in[0].astype(F32)).astype(BF16), dv.astype(BF16)
    send(r.part.at[1], r.sum_in.at[0], r.sum_s.at[0], r.sum_r.at[0], on_patch(z, right))
    weight_c()
    dk, dv = backward_chunk(2)
    await_at(r.pass_in.at[1], r.pass_s.at[1], r.pass_r.at[1], on_patch(z, right))
    r.part[2, 0], r.part[2, 1] = dk.astype(BF16), (dv + r.pass_in[1].astype(F32)).astype(BF16)
    send(r.part.at[2], r.sum_in.at[1], r.sum_s.at[1], r.sum_r.at[1], on_patch(z, left))
    weight_d()
    dk, dv = backward_chunk(0)
    r.part[0, 0], r.part[0, 1] = dk.astype(BF16), dv.astype(BF16)
    for to in range(4):
        r.dq_out[to] = (r.dq[to] * SCALE).astype(BF16)
    first_leg(5, r.far_dq, r.dq_out.at[opposite, top], r.dq_out.at[opposite, low])
    for d in (1, 3):
        to = (z + d) % 4
        send(r.dq_out.at[to], r.z_in.at[z, 2], r.zq_s.at[d], r.zq_r.at[d], on_patch(to, x))
    r.z_in[z, 2] = r.dq_out[z]
    weight_e()
    await_at(r.sum_in.at[0], r.sum_s.at[0], r.sum_r.at[0], on_patch(z, left))
    await_at(r.sum_in.at[1], r.sum_s.at[1], r.sum_r.at[1], on_patch(z, right))
    for d in (2, 1, 3, 0):
        to = (z + d) % 4
        for i in range(2):
            total = r.part[0, i, to].astype(F32)
            total = total + r.sum_in[0, i, to].astype(F32) + r.sum_in[1, i, to].astype(F32)
            if d:
                r.z_out[d, i] = total.astype(BF16)
            else:
                r.z_in[z, i] = total.astype(BF16)
        if d == 2:
            first_leg(4, r.far_dkv, r.z_out.at[d, 0], r.z_out.at[d, 1])
        elif d:
            send(r.z_out.at[d], r.z_in.at[z, pl.ds(0, 2)], r.zkv_s.at[d], r.zkv_r.at[d], on_patch(to, x))
    second_leg(5, r.far_dq, r.z_in.at[down, 2, top], r.z_in.at[up, 2, low])
    second_leg(4, r.far_dkv, r.z_in.at[down, 0], r.z_in.at[up, 1])
    weight_f()
    for d in (1, 3):
        at = (z + 4 - d) % 4
        await_at(r.z_in.at[at, 2], r.zq_s.at[d], r.zq_r.at[d], on_patch(at, x))
        await_at(r.z_in.at[at, pl.ds(0, 2)], r.zkv_s.at[d], r.zkv_r.at[d], on_patch(at, x))
    await_far(5, r.z_in.at[opposite, 2, top], r.z_in.at[opposite, 2, low])
    await_far(4, r.z_in.at[opposite, 0], r.z_in.at[opposite, 1])
    weight_out()
    for copy in started:
        copy.wait_send()


def finish(z_in, weight, features, d_queries, d_keys, d_values, d_weight, d_features):
    d_keys[...] = z_in[0, 0].astype(F32)
    d_values[...] = z_in[0, 1].astype(F32)
    d_queries[...] = z_in[0, 2].astype(F32)
    d_weight[...] = weight[...].astype(F32)
    d_features[...] = features[...]


def on_device(patch_queries, patch_keys, patch_values, residual, teacher, output_weight):
    vmem = pl.BlockSpec(memory_space=pltpu.VMEM)
    hbm = pl.BlockSpec(memory_space=pl.ANY)
    z_in, weight, features = pl.pallas_call(
        kernel,
        out_shape=[jax.ShapeDtypeStruct(shape, dtype) for shape, dtype in OUTPUTS.values()],
        in_specs=[hbm] * 6,
        out_specs=[vmem] * 3,
        scratch_shapes=list(SCRATCH.values()),
        compiler_params=pltpu.CompilerParams(
            collective_id=0, has_side_effects=True, vmem_limit_bytes=VMEM_LIMIT
        ),
        cost_estimate=pl.CostEstimate(
            flops=18_000_000_000, bytes_accessed=10_000_000, transcendentals=9_000_000
        ),
    )(patch_queries[0], patch_keys[0], patch_values[0], teacher[0], residual[0], output_weight)
    head_columns = pl.BlockSpec((ROWS, PAIR), lambda i: (0, i))
    d_queries, d_keys, d_values, d_weight, d_features = pl.pallas_call(
        finish,
        grid=(4,),
        out_shape=[jax.ShapeDtypeStruct((ROWS, 512), F32)] * 3
        + [jax.ShapeDtypeStruct((512, D), F32), jax.ShapeDtypeStruct((ROWS, D), F32)],
        in_specs=[
            pl.BlockSpec((1, 3, ROWS, PAIR), lambda i: (i, 0, 0, 0)),
            pl.BlockSpec((PAIR, D), lambda i: (i, 0)),
            pl.BlockSpec((64, D), lambda i: (i, 0)),
        ],
        out_specs=[head_columns] * 3
        + [pl.BlockSpec((PAIR, D), lambda i: (i, 0)), pl.BlockSpec((64, D), lambda i: (i, 0))],
        compiler_params=pltpu.CompilerParams(vmem_limit_bytes=VMEM_LIMIT),
    )(z_in, weight.reshape(512, D), features)
    return d_queries[None], d_keys[None], d_values[None], d_features[None], d_weight


def solution(mesh):
    placed = P("dp", "patch", None)
    return jax.shard_map(
        on_device,
        mesh=mesh,
        in_specs=(placed,) * 5 + (P(),),
        out_specs=(placed,) * 4 + (P(),),
        check_vma=False,
    )
```

```python
from types import SimpleNamespace

import jax
import jax.numpy as jnp
from jax import lax
from jax.experimental import pallas as pl
from jax.experimental.pallas import tpu as pltpu
from jax.sharding import PartitionSpec as P

MESH = pl.DeviceIdType.MESH
F32 = jnp.float32
BF16 = jnp.bfloat16
ROWS = 256
HALF = 128
PAIR = 128
HEAD = 64
D = 1024
KEYS = 1024
PIECES = 2
PIECE = ROWS // PIECES
SCALE = HEAD ** -0.5
VMEM_LIMIT = 60 * 1024 * 1024


def dma(*shape):
    return pltpu.SemaphoreType.DMA(shape)


def on_chip(*shape, dtype=BF16):
    return pltpu.VMEM(shape, dtype)


OUTPUTS = {
    "z_in": ((4, 3, ROWS, PAIR), BF16),
    "ge": ((2, 4, 4, 16, D), BF16),
    "d_features": ((ROWS, D), F32),
}
SCRATCH = {
    "t_raw": on_chip(ROWS, D),
    "res": on_chip(ROWS, D, dtype=F32),
    "w": on_chip(512, D),
    "q2": on_chip(4, ROWS, PAIR),
    "kv": on_chip(4, 4, 2, ROWS, PAIR),
    "expo": on_chip(4, 2, 4, ROWS, KEYS),
    "m": on_chip(4, 4, ROWS, PAIR, dtype=F32),
    "l": on_chip(4, 4, ROWS, PAIR, dtype=F32),
    "o": on_chip(4, 4, ROWS, PAIR, dtype=F32),
    "att2": on_chip(4, ROWS, PAIR),
    "att_full": on_chip(ROWS, 512),
    "local": dma(6),
    "qkv_s": dma(3, 4), "qkv_r": dma(3, 4),
    "spread_s": dma(2, 4), "spread_r": dma(2, 4),
    "relay_s": dma(2, 4), "relay_r": dma(2, 4),
    "att_s": dma(4), "att_r": dma(4), "att_own": dma(1),
    "far_kv": on_chip(2, ROWS, PAIR),
    "far_q": on_chip(2, HALF, PAIR),
    "far_att": on_chip(2, HALF, PAIR),
    "far_datt": on_chip(2, HALF, PAIR),
    "far_dkv": on_chip(2, ROWS, PAIR),
    "far_dq": on_chip(2, HALF, PAIR),
    "first_s": dma(6, 2), "first_r": dma(6, 2), "second_s": dma(6, 2), "second_r": dma(6, 2),
    "t_row": on_chip(4, ROWS, D),
    "t_lhs": on_chip(2, ROWS, D),
    "t_ext": on_chip(ROWS, D),
    "tiles": on_chip(4, PIECE, KEYS, dtype=F32),
    "s_row": on_chip(4, ROWS, D),
    "s_lhs": on_chip(4, PIECE, D),
    "terms": on_chip(4, PIECE, D, dtype=F32),
    "s_ext": on_chip(PIECES, PIECE, D),
    "back_out": on_chip(PIECES, PIECE, D),
    "back_in": on_chip(PIECES, PIECE, D),
    "student": on_chip(ROWS, D, dtype=F32),
    "inverse": on_chip(ROWS, PAIR, dtype=F32),
    "grad": on_chip(ROWS, D),
    "datt": on_chip(ROWS, 512),
    "datt2": on_chip(4, ROWS, PAIR),
    "tx_s": dma(2), "tx_r": dma(2), "tr_s": dma(2), "tr_r": dma(2),
    "tz_s": dma(1), "tz_r": dma(1), "te_s": dma(1), "te_r": dma(1),
    "sx_s": dma(2), "sx_r": dma(2), "sr_s": dma(2), "sr_r": dma(2),
    "sz_s": dma(PIECES), "sz_r": dma(PIECES), "se_s": dma(PIECES), "se_r": dma(PIECES),
    "back_s": dma(PIECES), "back_r": dma(PIECES),
    "datt_s": dma(PIECES, 4), "datt_r": dma(PIECES, 4), "datt_own": dma(PIECES),
    "q_t": on_chip(4, PAIR, ROWS),
    "do_t": on_chip(PAIR, ROWS),
    "dq": on_chip(4, ROWS, PAIR, dtype=F32),
    "dots": on_chip(4, ROWS, PAIR, dtype=F32),
    "dk": on_chip(PAIR, KEYS, dtype=F32),
    "dv": on_chip(PAIR, KEYS, dtype=F32),
    "part": on_chip(4, 2, 4, ROWS, PAIR),
    "pass_in": on_chip(2, 4, ROWS, PAIR),
    "sum_in": on_chip(2, 2, 4, ROWS, PAIR),
    "z_out": on_chip(4, 2, ROWS, PAIR),
    "dq_out": on_chip(4, ROWS, PAIR),
    "pass_s": dma(2), "pass_r": dma(2), "sum_s": dma(2), "sum_r": dma(2),
    "zkv_s": dma(4), "zkv_r": dma(4), "zq_s": dma(4), "zq_r": dma(4),
    "w_term": on_chip(512, D),
    "rs": on_chip(256, D), "ps": on_chip(256, D),
    "ra": on_chip(3, 64, D), "pa": on_chip(64, D),
    "rb": on_chip(3, 16, D), "pb": on_chip(16, D),
    "rc": on_chip(8, 16, D), "pc": on_chip(16, D),
    "gd": on_chip(4, 16, D),
    "ws_s": dma(1), "ws_r": dma(1), "wa_s": dma(4), "wa_r": dma(4), "wb_s": dma(4), "wb_r": dma(4), "wc_s": dma(8), "wc_r": dma(8),
    "wd_s": dma(4), "wd_r": dma(4), "we_s": dma(4), "we_r": dma(4), "wf_s": dma(1), "wf_r": dma(1),
}
INPUTS = ("q", "k", "v", "teacher", "residual", "weight")
NAMES = INPUTS + tuple(OUTPUTS) + tuple(SCRATCH)


def on_patch(z, x):
    return {"patch": z * 4 + x}


def remote(src, dst, send_sem, recv_sem, device):
    return pltpu.make_async_remote_copy(
        src_ref=src,
        dst_ref=dst,
        send_sem=send_sem,
        recv_sem=recv_sem,
        device_id=device,
        device_id_type=MESH,
    )


def columns(index):
    return pl.ds(pl.multiple_of(index * PAIR, PAIR), PAIR)


def around(i):
    return i + (i // 2) * (1 - 2 * (i % 2))


def matmul(a, b):
    return jnp.dot(a, b, preferred_element_type=F32)


def matmul_t(a, b):
    return lax.dot_general(a, b, (((1,), (1,)), ((), ())), preferred_element_type=F32)


def kernel(*refs):
    r = SimpleNamespace(**dict(zip(NAMES, refs, strict=True)))
    index = lax.axis_index("patch")
    z, x = index // 4, index % 4
    dp = lax.axis_index("dp")
    y, z_lo, core = dp // 4, (dp // 2) % 2, dp % 2
    ring = z * 2 + z_lo
    right, left, across = (x + 1) % 4, (x + 3) % 4, (x + 2) % 4
    up, down, opposite = (z + 1) % 4, (z + 3) % 4, (z + 2) % 4
    high = x // 2
    step = 3 - 2 * high
    shift_to, shift_from = (z + step) % 4, (z + 4 - step) % 4
    swap = x + 1 - 2 * (x % 2)
    inner = (x * (3 - x)) // 2

    sibling = {"dp": y * 4 + z_lo * 2 + 1 - core}

    def on_y(i):
        return {"dp": i * 4 + z_lo * 2 + core}

    def ring_device(i):
        return {"dp": y * 4 + (i % 2) * 2 + core, "patch": (i // 2) * 4 + x}

    started = []

    def send(src, dst, send_sem, recv_sem, device):
        copy = remote(src, dst, send_sem, recv_sem, device)
        copy.start()
        started.append(copy)

    later = []

    def begin(*copy):
        remote(*copy).start()

    def group(copies):
        later.append(copies)
        return copies

    def await_at(slot, send_sem, recv_sem, device):
        remote(slot, slot, send_sem, recv_sem, device).wait_recv()

    def first_leg(n, relay, by_up, by_down):
        send(by_up, relay.at[0], r.first_s.at[n, 0], r.first_r.at[n, 0], on_patch(up, x))
        send(by_down, relay.at[1], r.first_s.at[n, 1], r.first_r.at[n, 1], on_patch(down, x))

    def second_leg(n, relay, to_up, to_down):
        for i, origin, to, target in ((0, down, up, to_up), (1, up, down, to_down)):
            await_at(relay.at[i], r.first_s.at[n, i], r.first_r.at[n, i], on_patch(origin, x))
            send(relay.at[i], target, r.second_s.at[n, i], r.second_r.at[n, i], on_patch(to, x))

    def await_far(n, by_up, by_down):
        await_at(by_up, r.second_s.at[n, 0], r.second_r.at[n, 0], on_patch(down, x))
        await_at(by_down, r.second_s.at[n, 1], r.second_r.at[n, 1], on_patch(up, x))

    top, low = pl.ds(0, HALF), pl.ds(HALF, HALF)

    local = [
        pltpu.make_async_copy(r.teacher, r.t_raw, r.local.at[0]),
        pltpu.make_async_copy(r.k.at[:, columns(z)], r.kv.at[x, z, 0], r.local.at[1]),
        pltpu.make_async_copy(r.v.at[:, columns(z)], r.kv.at[x, z, 1], r.local.at[2]),
        pltpu.make_async_copy(r.q.at[:, columns(z)], r.q2.at[z], r.local.at[3]),
        pltpu.make_async_copy(r.residual, r.res, r.local.at[4]),
        pltpu.make_async_copy(r.weight, r.w, r.local.at[5]),
    ]
    for copy in local:
        copy.start()
    peers = (
        [ring_device((ring + d) % 8) for d in range(1, 8)]
        + [on_patch(z, (x + d) % 4) for d in range(1, 4)]
        + [on_y((y + d) % 4) for d in range(1, 4)]
        + [sibling]
    )
    barrier = pltpu.get_barrier_semaphore()
    for peer in peers:
        pl.semaphore_signal(barrier, inc=1, device_id=peer, device_id_type=MESH)
    pl.semaphore_wait(barrier, len(peers))

    first_leg(0, r.far_kv, r.k.at[:, columns(opposite)], r.v.at[:, columns(opposite)])
    for d in (1, 3):
        to = (z + d) % 4
        for i, source in enumerate((r.k, r.v)):
            send(source.at[:, columns(to)], r.kv.at[x, z, i], r.qkv_s.at[i, d], r.qkv_r.at[i, d], on_patch(to, x))
    first_leg(1, r.far_q, r.q.at[top, columns(opposite)], r.q.at[low, columns(opposite)])
    for d in (1, 3):
        to = (z + d) % 4
        send(r.q.at[:, columns(to)], r.q2.at[z], r.qkv_s.at[2, d], r.qkv_r.at[2, d], on_patch(to, x))

    def spread(d):
        at = (z + 4 - d) % 4
        for side, to in enumerate((right, left)):
            slot = r.kv.at[x, at]
            send(slot, slot, r.spread_s.at[side, d], r.spread_r.at[side, d], on_patch(z, to))

    local[1].wait()
    local[2].wait()
    spread(0)
    local[0].wait()
    teacher = r.t_raw[...].astype(F32)
    teacher = teacher * lax.rsqrt(jnp.sum(teacher * teacher, axis=1, keepdims=True) + 1e-06)
    r.t_row[x] = teacher.astype(BF16)
    r.t_lhs[1] = teacher.astype(BF16)
    for side, to in enumerate((right, left)):
        send(r.t_row.at[x], r.t_row.at[x], r.tx_s.at[side], r.tx_r.at[side], on_patch(z, to))
    second_leg(0, r.far_kv, r.kv.at[x, down, 0], r.kv.at[x, up, 1])
    for d in (1, 3):
        at = (z + 4 - d) % 4
        for i in range(2):
            await_at(r.kv.at[x, at, i], r.qkv_s.at[i, d], r.qkv_r.at[i, d], on_patch(at, x))
        spread(d)
    second_leg(1, r.far_q, r.q2.at[down, top], r.q2.at[up, low])
    await_far(0, r.kv.at[x, opposite, 0], r.kv.at[x, opposite, 1])
    spread(2)
    send(r.t_row.at[x], r.t_lhs.at[0], r.tz_s.at[0], r.tz_r.at[0], on_patch(shift_to, x))
    local[3].wait()

    first_head = lax.broadcasted_iota(jnp.int32, (ROWS, PAIR), 1) < HEAD

    def forward_block(c, qt):
        xc = (x + around(c)) % 4
        keys = r.kv[xc, :, 0].reshape(KEYS, PAIR)
        values = r.kv[xc, :, 1].reshape(KEYS, PAIR)
        queries = r.q2[qt].astype(F32) * SCALE
        parts = []
        for h in range(2):
            mask = first_head if h == 0 else jnp.logical_not(first_head)
            masked = jnp.where(mask, queries, 0.0).astype(BF16)
            scores = matmul_t(masked, keys)
            top = jnp.max(scores, axis=1, keepdims=True)
            expo = jnp.exp(scores - top)
            total = jnp.sum(expo, axis=1, keepdims=True)
            rounded = expo.astype(BF16)
            r.expo[c, h, qt] = rounded
            parts.append((top, total, matmul(rounded, values)))
        (m0, l0, o0), (m1, l1, o1) = parts
        r.m[c, qt] = jnp.where(first_head, m0, m1)
        r.l[c, qt] = jnp.where(first_head, l0, l1)
        r.o[c, qt] = jnp.where(first_head, o0, o1)

    def join(qt):
        tops = [r.m[c, qt] for c in range(4)]
        top = jnp.maximum(jnp.maximum(tops[0], tops[1]), jnp.maximum(tops[2], tops[3]))
        scale = [jnp.exp(tops[c] - top) for c in range(4)]
        total = sum(scale[c] * r.l[c, qt] for c in range(4))
        joined = sum(scale[c] * r.o[c, qt] for c in range(4))
        inverse = 1.0 / total
        r.att2[qt] = (joined * inverse).astype(BF16)
        for c in range(4):
            r.m[c, qt] = scale[c] * inverse

    def await_queries(d):
        at = (z + 4 - d) % 4
        if d == 2:
            await_far(1, r.q2.at[at, top], r.q2.at[at, low])
        elif d:
            await_at(r.q2.at[at], r.qkv_s.at[2, d], r.qkv_r.at[2, d], on_patch(at, x))

    @group
    def relay_keys(act):
        for d in (0, 1, 3, 2):
            at = (z + 4 - d) % 4
            if act is begin:
                await_at(r.kv.at[right, at], r.spread_s.at[1, d], r.spread_r.at[1, d], on_patch(z, right))
            slot = r.kv.at[right, at, 0]
            act(slot, slot, r.relay_s.at[0, d], r.relay_r.at[0, d], on_patch(z, left))
            if act is begin:
                await_at(r.kv.at[left, at], r.spread_s.at[0, d], r.spread_r.at[0, d], on_patch(z, left))
            slot = r.kv.at[left, at, 1]
            act(slot, slot, r.relay_s.at[1, d], r.relay_r.at[1, d], on_patch(z, right))

    def pass_on(act, row, x_s, x_r, on_s, on_r):
        if act is begin:
            await_at(row.at[right], x_s.at[1], x_r.at[1], on_patch(z, right))
        slot = row.at[right, top]
        act(slot, slot, on_s.at[0], on_r.at[0], on_patch(z, left))
        if act is begin:
            await_at(row.at[left], x_s.at[0], x_r.at[0], on_patch(z, left))
        slot = row.at[left, low]
        act(slot, slot, on_s.at[1], on_r.at[1], on_patch(z, right))

    def await_across(row, on_s, on_r):
        for i in range(2):
            await_at(row.at[across, pl.ds(i * HALF, HALF)], on_s.at[i], on_r.at[i], on_patch(z, right))

    @group
    def pass_teachers(act):
        pass_on(act, r.t_row, r.tx_s, r.tx_r, r.tr_s, r.tr_r)

    def await_keys():
        for d in range(4):
            at = (z + 4 - d) % 4
            for i in range(2):
                await_at(r.kv.at[across, at, i], r.relay_s.at[i, d], r.relay_r.at[i, d], on_patch(z, right))

    @group
    def send_attended(act, places=(1, 3, 2)):
        for d in places:
            to = (z + d) % 4
            if d == 2:
                for i, rows, side in ((0, top, up), (1, low, down)):
                    target = r.far_att.at[i]
                    act(r.att2.at[to, rows], target, r.first_s.at[2, i], r.first_r.at[2, i], on_patch(side, x))
            else:
                act(r.att2.at[to], r.att_full.at[:, columns(z)], r.att_s.at[d], r.att_r.at[d], on_patch(to, x))

    def forward_step(step, carry):
        c, i = step // 4, step % 4
        start = (3 - c) // 3
        qt = (z + start * (4 - around(i)) + (1 - start) * around(3 - i)) % 4
        for at, work in (
            (1, lambda: await_queries(1)),
            (2, lambda: await_queries(3)),
            (3, lambda: await_queries(2)),
            (4, lambda: relay_keys(begin)),
            (8, lambda: pass_teachers(begin)),
            (12, await_keys),
        ):
            pl.when(step == at)(work)
        forward_block(c, qt)

        @pl.when(c == 3)
        def _():
            join(qt)

        for i, d in enumerate((2, 3, 1)):
            pl.when(step == 12 + i)(lambda d=d: send_attended(begin, (d,)))
        return carry

    lax.fori_loop(0, 16, forward_step, 0)
    own = pltpu.make_async_copy(r.att2.at[z], r.att_full.at[:, columns(z)], r.att_own.at[0])
    own.start()
    second_leg(2, r.far_att, r.att_full.at[top, columns(down)], r.att_full.at[low, columns(up)])

    await_at(r.t_lhs.at[0], r.tz_s.at[0], r.tz_r.at[0], on_patch(shift_from, x))
    send(r.t_lhs.at[0], r.t_ext, r.te_s.at[0], r.te_r.at[0], on_patch(z, swap))
    own.wait()
    local[4].wait()
    local[5].wait()
    await_far(2, r.att_full.at[top, columns(opposite)], r.att_full.at[low, columns(opposite)])
    for d in (1, 3):
        at = (z + 4 - d) % 4
        await_at(r.att_full.at[:, columns(at)], r.att_s.at[d], r.att_r.at[d], on_patch(at, x))

    features = r.res[...] + matmul(r.att_full[...], r.w[...])
    inverse = lax.rsqrt(jnp.sum(features * features, axis=1, keepdims=True) + 1e-06)
    student = features * inverse
    rounded = student.astype(BF16)
    r.s_row[x] = rounded
    for p in range(PIECES):
        r.s_lhs[PIECES + p] = rounded[p * PIECE : (p + 1) * PIECE]
        source = r.s_row.at[x, pl.ds(p * PIECE, PIECE)]
        send(source, r.s_lhs.at[p], r.sz_s.at[p], r.sz_r.at[p], on_patch(shift_to, x))
    for side, to in enumerate((right, left)):
        send(r.s_row.at[x], r.s_row.at[x], r.sx_s.at[side], r.sx_r.at[side], on_patch(z, to))
    r.student[...] = student
    r.inverse[...] = jnp.broadcast_to(inverse, (ROWS, PAIR))

    @group
    def pass_students(act):
        pass_on(act, r.s_row, r.sx_s, r.sx_r, r.sr_s, r.sr_r)

    await_across(r.t_row, r.tr_s, r.tr_r)

    def teacher_tile(i, carry):
        pl.when(i == 1)(lambda: pass_students(begin))
        tile = matmul_t(r.t_lhs[i], r.t_row[...].reshape(KEYS, D))
        r.tiles[pl.ds(2 * i, 2)] = tile.reshape(2, PIECE, KEYS)
        return carry

    lax.fori_loop(0, 2, teacher_tile, 0)
    await_across(r.s_row, r.sr_s, r.sr_r)

    first = (1 - high) * (x + 1) * ROWS
    last = KEYS - high * (KEYS - x * ROWS)

    @group
    def swap_students(act, pieces=range(PIECES)):
        for p in pieces:
            slot = r.s_lhs.at[p]
            if act is begin:
                await_at(slot, r.sz_s.at[p], r.sz_r.at[p], on_patch(shift_from, x))
            act(slot, r.s_ext.at[p], r.se_s.at[p], r.se_r.at[p], on_patch(z, swap))

    @group
    def send_back(act, pieces=range(PIECES)):
        for p in pieces:
            if act is begin:
                r.back_out[p] = r.terms[p].astype(BF16)
            act(r.back_out.at[p], r.back_in.at[p], r.back_s.at[p], r.back_r.at[p], on_patch(shift_from, x))

    def term(i, carry):
        for p in range(PIECES):
            pl.when(i == p)(lambda p=p: swap_students(begin, (p,)))
        row = r.s_row[...].reshape(KEYS, D)
        tile = matmul_t(r.s_lhs[i], row) - r.tiles[i]
        at = lax.broadcasted_iota(jnp.int32, tile.shape, 1)
        whole = i // 2
        keep = jnp.logical_and(at >= first * (1 - whole), at < last + whole * (KEYS - last))
        r.terms[i] = matmul(jnp.where(keep, tile, 0.0).astype(BF16), row)
        for p in range(PIECES):
            pl.when(i == p)(lambda p=p: send_back(begin, (p,)))
        return carry

    lax.fori_loop(0, 4, term, 0)
    await_at(r.t_ext, r.te_s.at[0], r.te_r.at[0], on_patch(z, swap))
    for p in range(PIECES):
        await_at(r.s_ext.at[p], r.se_s.at[p], r.se_r.at[p], on_patch(z, swap))
    other = r.s_ext[...].reshape(ROWS, D)
    tile = matmul_t(r.s_row[x], other) - matmul_t(r.t_row[x], r.t_ext[...])
    tile = jnp.where(lax.broadcasted_iota(jnp.int32, tile.shape, 1) < inner * ROWS, tile, 0.0)
    added = matmul(tile.astype(BF16), other)
    for p in range(PIECES):
        r.terms[PIECES + p] += added[p * PIECE : (p + 1) * PIECE]

    datt_own = []
    for p in range(PIECES):
        rows = pl.ds(p * PIECE, PIECE)
        await_at(r.back_in.at[p], r.back_s.at[p], r.back_r.at[p], on_patch(shift_to, x))
        gram_grad = 32.0 * (r.terms[PIECES + p] + r.back_in[p].astype(F32))
        student = r.student[rows]
        dot = jnp.sum(student * gram_grad, axis=1, keepdims=True)
        grad = r.inverse[rows, :1] * (gram_grad - student * dot)
        r.d_features[rows] = grad
        rounded = grad.astype(BF16)
        r.grad[rows] = rounded
        r.datt[rows] = matmul_t(rounded, r.w[...]).astype(BF16)
        side = (up, down)[p]
        source = r.datt.at[rows, columns(opposite)]
        send(source, r.far_datt.at[p], r.first_s.at[3, p], r.first_r.at[3, p], on_patch(side, x))
        for d in (1, 3):
            to = (z + d) % 4
            source = r.datt.at[rows, columns(to)]
            send(source, r.datt2.at[z, rows], r.datt_s.at[p, d], r.datt_r.at[p, d], on_patch(to, x))
        own = pltpu.make_async_copy(r.datt.at[rows, columns(z)], r.datt2.at[z, rows], r.datt_own.at[p])
        own.start()
        datt_own.append(own)
    second_leg(3, r.far_datt, r.datt2.at[down, top], r.datt2.at[up, low])
    transposed = r.att_full[...].astype(F32).T.astype(BF16)
    r.w_term[...] = matmul(transposed, r.grad[...]).astype(BF16)

    def weight_sibling():
        rows = pl.ds(pl.multiple_of((1 - core) * 256, 256), 256)
        send(r.w_term.at[rows], r.rs, r.ws_s.at[0], r.ws_r.at[0], sibling)

    def weight_a():
        await_at(r.rs, r.ws_s.at[0], r.ws_r.at[0], sibling)
        own_rows = pl.ds(pl.multiple_of(core * 256, 256), 256)
        r.ps[...] = (r.w_term[own_rows].astype(F32) + r.rs[...].astype(F32)).astype(BF16)
        for d in (2, 1, 3):
            to = (y + d) % 4
            rows = pl.ds(pl.multiple_of(to * 64, 64), 64)
            send(r.ps.at[rows], r.ra.at[d - 1], r.wa_s.at[d], r.wa_r.at[d], on_y(to))

    @group
    def send_b(act):
        for d in range(1, 4):
            to = (x + d) % 4
            rows = pl.ds(pl.multiple_of(to * 16, 16), 16)
            act(r.pa.at[rows], r.rb.at[d - 1], r.wb_s.at[d], r.wb_r.at[d], on_patch(z, to))

    def weight_b():
        total = r.ps[pl.ds(pl.multiple_of(y * 64, 64), 64)].astype(F32)
        for d in range(1, 4):
            await_at(r.ra.at[d - 1], r.wa_s.at[d], r.wa_r.at[d], on_y((y + d) % 4))
            total = total + r.ra[d - 1].astype(F32)
        r.pa[...] = total.astype(BF16)
        send_b(begin)

    @group
    def send_c(act):
        for d in range(1, 8):
            act(r.pb, r.rc.at[ring], r.wc_s.at[d], r.wc_r.at[d], ring_device((ring + d) % 8))

    def weight_c():
        total = r.pa[pl.ds(pl.multiple_of(x * 16, 16), 16)].astype(F32)
        for d in range(1, 4):
            await_at(r.rb.at[d - 1], r.wb_s.at[d], r.wb_r.at[d], on_patch(z, (x + d) % 4))
            total = total + r.rb[d - 1].astype(F32)
        r.pb[...] = total.astype(BF16)
        r.rc[ring] = r.pb[...]
        send_c(begin)

    @group
    def send_d(act):
        for d in range(1, 4):
            act(r.pc, r.gd.at[x], r.wd_s.at[d], r.wd_r.at[d], on_patch(z, (x + d) % 4))

    def weight_d():
        for d in range(1, 8):
            at = (ring + 8 - d) % 8
            await_at(r.rc.at[at], r.wc_s.at[d], r.wc_r.at[d], ring_device(at))
        total = r.rc[0].astype(F32)
        for i in range(1, 8):
            total = total + r.rc[i].astype(F32)
        r.pc[...] = total.astype(BF16)
        r.gd[x] = r.pc[...]
        send_d(begin)

    def weight_e():
        for d in range(1, 4):
            at = (x + 4 - d) % 4
            await_at(r.gd.at[at], r.wd_s.at[d], r.wd_r.at[d], on_patch(z, at))
        r.ge[core, y] = r.gd[...]
        for d in range(1, 4):
            send(r.gd, r.ge.at[core, y], r.we_s.at[d], r.we_r.at[d], on_y((y + d) % 4))

    def weight_f():
        for d in range(1, 4):
            at = (y + 4 - d) % 4
            await_at(r.ge.at[core, at], r.we_s.at[d], r.we_r.at[d], on_y(at))
        send(r.ge.at[core], r.ge.at[core], r.wf_s.at[0], r.wf_r.at[0], sibling)

    def weight_out():
        await_at(r.ge.at[1 - core], r.wf_s.at[0], r.wf_r.at[0], sibling)

    weight_sibling()
    for qt in range(4):
        r.q_t[qt] = (r.q2[qt].astype(F32) * SCALE).T.astype(BF16)
        r.dq[qt] = jnp.zeros((ROWS, PAIR), F32)
    weight_a()

    def await_grads(d):
        at = (z + 4 - d) % 4
        if d == 2:
            await_far(3, r.datt2.at[at, top], r.datt2.at[at, low])
            return
        for p in range(2):
            if d:
                slot = r.datt2.at[at, pl.ds(p * PIECE, PIECE)]
                await_at(slot, r.datt_s.at[p, d], r.datt_r.at[p, d], on_patch(at, x))
            else:
                datt_own[p].wait()

    def backward_block(c, qt):
        xc = (x + around(c)) % 4
        keys = r.kv[xc, :, 0].reshape(KEYS, PAIR)
        values = r.kv[xc, :, 1].reshape(KEYS, PAIR)
        factor = r.m[c, qt]
        scaled = r.datt2[qt].astype(F32) * factor
        r.do_t[...] = scaled.T.astype(BF16)
        dots = r.dots[qt] * factor
        found = []
        for h in range(2):
            mask = first_head if h == 0 else jnp.logical_not(first_head)
            rows = pl.ds(h * HEAD, HEAD)
            masked = jnp.where(mask, scaled, 0.0).astype(BF16)
            expo = r.expo[c, h, qt]
            prob_grad = matmul_t(masked, values)
            prob_grad = prob_grad - dots[:, h * HEAD : h * HEAD + 1]
            score_grad = (expo.astype(F32) * prob_grad).astype(BF16)
            found.append(matmul(score_grad, keys))
            r.dk[rows] += matmul(r.q_t[qt, rows], score_grad)
            r.dv[rows] += matmul(r.do_t[rows], expo)
        r.dq[qt] += jnp.where(first_head, found[0], found[1])

    def row_dots(qt):
        dots = r.datt2[qt].astype(F32) * r.att2[qt].astype(F32)
        sums = [
            jnp.sum(jnp.where(mask, dots, 0.0), axis=1, keepdims=True)
            for mask in (first_head, jnp.logical_not(first_head))
        ]
        r.dots[qt] = jnp.where(first_head, sums[0], sums[1])

    @group
    def send_across(act):
        act(r.part.at[3, 0], r.pass_in.at[0], r.pass_s.at[0], r.pass_r.at[0], on_patch(z, right))
        act(r.part.at[3, 1], r.pass_in.at[1], r.pass_s.at[1], r.pass_r.at[1], on_patch(z, left))

    @group
    def send_sides(act, chunks=(1, 2)):
        for c in chunks:
            i, origin, to = ((0, left, right), (1, right, left))[c - 1]
            if act is begin:
                await_at(r.pass_in.at[i], r.pass_s.at[i], r.pass_r.at[i], on_patch(z, origin))
                added = r.part[c, i].astype(F32) + r.pass_in[i].astype(F32)
                r.part[c, i] = added.astype(BF16)
            act(r.part.at[c], r.sum_in.at[i], r.sum_s.at[i], r.sum_r.at[i], on_patch(z, to))

    def backward_step(step, carry):
        k, i = step // 4, step % 4
        c = k + 3 * ((3 - k) // 3) - 3 * (k // 3)
        qt = (z + 4 - around(i)) % 4
        for at, d in ((0, 0), (1, 1), (2, 3), (3, 2)):
            pl.when(step == at)(lambda d=d: await_grads(d))

        @pl.when(k == 0)
        def _():
            row_dots(qt)

        @pl.when(i == 0)
        def _():
            r.dk[...] = jnp.zeros((PAIR, KEYS), F32)
            r.dv[...] = jnp.zeros((PAIR, KEYS), F32)

        backward_block(c, qt)

        @pl.when(i == 3)
        def _():
            r.part[c, 0] = r.dk[...].T.astype(BF16).reshape(4, ROWS, PAIR)
            r.part[c, 1] = r.dv[...].T.astype(BF16).reshape(4, ROWS, PAIR)

        for at, work in (
            (3, lambda: send_across(begin)),
            (4, weight_b),
            (7, lambda: send_sides(begin, (1,))),
            (8, weight_c),
            (11, lambda: send_sides(begin, (2,))),
            (12, weight_d),
        ):
            pl.when(step == at)(work)
        return carry

    lax.fori_loop(0, 16, backward_step, 0)
    for to in range(4):
        r.dq_out[to] = (r.dq[to] * SCALE).astype(BF16)
    first_leg(5, r.far_dq, r.dq_out.at[opposite, top], r.dq_out.at[opposite, low])
    for d in (1, 3):
        to = (z + d) % 4
        send(r.dq_out.at[to], r.z_in.at[z, 2], r.zq_s.at[d], r.zq_r.at[d], on_patch(to, x))
    r.z_in[z, 2] = r.dq_out[z]
    weight_e()
    await_at(r.sum_in.at[0], r.sum_s.at[0], r.sum_r.at[0], on_patch(z, left))
    await_at(r.sum_in.at[1], r.sum_s.at[1], r.sum_r.at[1], on_patch(z, right))
    for d in (2, 1, 3, 0):
        to = (z + d) % 4
        for i in range(2):
            total = r.part[0, i, to].astype(F32)
            total = total + r.sum_in[0, i, to].astype(F32) + r.sum_in[1, i, to].astype(F32)
            if d:
                r.z_out[d, i] = total.astype(BF16)
            else:
                r.z_in[z, i] = total.astype(BF16)
        if d == 2:
            first_leg(4, r.far_dkv, r.z_out.at[d, 0], r.z_out.at[d, 1])
        elif d:
            send(r.z_out.at[d], r.z_in.at[z, pl.ds(0, 2)], r.zkv_s.at[d], r.zkv_r.at[d], on_patch(to, x))
    second_leg(5, r.far_dq, r.z_in.at[down, 2, top], r.z_in.at[up, 2, low])
    second_leg(4, r.far_dkv, r.z_in.at[down, 0], r.z_in.at[up, 1])
    weight_f()
    for d in (1, 3):
        at = (z + 4 - d) % 4
        await_at(r.z_in.at[at, 2], r.zq_s.at[d], r.zq_r.at[d], on_patch(at, x))
        await_at(r.z_in.at[at, pl.ds(0, 2)], r.zkv_s.at[d], r.zkv_r.at[d], on_patch(at, x))
    await_far(5, r.z_in.at[opposite, 2, top], r.z_in.at[opposite, 2, low])
    await_far(4, r.z_in.at[opposite, 0], r.z_in.at[opposite, 1])
    weight_out()
    for copy in started:
        copy.wait_send()
    for copies in later:
        copies(lambda *copy: remote(*copy).wait_send())


def finish(z_in, weight, features, d_queries, d_keys, d_values, d_weight, d_features):
    d_keys[...] = z_in[0, 0].astype(F32)
    d_values[...] = z_in[0, 1].astype(F32)
    d_queries[...] = z_in[0, 2].astype(F32)
    d_weight[...] = weight[...].astype(F32)
    d_features[...] = features[...]


def on_device(patch_queries, patch_keys, patch_values, residual, teacher, output_weight):
    vmem = pl.BlockSpec(memory_space=pltpu.VMEM)
    hbm = pl.BlockSpec(memory_space=pl.ANY)
    z_in, weight, features = pl.pallas_call(
        kernel,
        out_shape=[jax.ShapeDtypeStruct(shape, dtype) for shape, dtype in OUTPUTS.values()],
        in_specs=[hbm] * 6,
        out_specs=[vmem] * 3,
        scratch_shapes=list(SCRATCH.values()),
        compiler_params=pltpu.CompilerParams(
            collective_id=0, has_side_effects=True, vmem_limit_bytes=VMEM_LIMIT
        ),
        cost_estimate=pl.CostEstimate(
            flops=18_000_000_000, bytes_accessed=10_000_000, transcendentals=9_000_000
        ),
    )(patch_queries[0], patch_keys[0], patch_values[0], teacher[0], residual[0], output_weight)
    head_columns = pl.BlockSpec((ROWS, PAIR), lambda i: (0, i))
    d_queries, d_keys, d_values, d_weight, d_features = pl.pallas_call(
        finish,
        grid=(4,),
        out_shape=[jax.ShapeDtypeStruct((ROWS, 512), F32)] * 3
        + [jax.ShapeDtypeStruct((512, D), F32), jax.ShapeDtypeStruct((ROWS, D), F32)],
        in_specs=[
            pl.BlockSpec((1, 3, ROWS, PAIR), lambda i: (i, 0, 0, 0)),
            pl.BlockSpec((PAIR, D), lambda i: (i, 0)),
            pl.BlockSpec((64, D), lambda i: (i, 0)),
        ],
        out_specs=[head_columns] * 3
        + [pl.BlockSpec((PAIR, D), lambda i: (i, 0)), pl.BlockSpec((64, D), lambda i: (i, 0))],
        compiler_params=pltpu.CompilerParams(vmem_limit_bytes=VMEM_LIMIT),
    )(z_in, weight.reshape(512, D), features)
    return d_queries[None], d_keys[None], d_values[None], d_features[None], d_weight


def solution(mesh):
    placed = P("dp", "patch", None)
    return jax.shard_map(
        on_device,
        mesh=mesh,
        in_specs=(placed,) * 5 + (P(),),
        out_specs=(placed,) * 4 + (P(),),
        check_vma=False,
    )
```

```python
from types import SimpleNamespace

import jax
import jax.numpy as jnp
from jax import lax
from jax.experimental import pallas as pl
from jax.experimental.pallas import tpu as pltpu
from jax.sharding import PartitionSpec as P

MESH = pl.DeviceIdType.MESH
F32 = jnp.float32
BF16 = jnp.bfloat16
ROWS = 256
HALF = 128
PAIR = 128
HEAD = 64
D = 1024
KEYS = 1024
PIECES = 2
PIECE = ROWS // PIECES
SCALE = HEAD ** -0.5
VMEM_LIMIT = 60 * 1024 * 1024


def dma(*shape):
    return pltpu.SemaphoreType.DMA(shape)


def on_chip(*shape, dtype=BF16):
    return pltpu.VMEM(shape, dtype)


OUTPUTS = {
    "z_in": ((4, 3, ROWS, PAIR), BF16),
    "ge": ((2, 4, 4, 16, D), BF16),
    "d_features": ((ROWS, D), F32),
}
SCRATCH = {
    "t_raw": on_chip(ROWS, D),
    "res": on_chip(ROWS, D, dtype=F32),
    "w": on_chip(512, D),
    "q2": on_chip(4, ROWS, PAIR),
    "kv": on_chip(4, 4, 2, ROWS, PAIR),
    "expo": on_chip(4, 2, 4, ROWS, KEYS),
    "m": on_chip(4, 4, ROWS, PAIR, dtype=F32),
    "l": on_chip(4, 4, ROWS, PAIR, dtype=F32),
    "o": on_chip(4, 4, ROWS, PAIR, dtype=F32),
    "att2": on_chip(4, ROWS, PAIR),
    "att_full": on_chip(ROWS, 512),
    "local": dma(6),
    "qkv_s": dma(3, 4), "qkv_r": dma(3, 4),
    "spread_s": dma(2, 4), "spread_r": dma(2, 4),
    "relay_s": dma(2, 4), "relay_r": dma(2, 4),
    "att_s": dma(4), "att_r": dma(4), "att_own": dma(1),
    "far_kv": on_chip(2, ROWS, PAIR),
    "far_q": on_chip(2, HALF, PAIR),
    "far_att": on_chip(2, HALF, PAIR),
    "far_datt": on_chip(2, HALF, PAIR),
    "far_dkv": on_chip(2, ROWS, PAIR),
    "far_dq": on_chip(2, HALF, PAIR),
    "first_s": dma(6, 2), "first_r": dma(6, 2), "second_s": dma(6, 2), "second_r": dma(6, 2),
    "t_row": on_chip(4, ROWS, D),
    "t_lhs": on_chip(2, ROWS, D),
    "t_ext": on_chip(ROWS, D),
    "tiles": on_chip(4, PIECE, KEYS, dtype=F32),
    "s_row": on_chip(4, ROWS, D),
    "s_lhs": on_chip(4, PIECE, D),
    "terms": on_chip(4, PIECE, D, dtype=F32),
    "s_ext": on_chip(PIECES, PIECE, D),
    "back_out": on_chip(PIECES, PIECE, D),
    "back_in": on_chip(PIECES, PIECE, D),
    "student": on_chip(ROWS, D, dtype=F32),
    "inverse": on_chip(ROWS, PAIR, dtype=F32),
    "grad": on_chip(ROWS, D),
    "datt": on_chip(ROWS, 512),
    "datt2": on_chip(4, ROWS, PAIR),
    "tx_s": dma(2), "tx_r": dma(2), "tr_s": dma(2), "tr_r": dma(2),
    "tz_s": dma(1), "tz_r": dma(1), "te_s": dma(1), "te_r": dma(1),
    "sx_s": dma(2), "sx_r": dma(2), "sr_s": dma(2), "sr_r": dma(2),
    "sz_s": dma(PIECES), "sz_r": dma(PIECES), "se_s": dma(PIECES), "se_r": dma(PIECES),
    "back_s": dma(PIECES), "back_r": dma(PIECES),
    "datt_s": dma(PIECES, 4), "datt_r": dma(PIECES, 4), "datt_own": dma(PIECES),
    "q_t": on_chip(4, PAIR, ROWS),
    "do_t": on_chip(PAIR, ROWS),
    "dq": on_chip(4, ROWS, PAIR, dtype=F32),
    "v_one": on_chip(2, KEYS, PAIR),
    "dots": on_chip(4, ROWS, PAIR, dtype=F32),
    "dk": on_chip(PAIR, KEYS, dtype=F32),
    "dv": on_chip(PAIR, KEYS, dtype=F32),
    "part": on_chip(4, 2, 4, ROWS, PAIR),
    "pass_in": on_chip(2, 4, ROWS, PAIR),
    "sum_in": on_chip(2, 2, 4, ROWS, PAIR),
    "z_out": on_chip(4, 2, ROWS, PAIR),
    "dq_out": on_chip(4, ROWS, PAIR),
    "pass_s": dma(2), "pass_r": dma(2), "sum_s": dma(2), "sum_r": dma(2),
    "zkv_s": dma(4), "zkv_r": dma(4), "zq_s": dma(4), "zq_r": dma(4),
    "w_term": on_chip(512, D),
    "rs": on_chip(256, D), "ps": on_chip(256, D),
    "ra": on_chip(3, 64, D), "pa": on_chip(64, D),
    "rb": on_chip(3, 16, D), "pb": on_chip(16, D),
    "rc": on_chip(8, 16, D), "pc": on_chip(16, D),
    "gd": on_chip(4, 16, D),
    "ws_s": dma(1), "ws_r": dma(1), "wa_s": dma(4), "wa_r": dma(4), "wb_s": dma(4), "wb_r": dma(4), "wc_s": dma(8), "wc_r": dma(8),
    "wd_s": dma(4), "wd_r": dma(4), "we_s": dma(4), "we_r": dma(4), "wf_s": dma(1), "wf_r": dma(1),
}
INPUTS = ("q", "k", "v", "teacher", "residual", "weight")
NAMES = INPUTS + tuple(OUTPUTS) + tuple(SCRATCH)


def on_patch(z, x):
    return {"patch": z * 4 + x}


def remote(src, dst, send_sem, recv_sem, device):
    return pltpu.make_async_remote_copy(
        src_ref=src,
        dst_ref=dst,
        send_sem=send_sem,
        recv_sem=recv_sem,
        device_id=device,
        device_id_type=MESH,
    )


def columns(index):
    return pl.ds(pl.multiple_of(index * PAIR, PAIR), PAIR)


def around(i):
    return i + (i // 2) * (1 - 2 * (i % 2))


def matmul(a, b):
    return jnp.dot(a, b, preferred_element_type=F32)


def matmul_t(a, b):
    return lax.dot_general(a, b, (((1,), (1,)), ((), ())), preferred_element_type=F32)


def kernel(*refs):
    r = SimpleNamespace(**dict(zip(NAMES, refs, strict=True)))
    index = lax.axis_index("patch")
    z, x = index // 4, index % 4
    dp = lax.axis_index("dp")
    y, z_lo, core = dp // 4, (dp // 2) % 2, dp % 2
    ring = z * 2 + z_lo
    right, left, across = (x + 1) % 4, (x + 3) % 4, (x + 2) % 4
    up, down, opposite = (z + 1) % 4, (z + 3) % 4, (z + 2) % 4
    high = x // 2
    step = 3 - 2 * high
    shift_to, shift_from = (z + step) % 4, (z + 4 - step) % 4
    swap = x + 1 - 2 * (x % 2)
    inner = (x * (3 - x)) // 2

    sibling = {"dp": y * 4 + z_lo * 2 + 1 - core}

    def on_y(i):
        return {"dp": i * 4 + z_lo * 2 + core}

    def ring_device(i):
        return {"dp": y * 4 + (i % 2) * 2 + core, "patch": (i // 2) * 4 + x}

    started = []

    def send(src, dst, send_sem, recv_sem, device):
        copy = remote(src, dst, send_sem, recv_sem, device)
        copy.start()
        started.append(copy)

    later = []

    def begin(*copy):
        remote(*copy).start()

    def group(copies):
        later.append(copies)
        return copies

    def await_at(slot, send_sem, recv_sem, device):
        remote(slot, slot, send_sem, recv_sem, device).wait_recv()

    def first_leg(n, relay, by_up, by_down):
        send(by_up, relay.at[0], r.first_s.at[n, 0], r.first_r.at[n, 0], on_patch(up, x))
        send(by_down, relay.at[1], r.first_s.at[n, 1], r.first_r.at[n, 1], on_patch(down, x))

    def second_leg(n, relay, to_up, to_down):
        for i, origin, to, target in ((0, down, up, to_up), (1, up, down, to_down)):
            await_at(relay.at[i], r.first_s.at[n, i], r.first_r.at[n, i], on_patch(origin, x))
            send(relay.at[i], target, r.second_s.at[n, i], r.second_r.at[n, i], on_patch(to, x))

    def await_far(n, by_up, by_down):
        await_at(by_up, r.second_s.at[n, 0], r.second_r.at[n, 0], on_patch(down, x))
        await_at(by_down, r.second_s.at[n, 1], r.second_r.at[n, 1], on_patch(up, x))

    top, low = pl.ds(0, HALF), pl.ds(HALF, HALF)

    local = [
        pltpu.make_async_copy(r.teacher, r.t_raw, r.local.at[0]),
        pltpu.make_async_copy(r.k.at[:, columns(z)], r.kv.at[x, z, 0], r.local.at[1]),
        pltpu.make_async_copy(r.v.at[:, columns(z)], r.kv.at[x, z, 1], r.local.at[2]),
        pltpu.make_async_copy(r.q.at[:, columns(z)], r.q2.at[z], r.local.at[3]),
        pltpu.make_async_copy(r.residual, r.res, r.local.at[4]),
        pltpu.make_async_copy(r.weight, r.w, r.local.at[5]),
    ]
    for copy in local:
        copy.start()
    peers = (
        [ring_device((ring + d) % 8) for d in range(1, 8)]
        + [on_patch(z, (x + d) % 4) for d in range(1, 4)]
        + [on_y((y + d) % 4) for d in range(1, 4)]
        + [sibling]
    )
    barrier = pltpu.get_barrier_semaphore()
    for peer in peers:
        pl.semaphore_signal(barrier, inc=1, device_id=peer, device_id_type=MESH)
    pl.semaphore_wait(barrier, len(peers))

    first_leg(0, r.far_kv, r.k.at[:, columns(opposite)], r.v.at[:, columns(opposite)])
    for d in (1, 3):
        to = (z + d) % 4
        for i, source in enumerate((r.k, r.v)):
            send(source.at[:, columns(to)], r.kv.at[x, z, i], r.qkv_s.at[i, d], r.qkv_r.at[i, d], on_patch(to, x))
    first_leg(1, r.far_q, r.q.at[top, columns(opposite)], r.q.at[low, columns(opposite)])
    for d in (1, 3):
        to = (z + d) % 4
        send(r.q.at[:, columns(to)], r.q2.at[z], r.qkv_s.at[2, d], r.qkv_r.at[2, d], on_patch(to, x))

    def spread(d):
        at = (z + 4 - d) % 4
        for side, to in enumerate((right, left)):
            slot = r.kv.at[x, at]
            send(slot, slot, r.spread_s.at[side, d], r.spread_r.at[side, d], on_patch(z, to))

    local[1].wait()
    local[2].wait()
    spread(0)
    local[0].wait()
    teacher = r.t_raw[...].astype(F32)
    teacher = teacher * lax.rsqrt(jnp.sum(teacher * teacher, axis=1, keepdims=True) + 1e-06)
    r.t_row[x] = teacher.astype(BF16)
    r.t_lhs[1] = teacher.astype(BF16)
    for side, to in enumerate((right, left)):
        send(r.t_row.at[x], r.t_row.at[x], r.tx_s.at[side], r.tx_r.at[side], on_patch(z, to))
    second_leg(0, r.far_kv, r.kv.at[x, down, 0], r.kv.at[x, up, 1])
    for d in (1, 3):
        at = (z + 4 - d) % 4
        for i in range(2):
            await_at(r.kv.at[x, at, i], r.qkv_s.at[i, d], r.qkv_r.at[i, d], on_patch(at, x))
        spread(d)
    second_leg(1, r.far_q, r.q2.at[down, top], r.q2.at[up, low])
    await_far(0, r.kv.at[x, opposite, 0], r.kv.at[x, opposite, 1])
    spread(2)
    send(r.t_row.at[x], r.t_lhs.at[0], r.tz_s.at[0], r.tz_r.at[0], on_patch(shift_to, x))
    local[3].wait()

    first_head = lax.broadcasted_iota(jnp.int32, (ROWS, PAIR), 1) < HEAD

    def value_ones(c):
        values = r.kv[(x + around(c)) % 4, :, 1].reshape(KEYS, PAIR).astype(F32)
        mask = lax.broadcasted_iota(jnp.int32, (KEYS, PAIR), 1) < HEAD
        r.v_one[0] = jnp.where(mask, values, 1.0).astype(BF16)
        r.v_one[1] = jnp.where(mask, 1.0, values).astype(BF16)

    def of_head(h, block):
        return jnp.where(first_head if h == 0 else jnp.logical_not(first_head), block, 0.0).astype(BF16)

    def forward_block(c, qt):
        keys = r.kv[(x + around(c)) % 4, :, 0].reshape(KEYS, PAIR)
        queries = r.q2[qt].astype(F32) * SCALE
        scores = [matmul_t(of_head(h, queries), keys) for h in range(2)]
        tops, weighted = [], []
        for h in range(2):
            tops.append(jnp.max(scores[h], axis=1, keepdims=True))
            rounded = jnp.exp(scores[h] - tops[h]).astype(BF16)
            r.expo[c, h, qt] = rounded
            weighted.append(matmul(rounded, r.v_one[h]))
        r.m[c, qt] = jnp.where(first_head, *tops)
        r.o[c, qt] = jnp.where(first_head, *weighted)
        r.l[c, qt] = pltpu.roll(jnp.where(first_head, *weighted[::-1]), HEAD, 1)

    def join(qt):
        tops = [r.m[c, qt] for c in range(4)]
        top = jnp.maximum(jnp.maximum(tops[0], tops[1]), jnp.maximum(tops[2], tops[3]))
        scale = [jnp.exp(tops[c] - top) for c in range(4)]
        total = sum(scale[c] * r.l[c, qt] for c in range(4))
        joined = sum(scale[c] * r.o[c, qt] for c in range(4))
        inverse = 1.0 / total
        r.att2[qt] = (joined * inverse).astype(BF16)
        for c in range(4):
            r.m[c, qt] = scale[c] * inverse

    def await_queries(d):
        at = (z + 4 - d) % 4
        if d == 2:
            await_far(1, r.q2.at[at, top], r.q2.at[at, low])
        elif d:
            await_at(r.q2.at[at], r.qkv_s.at[2, d], r.qkv_r.at[2, d], on_patch(at, x))

    @group
    def relay_keys(act):
        for d in (0, 1, 3, 2):
            at = (z + 4 - d) % 4
            if act is begin:
                await_at(r.kv.at[right, at], r.spread_s.at[1, d], r.spread_r.at[1, d], on_patch(z, right))
            slot = r.kv.at[right, at, 0]
            act(slot, slot, r.relay_s.at[0, d], r.relay_r.at[0, d], on_patch(z, left))
            if act is begin:
                await_at(r.kv.at[left, at], r.spread_s.at[0, d], r.spread_r.at[0, d], on_patch(z, left))
            slot = r.kv.at[left, at, 1]
            act(slot, slot, r.relay_s.at[1, d], r.relay_r.at[1, d], on_patch(z, right))

    def pass_on(act, row, x_s, x_r, on_s, on_r):
        if act is begin:
            await_at(row.at[right], x_s.at[1], x_r.at[1], on_patch(z, right))
        slot = row.at[right, top]
        act(slot, slot, on_s.at[0], on_r.at[0], on_patch(z, left))
        if act is begin:
            await_at(row.at[left], x_s.at[0], x_r.at[0], on_patch(z, left))
        slot = row.at[left, low]
        act(slot, slot, on_s.at[1], on_r.at[1], on_patch(z, right))

    def await_across(row, on_s, on_r):
        for i in range(2):
            await_at(row.at[across, pl.ds(i * HALF, HALF)], on_s.at[i], on_r.at[i], on_patch(z, right))

    @group
    def pass_teachers(act):
        pass_on(act, r.t_row, r.tx_s, r.tx_r, r.tr_s, r.tr_r)

    def await_keys():
        for d in range(4):
            at = (z + 4 - d) % 4
            for i in range(2):
                await_at(r.kv.at[across, at, i], r.relay_s.at[i, d], r.relay_r.at[i, d], on_patch(z, right))

    @group
    def send_attended(act, places=(1, 3, 2)):
        for d in places:
            to = (z + d) % 4
            if d == 2:
                for i, rows, side in ((0, top, up), (1, low, down)):
                    target = r.far_att.at[i]
                    act(r.att2.at[to, rows], target, r.first_s.at[2, i], r.first_r.at[2, i], on_patch(side, x))
            else:
                act(r.att2.at[to], r.att_full.at[:, columns(z)], r.att_s.at[d], r.att_r.at[d], on_patch(to, x))

    def forward_step(step, carry):
        c, i = step // 4, step % 4
        start = (3 - c) // 3
        qt = (z + start * (4 - around(i)) + (1 - start) * around(3 - i)) % 4
        for at, work in (
            (1, lambda: await_queries(1)),
            (2, lambda: await_queries(3)),
            (3, lambda: await_queries(2)),
            (4, lambda: relay_keys(begin)),
            (8, lambda: pass_teachers(begin)),
            (12, await_keys),
        ):
            pl.when(step == at)(work)
        pl.when(i == 0)(lambda: value_ones(c))
        forward_block(c, qt)

        @pl.when(c == 3)
        def _():
            join(qt)

        for i, d in enumerate((2, 3, 1)):
            pl.when(step == 12 + i)(lambda d=d: send_attended(begin, (d,)))
        return carry

    lax.fori_loop(0, 16, forward_step, 0)
    own = pltpu.make_async_copy(r.att2.at[z], r.att_full.at[:, columns(z)], r.att_own.at[0])
    own.start()
    second_leg(2, r.far_att, r.att_full.at[top, columns(down)], r.att_full.at[low, columns(up)])

    own.wait()
    local[4].wait()
    local[5].wait()
    await_far(2, r.att_full.at[top, columns(opposite)], r.att_full.at[low, columns(opposite)])
    for d in (1, 3):
        at = (z + 4 - d) % 4
        await_at(r.att_full.at[:, columns(at)], r.att_s.at[d], r.att_r.at[d], on_patch(at, x))

    features = r.res[...] + matmul(r.att_full[...], r.w[...])
    inverse = lax.rsqrt(jnp.sum(features * features, axis=1, keepdims=True) + 1e-06)
    student = features * inverse
    rounded = student.astype(BF16)
    r.s_row[x] = rounded
    for p in range(PIECES):
        r.s_lhs[PIECES + p] = rounded[p * PIECE : (p + 1) * PIECE]
        source = r.s_row.at[x, pl.ds(p * PIECE, PIECE)]
        send(source, r.s_lhs.at[p], r.sz_s.at[p], r.sz_r.at[p], on_patch(shift_to, x))
    for side, to in enumerate((right, left)):
        send(r.s_row.at[x], r.s_row.at[x], r.sx_s.at[side], r.sx_r.at[side], on_patch(z, to))
    r.student[...] = student
    r.inverse[...] = jnp.broadcast_to(inverse, (ROWS, PAIR))

    @group
    def pass_students(act):
        pass_on(act, r.s_row, r.sx_s, r.sx_r, r.sr_s, r.sr_r)

    await_at(r.t_lhs.at[0], r.tz_s.at[0], r.tz_r.at[0], on_patch(shift_from, x))
    send(r.t_lhs.at[0], r.t_ext, r.te_s.at[0], r.te_r.at[0], on_patch(z, swap))
    await_across(r.t_row, r.tr_s, r.tr_r)

    def teacher_tile(i, carry):
        pl.when(i == 1)(lambda: pass_students(begin))
        tile = matmul_t(r.t_lhs[i], r.t_row[...].reshape(KEYS, D))
        r.tiles[pl.ds(2 * i, 2)] = tile.reshape(2, PIECE, KEYS)
        return carry

    lax.fori_loop(0, 2, teacher_tile, 0)
    await_across(r.s_row, r.sr_s, r.sr_r)

    first = (1 - high) * (x + 1) * ROWS
    last = KEYS - high * (KEYS - x * ROWS)

    @group
    def swap_students(act, pieces=range(PIECES)):
        for p in pieces:
            slot = r.s_lhs.at[p]
            if act is begin:
                await_at(slot, r.sz_s.at[p], r.sz_r.at[p], on_patch(shift_from, x))
            act(slot, r.s_ext.at[p], r.se_s.at[p], r.se_r.at[p], on_patch(z, swap))

    @group
    def send_back(act, pieces=range(PIECES)):
        for p in pieces:
            if act is begin:
                r.back_out[p] = r.terms[p].astype(BF16)
            act(r.back_out.at[p], r.back_in.at[p], r.back_s.at[p], r.back_r.at[p], on_patch(shift_from, x))

    def term(i, carry):
        for p in range(PIECES):
            pl.when(i == p)(lambda p=p: swap_students(begin, (p,)))
        row = r.s_row[...].reshape(KEYS, D)
        tile = matmul_t(r.s_lhs[i], row) - r.tiles[i]
        at = lax.broadcasted_iota(jnp.int32, tile.shape, 1)
        whole = i // 2
        keep = jnp.logical_and(at >= first * (1 - whole), at < last + whole * (KEYS - last))
        r.terms[i] = matmul(jnp.where(keep, tile, 0.0).astype(BF16), row)
        for p in range(PIECES):
            pl.when(i == p)(lambda p=p: send_back(begin, (p,)))
        return carry

    lax.fori_loop(0, 4, term, 0)
    await_at(r.t_ext, r.te_s.at[0], r.te_r.at[0], on_patch(z, swap))
    for p in range(PIECES):
        await_at(r.s_ext.at[p], r.se_s.at[p], r.se_r.at[p], on_patch(z, swap))
    other = r.s_ext[...].reshape(ROWS, D)
    tile = matmul_t(r.s_row[x], other) - matmul_t(r.t_row[x], r.t_ext[...])
    tile = jnp.where(lax.broadcasted_iota(jnp.int32, tile.shape, 1) < inner * ROWS, tile, 0.0)
    added = matmul(tile.astype(BF16), other)
    for p in range(PIECES):
        r.terms[PIECES + p] += added[p * PIECE : (p + 1) * PIECE]

    datt_own = []
    for p in range(PIECES):
        rows = pl.ds(p * PIECE, PIECE)
        await_at(r.back_in.at[p], r.back_s.at[p], r.back_r.at[p], on_patch(shift_to, x))
        gram_grad = 32.0 * (r.terms[PIECES + p] + r.back_in[p].astype(F32))
        student = r.student[rows]
        dot = jnp.sum(student * gram_grad, axis=1, keepdims=True)
        grad = r.inverse[rows, :1] * (gram_grad - student * dot)
        r.d_features[rows] = grad
        rounded = grad.astype(BF16)
        r.grad[rows] = rounded
        r.datt[rows] = matmul_t(rounded, r.w[...]).astype(BF16)
        side = (up, down)[p]
        source = r.datt.at[rows, columns(opposite)]
        send(source, r.far_datt.at[p], r.first_s.at[3, p], r.first_r.at[3, p], on_patch(side, x))
        for d in (1, 3):
            to = (z + d) % 4
            source = r.datt.at[rows, columns(to)]
            send(source, r.datt2.at[z, rows], r.datt_s.at[p, d], r.datt_r.at[p, d], on_patch(to, x))
        own = pltpu.make_async_copy(r.datt.at[rows, columns(z)], r.datt2.at[z, rows], r.datt_own.at[p])
        own.start()
        datt_own.append(own)
    second_leg(3, r.far_datt, r.datt2.at[down, top], r.datt2.at[up, low])
    transposed = r.att_full[...].astype(F32).T.astype(BF16)
    r.w_term[...] = matmul(transposed, r.grad[...]).astype(BF16)

    def weight_sibling():
        rows = pl.ds(pl.multiple_of((1 - core) * 256, 256), 256)
        send(r.w_term.at[rows], r.rs, r.ws_s.at[0], r.ws_r.at[0], sibling)

    def weight_a():
        await_at(r.rs, r.ws_s.at[0], r.ws_r.at[0], sibling)
        own_rows = pl.ds(pl.multiple_of(core * 256, 256), 256)
        r.ps[...] = (r.w_term[own_rows].astype(F32) + r.rs[...].astype(F32)).astype(BF16)
        for d in (2, 1, 3):
            to = (y + d) % 4
            rows = pl.ds(pl.multiple_of(to * 64, 64), 64)
            send(r.ps.at[rows], r.ra.at[d - 1], r.wa_s.at[d], r.wa_r.at[d], on_y(to))

    @group
    def send_b(act):
        for d in range(1, 4):
            to = (x + d) % 4
            rows = pl.ds(pl.multiple_of(to * 16, 16), 16)
            act(r.pa.at[rows], r.rb.at[d - 1], r.wb_s.at[d], r.wb_r.at[d], on_patch(z, to))

    def weight_b():
        total = r.ps[pl.ds(pl.multiple_of(y * 64, 64), 64)].astype(F32)
        for d in range(1, 4):
            await_at(r.ra.at[d - 1], r.wa_s.at[d], r.wa_r.at[d], on_y((y + d) % 4))
            total = total + r.ra[d - 1].astype(F32)
        r.pa[...] = total.astype(BF16)
        send_b(begin)

    @group
    def send_c(act):
        for d in range(1, 8):
            act(r.pb, r.rc.at[ring], r.wc_s.at[d], r.wc_r.at[d], ring_device((ring + d) % 8))

    def weight_c():
        total = r.pa[pl.ds(pl.multiple_of(x * 16, 16), 16)].astype(F32)
        for d in range(1, 4):
            await_at(r.rb.at[d - 1], r.wb_s.at[d], r.wb_r.at[d], on_patch(z, (x + d) % 4))
            total = total + r.rb[d - 1].astype(F32)
        r.pb[...] = total.astype(BF16)
        r.rc[ring] = r.pb[...]
        send_c(begin)

    @group
    def send_d(act):
        for d in range(1, 4):
            act(r.pc, r.gd.at[x], r.wd_s.at[d], r.wd_r.at[d], on_patch(z, (x + d) % 4))

    def weight_d():
        for d in range(1, 8):
            at = (ring + 8 - d) % 8
            await_at(r.rc.at[at], r.wc_s.at[d], r.wc_r.at[d], ring_device(at))
        total = r.rc[0].astype(F32)
        for i in range(1, 8):
            total = total + r.rc[i].astype(F32)
        r.pc[...] = total.astype(BF16)
        r.gd[x] = r.pc[...]
        send_d(begin)

    def weight_e():
        for d in range(1, 4):
            at = (x + 4 - d) % 4
            await_at(r.gd.at[at], r.wd_s.at[d], r.wd_r.at[d], on_patch(z, at))
        r.ge[core, y] = r.gd[...]
        for d in range(1, 4):
            send(r.gd, r.ge.at[core, y], r.we_s.at[d], r.we_r.at[d], on_y((y + d) % 4))

    def weight_f():
        for d in range(1, 4):
            at = (y + 4 - d) % 4
            await_at(r.ge.at[core, at], r.we_s.at[d], r.we_r.at[d], on_y(at))
        send(r.ge.at[core], r.ge.at[core], r.wf_s.at[0], r.wf_r.at[0], sibling)

    def weight_out():
        await_at(r.ge.at[1 - core], r.wf_s.at[0], r.wf_r.at[0], sibling)

    weight_sibling()
    for qt in range(4):
        r.q_t[qt] = (r.q2[qt].astype(F32) * SCALE).T.astype(BF16)
        r.dq[qt] = jnp.zeros((ROWS, PAIR), F32)
    weight_a()

    def await_grads(d):
        at = (z + 4 - d) % 4
        if d == 2:
            await_far(3, r.datt2.at[at, top], r.datt2.at[at, low])
            return
        for p in range(2):
            if d:
                slot = r.datt2.at[at, pl.ds(p * PIECE, PIECE)]
                await_at(slot, r.datt_s.at[p, d], r.datt_r.at[p, d], on_patch(at, x))
            else:
                datt_own[p].wait()

    def backward_block(c, qt):
        xc = (x + around(c)) % 4
        keys = r.kv[xc, :, 0].reshape(KEYS, PAIR)
        values = r.kv[xc, :, 1].reshape(KEYS, PAIR)
        factor = r.m[c, qt]
        scaled = r.datt2[qt].astype(F32) * factor
        r.do_t[...] = scaled.T.astype(BF16)
        dots = r.dots[qt] * factor
        prob_grads, expos, found = [], [], []
        for h in range(2):
            expos.append(r.expo[c, h, qt])
            prob_grads.append(matmul_t(of_head(h, scaled), values))
        for h in range(2):
            rows = pl.ds(h * HEAD, HEAD)
            r.dv[rows] += matmul(r.do_t[rows], expos[h])
            prob_grad = prob_grads[h] - dots[:, h * HEAD : h * HEAD + 1]
            score_grad = expos[h] * prob_grad.astype(BF16)
            found.append(matmul(score_grad, keys))
            r.dk[rows] += matmul(r.q_t[qt, rows], score_grad)
        r.dq[qt] += jnp.where(first_head, *found)

    def row_dots(qt):
        dots = r.datt2[qt].astype(F32) * r.att2[qt].astype(F32)
        sums = [
            jnp.sum(jnp.where(mask, dots, 0.0), axis=1, keepdims=True)
            for mask in (first_head, jnp.logical_not(first_head))
        ]
        r.dots[qt] = jnp.where(first_head, sums[0], sums[1])

    @group
    def send_across(act):
        act(r.part.at[3, 0], r.pass_in.at[0], r.pass_s.at[0], r.pass_r.at[0], on_patch(z, right))
        act(r.part.at[3, 1], r.pass_in.at[1], r.pass_s.at[1], r.pass_r.at[1], on_patch(z, left))

    @group
    def send_sides(act, chunks=(1, 2)):
        for c in chunks:
            i, origin, to = ((0, left, right), (1, right, left))[c - 1]
            if act is begin:
                await_at(r.pass_in.at[i], r.pass_s.at[i], r.pass_r.at[i], on_patch(z, origin))
                added = r.part[c, i].astype(F32) + r.pass_in[i].astype(F32)
                r.part[c, i] = added.astype(BF16)
            act(r.part.at[c], r.sum_in.at[i], r.sum_s.at[i], r.sum_r.at[i], on_patch(z, to))

    def backward_step(step, carry):
        k, i = step // 4, step % 4
        c = k + 3 * ((3 - k) // 3) - 3 * (k // 3)
        qt = (z + 4 - around(i)) % 4
        for at, d in ((0, 0), (1, 1), (2, 3), (3, 2)):
            pl.when(step == at)(lambda d=d: await_grads(d))

        @pl.when(k == 0)
        def _():
            row_dots(qt)

        @pl.when(i == 0)
        def _():
            r.dk[...] = jnp.zeros((PAIR, KEYS), F32)
            r.dv[...] = jnp.zeros((PAIR, KEYS), F32)

        backward_block(c, qt)

        @pl.when(i == 3)
        def _():
            r.part[c, 0] = r.dk[...].T.astype(BF16).reshape(4, ROWS, PAIR)
            r.part[c, 1] = r.dv[...].T.astype(BF16).reshape(4, ROWS, PAIR)

        for at, work in (
            (3, lambda: send_across(begin)),
            (5, weight_b),
            (7, lambda: send_sides(begin, (1,))),
            (9, weight_c),
            (11, lambda: send_sides(begin, (2,))),
            (13, weight_d),
        ):
            pl.when(step == at)(work)
        return carry

    lax.fori_loop(0, 16, backward_step, 0)
    for to in range(4):
        r.dq_out[to] = (r.dq[to] * SCALE).astype(BF16)
    first_leg(5, r.far_dq, r.dq_out.at[opposite, top], r.dq_out.at[opposite, low])
    for d in (1, 3):
        to = (z + d) % 4
        send(r.dq_out.at[to], r.z_in.at[z, 2], r.zq_s.at[d], r.zq_r.at[d], on_patch(to, x))
    r.z_in[z, 2] = r.dq_out[z]
    weight_e()
    await_at(r.sum_in.at[0], r.sum_s.at[0], r.sum_r.at[0], on_patch(z, left))
    await_at(r.sum_in.at[1], r.sum_s.at[1], r.sum_r.at[1], on_patch(z, right))
    for d in (2, 1, 3, 0):
        to = (z + d) % 4
        for i in range(2):
            total = r.part[0, i, to].astype(F32)
            total = total + r.sum_in[0, i, to].astype(F32) + r.sum_in[1, i, to].astype(F32)
            if d:
                r.z_out[d, i] = total.astype(BF16)
            else:
                r.z_in[z, i] = total.astype(BF16)
        if d == 2:
            first_leg(4, r.far_dkv, r.z_out.at[d, 0], r.z_out.at[d, 1])
        elif d:
            send(r.z_out.at[d], r.z_in.at[z, pl.ds(0, 2)], r.zkv_s.at[d], r.zkv_r.at[d], on_patch(to, x))
    second_leg(5, r.far_dq, r.z_in.at[down, 2, top], r.z_in.at[up, 2, low])
    second_leg(4, r.far_dkv, r.z_in.at[down, 0], r.z_in.at[up, 1])
    weight_f()
    for d in (1, 3):
        at = (z + 4 - d) % 4
        await_at(r.z_in.at[at, 2], r.zq_s.at[d], r.zq_r.at[d], on_patch(at, x))
        await_at(r.z_in.at[at, pl.ds(0, 2)], r.zkv_s.at[d], r.zkv_r.at[d], on_patch(at, x))
    await_far(5, r.z_in.at[opposite, 2, top], r.z_in.at[opposite, 2, low])
    await_far(4, r.z_in.at[opposite, 0], r.z_in.at[opposite, 1])
    weight_out()
    for copy in started:
        copy.wait_send()
    for copies in later:
        copies(lambda *copy: remote(*copy).wait_send())


def finish(z_in, weight, features, d_queries, d_keys, d_values, d_weight, d_features):
    d_keys[...] = z_in[0, 0].astype(F32)
    d_values[...] = z_in[0, 1].astype(F32)
    d_queries[...] = z_in[0, 2].astype(F32)
    d_weight[...] = weight[...].astype(F32)
    d_features[...] = features[...]


def on_device(patch_queries, patch_keys, patch_values, residual, teacher, output_weight):
    vmem = pl.BlockSpec(memory_space=pltpu.VMEM)
    hbm = pl.BlockSpec(memory_space=pl.ANY)
    z_in, weight, features = pl.pallas_call(
        kernel,
        out_shape=[jax.ShapeDtypeStruct(shape, dtype) for shape, dtype in OUTPUTS.values()],
        in_specs=[hbm] * 6,
        out_specs=[vmem] * 3,
        scratch_shapes=list(SCRATCH.values()),
        compiler_params=pltpu.CompilerParams(
            collective_id=0, has_side_effects=True, vmem_limit_bytes=VMEM_LIMIT
        ),
        cost_estimate=pl.CostEstimate(
            flops=18_000_000_000, bytes_accessed=10_000_000, transcendentals=9_000_000
        ),
    )(patch_queries[0], patch_keys[0], patch_values[0], teacher[0], residual[0], output_weight)
    head_columns = pl.BlockSpec((ROWS, PAIR), lambda i: (0, i))
    d_queries, d_keys, d_values, d_weight, d_features = pl.pallas_call(
        finish,
        grid=(4,),
        out_shape=[jax.ShapeDtypeStruct((ROWS, 512), F32)] * 3
        + [jax.ShapeDtypeStruct((512, D), F32), jax.ShapeDtypeStruct((ROWS, D), F32)],
        in_specs=[
            pl.BlockSpec((1, 3, ROWS, PAIR), lambda i: (i, 0, 0, 0)),
            pl.BlockSpec((PAIR, D), lambda i: (i, 0)),
            pl.BlockSpec((64, D), lambda i: (i, 0)),
        ],
        out_specs=[head_columns] * 3
        + [pl.BlockSpec((PAIR, D), lambda i: (i, 0)), pl.BlockSpec((64, D), lambda i: (i, 0))],
        compiler_params=pltpu.CompilerParams(vmem_limit_bytes=VMEM_LIMIT),
    )(z_in, weight.reshape(512, D), features)
    return d_queries[None], d_keys[None], d_values[None], d_features[None], d_weight


def solution(mesh):
    placed = P("dp", "patch", None)
    return jax.shard_map(
        on_device,
        mesh=mesh,
        in_specs=(placed,) * 5 + (P(),),
        out_specs=(placed,) * 4 + (P(),),
        check_vma=False,
    )
```
